256 devices in a mesh: shard: 64 (over z, y, core), tp: 4 (over x).
Axes of the slice: x: 4, y: 4, z: 8, core: 2. Of those that a mesh axis runs over, the one named last changes fastest.
Arguments:
- person_embedding: bfloat16 [128, 256], P('shard'), may hold values from -6 to 6
- catalog_embedding: bfloat16 [524288, 256], P(('shard', 'tp')), may hold values from -1.7 to 1.7
- catalog_attributes: bfloat16 [524288, 768], P(('shard', 'tp')), may hold values from -6 to 6
- kept_part_entries: int32 [128, 256, 8], P(None, ('shard', 'tp')), may hold values from 0 to 2047
- valid_slot_number: int32 [128, 256], P(None, ('shard', 'tp')), may hold values from 1 to 8, 1024 in all within a row
- pair_attributes: bfloat16 [128, 1024, 2048], P('shard', None, 'tp'), may hold values from -6 to 6
- lowrank_v_matrix: bfloat16 [2, 3072, 512], P(None, 'tp'), may hold values from -0.109375 to 0.109375
- lowrank_u_matrix: bfloat16 [2, 512, 3072], P(None, None, 'tp'), may hold values from -0.25 to 0.25
- interaction_offset: float32 [2, 3072], P(None, 'tp'), may hold values from -3 to 3
- final_projection: bfloat16 [3072], P('tp'), may hold values from -0.109375 to 0.109375
- similarity_coefficient: float32 [1], replicated, may hold values from 0.5 to 1.5
Outputs:
- ranked_scores: float32 [128, 1024], P('shard')
The draws below stay inside these ranges and needn't reach their ends.
Inputs may be any that keep to these rules, and one draw needn't show every extreme that they name: Only the first valid_slot_number[u, b] slots of kept_part_entries[u, b] are read; each is a row of shard b. `valid_slot_number`: each user has exactly 1024 survivors over all shards, and for each user some shard gives 8.
All inputs are finite; a program needn't handle non-finite values.
Results may differ from the reference program's by a relative error of at most 0.017.
Values may be sent and summed in bfloat16 or wider, within the bound.
No kernel may reach another device: no remote copies, remote signals or barrier semaphores. Data moves between devices by JAX's collectives and lax.ppermute only.
A program may use at most 64 MiB of HBM per device.

```python
import math
import jax
import jax.numpy as jnp
import numpy as np
from jax import lax

EMB = 256
FEAT = 768
CONTEXT_DIM = 2048
FACTOR_DIM = 512
LAYERS = 2
KEPT_PER_PART = 8
PART_ENTRIES = 2048
WIDTH = 3072
PERSON_NUMBER = 128
CATALOG_PARTS = 256
ITEMS = 524288
KEPT_PER_PERSON = 1024
N_SHARD = 64
N_TP = 4


def draw_catalog_embedding(key, part):
    key = jax.random.fold_in(key, 11)
    base_key, scale_key = jax.random.split(key)
    row_scale = jnp.exp(jax.random.uniform(scale_key, (ITEMS, 1), jnp.float32, 0.0, 1.5))
    base = jnp.clip(jax.random.normal(base_key, (ITEMS, EMB), jnp.float32), -6.0, 6.0)
    return (base * row_scale / 16.0).astype(jnp.bfloat16)


def with_ends(values, stream_key, least, largest):
    shape = values.shape
    index_at = [jax.random.randint(jax.random.fold_in(stream_key, axis), (), 0, shape[axis]) for axis in range(len(shape))]
    values = values.at[tuple(index_at)].set(least)
    longest = shape.index(max(shape))
    index_at[longest] = (index_at[longest] + 1) % shape[longest]
    return values.at[tuple(index_at)].set(largest)


def steps_of(rng, extent, shards, smallest, largest):
    def one(position, shards_of):
        draws = jax.random.uniform(jax.random.fold_in(jax.random.fold_in(rng, 6), position), (shards_of,), jnp.float32, smallest / len(shards), largest / len(shards))
        return jnp.repeat(jnp.exp(draws), extent[position] // shards_of).reshape((-1,) + (1,) * (len(extent) - position - 1))

    gain = one(*shards[0])
    for cut in shards[1:]:
        gain = gain * one(*cut)
    return gain


def length_profile(amount, total, reach, skew):
    portions = [(1 << 20) // math.isqrt(rank ** skew) + 1 for rank in range(2, amount + 1)]
    spare, counts = total - reach - (amount - 1), [1] * (amount - 1)
    while spare > 0:
        movable = [i for i in range(amount - 1) if counts[i] < reach]
        pool, budget = sum([portions[i] for i in movable]), spare
        for i in movable:
            extra = min(reach - counts[i], max(1, budget * portions[i] // pool), spare)
            counts[i] = counts[i] + extra
            spare = spare - extra
    return np.array([reach] + counts)


def uneven(rng, count, total, reach, lean):
    if count == 2:
        one = jax.random.randint(rng, (), max(1, total - reach), min(reach, total - 1) + 1)
        return jnp.stack([one, total - one])
    sizes = jnp.asarray(length_profile(count, total, reach, lean), jnp.int32)
    couples = (count - 1) // 2
    giver, sink = sizes[1:1 + 2 * couples:2], sizes[2:2 + 2 * couples:2]
    room = jnp.minimum(giver - 1, reach - sink)
    moved = jax.random.randint(jax.random.fold_in(rng, 1), (couples,), 0, 1 << 20) % (room + 1)
    sizes = sizes.at[1:1 + 2 * couples:2].set(giver - moved).at[2:2 + 2 * couples:2].set(sink + moved)
    return sizes[jax.random.permutation(jax.random.fold_in(rng, 2), count)]


def noise(own_key, dims, spread, limit, shards=(), kind=jnp.bfloat16):
    factor_of = steps_of(own_key, dims, shards, -0.22, 0.18) if shards else 1.0
    entries = jax.random.normal(own_key, dims, jnp.float32) * spread * factor_of
    return jnp.minimum(jnp.maximum(entries, -limit), limit).astype(kind)


def setup_inputs(seed: int = 0) -> dict:
    splits = jax.random.split(jax.random.key(seed), 12)
    return {
        "person_embedding": noise(splits[0], (PERSON_NUMBER, EMB), 1.0, 6.0, ((0, 64),)),
        "catalog_embedding": draw_catalog_embedding(jax.random.fold_in(splits[11], 71), 0),
        "catalog_attributes": noise(splits[2], (ITEMS, FEAT), 1.0, 6.0, ((0, 256),)),
        "kept_part_entries": with_ends(jax.random.randint(splits[3], (PERSON_NUMBER, CATALOG_PARTS, KEPT_PER_PART), 0, PART_ENTRIES), jax.random.fold_in(splits[3], 1), 0, PART_ENTRIES - 1).astype(jnp.int32),
        "valid_slot_number": jax.vmap(lambda own: uneven(own, CATALOG_PARTS, KEPT_PER_PERSON, KEPT_PER_PART, 2))(jax.random.split(splits[4], PERSON_NUMBER)).reshape((PERSON_NUMBER, CATALOG_PARTS)).astype(jnp.int32),
        "pair_attributes": noise(splits[5], (PERSON_NUMBER, KEPT_PER_PERSON, CONTEXT_DIM), 1.0, 6.0, ((0, 64), (2, 4))),
        "lowrank_v_matrix": noise(splits[6], (LAYERS, WIDTH, FACTOR_DIM), WIDTH ** -0.5, 0.109375, ((1, 4),)),
        "lowrank_u_matrix": noise(splits[7], (LAYERS, FACTOR_DIM, WIDTH), FACTOR_DIM ** -0.5, 0.25, ((2, 4),)),
        "interaction_offset": noise(splits[8], (LAYERS, WIDTH), 0.5, 3.0, ((1, 4),), jnp.float32),
        "final_projection": noise(splits[9], (WIDTH,), WIDTH ** -0.5, 0.109375, ((0, 4),)),
        "similarity_coefficient": jnp.clip(jax.random.uniform(splits[10], (1,), jnp.float32, 0.5, 1.5), 0.5, 1.5),
    }


def reference(person_embedding, catalog_embedding, catalog_attributes, kept_part_entries, valid_slot_number, pair_attributes, lowrank_v_matrix, lowrank_u_matrix, interaction_offset, final_projection, similarity_coefficient):
    part_holders = N_SHARD * N_TP
    blocks = catalog_embedding.reshape(part_holders, PART_ENTRIES, EMB)

    def block_best(block):
        scores = jnp.dot(person_embedding, block.T, preferred_element_type=jnp.float32)
        return jnp.max(scores, axis=1)

    best = jnp.max(lax.map(block_best, blocks), axis=0)
    beginning_positions = jnp.cumsum(valid_slot_number, axis=1).astype(jnp.int32) - valid_slot_number
    permutation = jnp.arange(KEPT_PER_PERSON, dtype=jnp.int32)
    holder_lookup = jnp.sum((beginning_positions[:, None, :] <= permutation[None, :, None]).astype(jnp.int32), axis=2) - 1
    beginning_lookup = jnp.take_along_axis(beginning_positions, holder_lookup, axis=1)
    linear_entries = kept_part_entries.reshape(PERSON_NUMBER, part_holders * KEPT_PER_PART)
    within_part_entry = jnp.take_along_axis(linear_entries, holder_lookup * KEPT_PER_PART + (permutation[None, :] - beginning_lookup), axis=1)
    item_id = (holder_lookup * PART_ENTRIES + within_part_entry).astype(jnp.int32)
    vec_rows = catalog_embedding[item_id]
    feat_rows = catalog_attributes[item_id]
    logit = jnp.einsum("ue,uke->uk", person_embedding.astype(jnp.float32), vec_rows.astype(jnp.float32))
    message_content = jnp.concatenate([vec_rows, feat_rows], axis=2)
    person_fourth = (EMB + FEAT) // N_TP
    cquart = CONTEXT_DIM // N_TP
    qwidth = person_fourth + cquart
    weight_value = similarity_coefficient[0]

    def rank_user(packed):
        pay, ctx, lgt, top = packed
        pieces = []
        for q in range(N_TP):
            pieces.append(pay[:, q * person_fourth:(q + 1) * person_fourth])
            pieces.append(ctx[:, q * cquart:(q + 1) * cquart])
        x_first = jnp.concatenate(pieces, axis=1)
        x_now = x_first
        for layer in range(LAYERS):
            grand_sum = jnp.zeros((KEPT_PER_PERSON, FACTOR_DIM), jnp.float32)
            for q in range(N_TP):
                term = jnp.dot(x_now[:, q * qwidth:(q + 1) * qwidth], lowrank_v_matrix[layer, q * qwidth:(q + 1) * qwidth], preferred_element_type=jnp.float32).astype(jnp.bfloat16)
                term = lax.optimization_barrier(term)
                grand_sum = grand_sum + term.astype(jnp.float32)
            proj = grand_sum.astype(jnp.bfloat16)
            hidden = jnp.dot(proj, lowrank_u_matrix[layer], preferred_element_type=jnp.float32)
            x_now = (x_first.astype(jnp.float32) * (hidden + interaction_offset[layer]) + x_now.astype(jnp.float32)).astype(jnp.bfloat16)
        score = jnp.sum(x_now.astype(jnp.float32) * final_projection.astype(jnp.float32)[None, :], axis=1)
        return score + weight_value * (lgt - top)

    return lax.map(rank_user, (message_content, pair_attributes, logit, best))
```

```python
import functools

import jax
import jax.numpy as jnp
from jax import lax
from jax.experimental import pallas as pl
from jax.experimental.pallas import tpu as pltpu
from jax.sharding import PartitionSpec as P

BF = jnp.bfloat16
F32 = jnp.float32
AXES = ("shard", "tp")
VMEM = pltpu.CompilerParams(vmem_limit_bytes=56 * 1024 * 1024)


def group_perm(groups, step, member=lambda x, c: True):
    pairs = []
    for g in range(groups):
        for c in range(2):
            for x in range(4):
                if member(x, c):
                    x2, c2 = step(x, c)
                    pairs.append((g * 8 + c * 4 + x, g * 8 + c2 * 4 + x2))
    return pairs


def is_home(x, c):
    return x // 2 == c


def is_away(x, c):
    return x // 2 != c


def near(x, c):
    return (x ^ 1, x // 2) if is_home(x, c) else (x ^ 3, x // 2)


def dot(a, b):
    return jnp.dot(a, b, preferred_element_type=F32)


def dot_nt(a, b):
    return lax.dot_general(a, b, (((1,), (1,)), ((), ())), preferred_element_type=F32)


def pick_kernel(rows_ref, emb_ref, attr_ref, out_ref):
    rows = rows_ref[...]
    n = rows.shape[0]
    items = emb_ref.shape[0]
    hot = (lax.broadcasted_iota(jnp.int32, (n, items), 1) == rows).astype(BF)
    unused = rows < 0
    odd = (lax.broadcasted_iota(jnp.int32, (n, 1), 0) // 8) % 2 == 1
    quarters = [
        jnp.where(unused, jnp.inf, dot(hot, emb_ref[...])),
        jnp.where(unused, jnp.inf, dot(hot, attr_ref[:, 0:256])),
        jnp.where(unused, jnp.inf, dot(hot, attr_ref[:, 256:512])),
        jnp.where(unused, jnp.inf, dot(hot, attr_ref[:, 512:768])),
    ]
    for c in range(2):
        low, high = quarters[2 * c], quarters[2 * c + 1]
        first = jnp.where(odd, low, high).astype(BF)
        second = jnp.where(odd, high, low).astype(BF)
        for g in range(n // 32):
            out_ref[g, c, :, 0:256] = first[g * 32 : (g + 1) * 32]
            out_ref[g, c, :, 256:512] = second[g * 32 : (g + 1) * 32]


def pick_rows(rows, emb, attr):
    n = rows.shape[0]
    steps = 4
    block = n // steps
    return pl.pallas_call(
        pick_kernel,
        grid=(steps,),
        in_specs=[
            pl.BlockSpec((block, 1), lambda i: (i, 0)),
            pl.BlockSpec(emb.shape, lambda i: (0, 0)),
            pl.BlockSpec(attr.shape, lambda i: (0, 0)),
        ],
        out_specs=pl.BlockSpec((block // 32, 2, 32, 512), lambda i: (i, 0, 0, 0)),
        out_shape=jax.ShapeDtypeStruct((n // 32, 2, 32, 512), BF),
        compiler_params=VMEM,
        cost_estimate=pl.CostEstimate(
            flops=2 * n * 2048 * 1024, bytes_accessed=6 << 20, transcendentals=0
        ),
        name="pick_rows",
    )(rows, emb, attr)


def first_kernel(
    recv_ref, ca_ref, cb_ref, va_ref, vb_ref, u_ref, pay_ref, piece_ref, logit_ref, clean, place
):
    step = pl.program_id(0)
    slots = recv_ref.shape[0]
    blk = 256

    @pl.when(step == 0)
    def _():
        r = lax.broadcasted_iota(jnp.int32, (blk, blk), 0)
        q = lax.broadcasted_iota(jnp.int32, (blk, blk), 1)
        upper = (r <= q).astype(BF)
        lane0 = (lax.broadcasted_iota(jnp.int32, (16, 128), 1) == 0).astype(BF)
        before = jnp.zeros((16, 1), F32)
        for i in range(slots // blk):
            got = recv_ref[i * blk : (i + 1) * blk, :].astype(F32)
            live = got < jnp.inf
            clean[i * blk : (i + 1) * blk, :] = jnp.where(live, got, 0.0).astype(BF)
            flags = dot_nt(lane0, live[:, 0:128].astype(F32).astype(BF))
            upto = dot(flags.astype(BF), upper) + before
            place[:, i * blk : (i + 1) * blk] = jnp.where(flags > 0.5, upto - 1.0, -1.0)
            before = upto[:, blk - 1 : blk]

    rows = pay_ref.shape[0]
    k = (lax.broadcasted_iota(jnp.int32, (rows, slots), 0) + step * rows).astype(F32)
    hot = (k == place[0:1, :]).astype(BF)
    pay = dot(hot, clean[...]).astype(BF)
    pay_ref[...] = pay
    piece = (
        dot(pay[:, 0:256], va_ref[0:256])
        + dot(ca_ref[...], va_ref[256:768])
        + dot(pay[:, 256:512], vb_ref[0:256])
        + dot(cb_ref[...], vb_ref[256:768])
    )
    piece_ref[...] = piece.astype(BF)
    logit_ref[...] = dot_nt(u_ref[...], pay)


def first_layer(recv, ctx_a, ctx_b, v_a, v_b, u_rows):
    surv = ctx_a.shape[0]
    steps = 4
    rows = surv // steps

    def full(a):
        return pl.BlockSpec(a.shape, lambda i: (0,) * a.ndim)

    by_row = pl.BlockSpec((rows, 512), lambda i: (i, 0))
    return pl.pallas_call(
        first_kernel,
        grid=(steps,),
        in_specs=[full(recv), by_row, by_row, full(v_a), full(v_b), full(u_rows)],
        out_specs=[by_row, by_row, pl.BlockSpec((16, rows), lambda i: (0, i))],
        out_shape=[
            jax.ShapeDtypeStruct((surv, 512), BF),
            jax.ShapeDtypeStruct((surv, 512), BF),
            jax.ShapeDtypeStruct((16, surv), F32),
        ],
        scratch_shapes=[pltpu.VMEM(recv.shape, BF), pltpu.VMEM((16, recv.shape[0]), F32)],
        compiler_params=VMEM,
        cost_estimate=pl.CostEstimate(flops=4 << 30, bytes_accessed=8 << 20, transcendentals=0),
        name="first_layer",
    )(recv, ctx_a, ctx_b, v_a, v_b, u_rows)


def cross(x0, hidden, offset, x):
    x0 = x0.astype(F32)
    return (x0 * (hidden + offset) + x.astype(F32)).astype(BF)


def second_kernel(
    mine_ref, other_ref, pay_ref, ca_ref, cb_ref, ua_ref, ub_ref, ba_ref, bb_ref, va_ref, vb_ref,
    xa_ref, xb_ref, piece_ref,
):
    proj = (mine_ref[...].astype(F32) + other_ref[...].astype(F32)).astype(BF)
    piece = None
    for x_ref, u_ref, b_ref, v_ref, c_ref, at in (
        (xa_ref, ua_ref, ba_ref, va_ref, ca_ref, 0),
        (xb_ref, ub_ref, bb_ref, vb_ref, cb_ref, 256),
    ):
        hidden = dot(proj, u_ref[...])
        pay = pay_ref[:, at : at + 256]
        x_ref[:, 0:256] = cross(pay, hidden[:, 0:256], b_ref[0:1, 0:256], pay)
        x_ref[:, 256:768] = cross(c_ref[...], hidden[:, 256:768], b_ref[0:1, 256:768], c_ref[...])
        term = dot(x_ref[...], v_ref[...])
        piece = term if piece is None else piece + term
    piece_ref[...] = piece.astype(BF)


def second_layer(mine, other, pay, ctx_a, ctx_b, u_a, u_b, b_a, b_b, v_a, v_b):
    surv = pay.shape[0]
    steps = 4
    rows = surv // steps

    def full(a):
        return pl.BlockSpec(a.shape, lambda i: (0,) * a.ndim)

    by_row = pl.BlockSpec((rows, 512), lambda i: (i, 0))
    wide = pl.BlockSpec((rows, 768), lambda i: (i, 0))
    return pl.pallas_call(
        second_kernel,
        grid=(steps,),
        in_specs=[by_row] * 5 + [full(a) for a in (u_a, u_b, b_a, b_b, v_a, v_b)],
        out_specs=[wide, wide, by_row],
        out_shape=[
            jax.ShapeDtypeStruct((surv, 768), BF),
            jax.ShapeDtypeStruct((surv, 768), BF),
            jax.ShapeDtypeStruct((surv, 512), BF),
        ],
        compiler_params=VMEM,
        cost_estimate=pl.CostEstimate(flops=7 << 29, bytes_accessed=12 << 20, transcendentals=0),
        name="second_layer",
    )(mine, other, pay, ctx_a, ctx_b, u_a, u_b, b_a, b_b, v_a, v_b)


def last_kernel(
    mine_ref, other_ref, pay_ref, ca_ref, cb_ref, xa_ref, xb_ref, ua_ref, ub_ref, ba_ref, bb_ref,
    fa_ref, fb_ref, extra_ref, score_ref,
):
    proj = (mine_ref[...].astype(F32) + other_ref[...].astype(F32)).astype(BF)
    score = extra_ref[...]
    for x_ref, u_ref, b_ref, f_ref, c_ref, at in (
        (xa_ref, ua_ref, ba_ref, fa_ref, ca_ref, 0),
        (xb_ref, ub_ref, bb_ref, fb_ref, cb_ref, 256),
    ):
        hidden = dot(proj, u_ref[...])
        pay = pay_ref[:, at : at + 256]
        low = cross(pay, hidden[:, 0:256], b_ref[0:1, 0:256], x_ref[:, 0:256])
        high = cross(c_ref[...], hidden[:, 256:768], b_ref[0:1, 256:768], x_ref[:, 256:768])
        score = score + dot_nt(f_ref[:, 0:256], low) + dot_nt(f_ref[:, 256:768], high)
    score_ref[...] = score


def last_layer(mine, other, pay, ctx_a, ctx_b, x_a, x_b, u_a, u_b, b_a, b_b, f_a, f_b, extra):
    surv = pay.shape[0]
    steps = 4
    rows = surv // steps

    def full(a):
        return pl.BlockSpec(a.shape, lambda i: (0,) * a.ndim)

    by_row = pl.BlockSpec((rows, 512), lambda i: (i, 0))
    wide = pl.BlockSpec((rows, 768), lambda i: (i, 0))
    lanes = pl.BlockSpec((16, rows), lambda i: (0, i))
    return pl.pallas_call(
        last_kernel,
        grid=(steps,),
        in_specs=[by_row] * 5
        + [wide, wide]
        + [full(a) for a in (u_a, u_b, b_a, b_b, f_a, f_b)]
        + [lanes],
        out_specs=lanes,
        out_shape=jax.ShapeDtypeStruct((16, surv), F32),
        compiler_params=VMEM,
        cost_estimate=pl.CostEstimate(flops=7 << 28, bytes_accessed=10 << 20, transcendentals=0),
        name="last_layer",
    )(mine, other, pay, ctx_a, ctx_b, x_a, x_b, u_a, u_b, b_a, b_b, f_a, f_b, extra)


def on_device(
    person_embedding,
    catalog_embedding,
    catalog_attributes,
    kept_part_entries,
    valid_slot_number,
    pair_attributes,
    lowrank_v_matrix,
    lowrank_u_matrix,
    interaction_offset,
    final_projection,
    similarity_coefficient,
):
    shards = lax.axis_size("shard")
    groups = shards // 2
    x = lax.axis_index("tp")
    core = lax.axis_index("shard") % 2
    home = x // 2 == core
    parity = x % 2
    move = functools.partial(lax.ppermute, axis_name=AXES)
    to_core = group_perm(groups, lambda x, c: (x, 1 - c))
    to_near = group_perm(groups, near)
    home_on = group_perm(groups, lambda x, c: (x ^ 3, c), is_home)
    away_swap = group_perm(groups, lambda x, c: (x ^ 1, c), is_away)
    ctx_near = group_perm(groups, lambda x, c: (x ^ 1, c) if is_home(x, c) else (x ^ 3, 1 - c))
    ctx_far = group_perm(groups, lambda x, c: (x ^ 2, 1 - c), is_away)

    persons, _, kept = kept_part_entries.shape
    slot = jnp.arange(kept, dtype=jnp.int32)[None, :]
    rows = jnp.where(slot < valid_slot_number, kept_part_entries[:, 0, :], -1)
    parcel = pick_rows(rows.reshape(persons * kept, 1), catalog_embedding, catalog_attributes)
    parcel = parcel.reshape(persons * 2, kept, 512)
    recv = lax.all_to_all(parcel, AXES, split_axis=0, concat_axis=0, tiled=True)
    recv = recv.reshape(persons * 2 * kept, 512)

    ctx_a = move(lax.dynamic_index_in_dim(pair_attributes, 1 - parity, 0, False), perm=ctx_near)
    ctx_own = lax.dynamic_index_in_dim(pair_attributes, parity, 0, False)
    ctx_b = jnp.where(home, ctx_own, move(ctx_own, perm=ctx_far))

    small = jnp.concatenate([interaction_offset, final_projection[None, :].astype(F32)], 0)
    v_a = move(lowrank_v_matrix, perm=to_near)
    u_a = move(lowrank_u_matrix, perm=to_near)
    small_a = move(small, perm=to_near)
    v_b = jnp.where(home, lowrank_v_matrix, move(v_a, perm=home_on))
    u_b = jnp.where(home, lowrank_u_matrix, move(u_a, perm=away_swap))
    small_b = jnp.where(home, small, move(small_a, perm=home_on))

    users = person_embedding[None]
    width = 1
    while width < shards:
        pairs = [(i, i ^ width) for i in range(shards)]
        users = jnp.concatenate([users, lax.ppermute(users, "shard", pairs)], 0)
        width *= 2
    all_scores = jnp.einsum(
        "ue,ie->ui", users.reshape(persons, -1), catalog_embedding, preferred_element_type=F32
    )
    best = jnp.max(all_scores, axis=1).reshape(shards, persons // shards)
    while width > 1:
        width //= 2
        pairs = [(i, i ^ width) for i in range(shards)]
        best = jnp.maximum(best[:width], lax.ppermute(best[width:], "shard", pairs))
    for flip in (1, 2):
        best = jnp.maximum(best, lax.ppermute(best, "tp", [(i, i ^ flip) for i in range(4)]))

    emb_other = move(person_embedding, perm=to_core)
    query = lax.dynamic_slice_in_dim(jnp.where(home, person_embedding, emb_other), parity, 1, 0)
    query = jnp.where(core == 0, query, jnp.zeros_like(query))
    zero = jnp.zeros_like(query)
    query = jnp.where(
        parity == 1, jnp.concatenate([query, zero], 1), jnp.concatenate([zero, query], 1)
    )
    query = jnp.broadcast_to(query, (16, 512))

    pay, piece, logit = first_layer(recv, ctx_a, ctx_b, v_a[0], v_b[0], query)
    other = move(piece, perm=to_core)
    x_a, x_b, piece1 = second_layer(
        piece, other, pay, ctx_a, ctx_b, u_a[0], u_b[0], small_a[0:1], small_b[0:1], v_a[1], v_b[1]
    )
    other1 = move(piece1, perm=to_core)
    top = jnp.where(home, lax.dynamic_slice_in_dim(best, parity, 1, 1), 0.0)
    extra = similarity_coefficient[0] * (logit - top)
    f_a = jnp.broadcast_to(small_a[2:3], (16, 768)).astype(BF)
    f_b = jnp.broadcast_to(small_b[2:3], (16, 768)).astype(BF)
    score = last_layer(
        piece1, other1, pay, ctx_a, ctx_b, x_a, x_b, u_a[1], u_b[1], small_a[1:2], small_b[1:2],
        f_a, f_b, extra,
    )[0:1]
    score = score + move(score, perm=to_core)
    score_a = move(score, perm=to_near)
    score_b = jnp.where(home, score, move(score, perm=ctx_far))
    return jnp.where(
        parity == 1,
        jnp.concatenate([score_a, score_b], 0),
        jnp.concatenate([score_b, score_a], 0),
    )


def solution(mesh):
    return jax.shard_map(
        on_device,
        mesh=mesh,
        in_specs=(
            P("shard", None),
            P(("shard", "tp"), None),
            P(("shard", "tp"), None),
            P(None, ("shard", "tp"), None),
            P(None, ("shard", "tp")),
            P("shard", None, "tp"),
            P(None, "tp", None),
            P(None, None, "tp"),
            P(None, "tp"),
            P("tp"),
            P(),
        ),
        out_specs=P("shard", None),
        check_vma=False,
    )
```

```python
import functools

import jax
import jax.numpy as jnp
from jax import lax
from jax.experimental import pallas as pl
from jax.experimental.pallas import tpu as pltpu
from jax.sharding import PartitionSpec as P

BF = jnp.bfloat16
F32 = jnp.float32
AXES = ("shard", "tp")
VMEM = pl.BlockSpec(memory_space=pltpu.VMEM)
SMEM = pl.BlockSpec(memory_space=pltpu.SMEM)
PARAMS = pltpu.CompilerParams(vmem_limit_bytes=24 * 1024 * 1024)


def group_perm(groups, step, member=lambda x, c: True, turn=lambda x, c: 0):
    pairs = []
    for g in range(groups):
        for c in range(2):
            for x in range(4):
                if member(x, c):
                    x2, c2 = step(x, c)
                    g2 = g // 4 * 4 + (g + turn(x, c)) % 4
                    pairs.append((g * 8 + c * 4 + x, g2 * 8 + c2 * 4 + x2))
    return pairs


def is_home(x, c):
    return x // 2 == c


def is_away(x, c):
    return x // 2 != c


def near(x, c):
    return (x ^ 1, x // 2) if is_home(x, c) else (x ^ 3, x // 2)


def dot(a, b):
    return jnp.dot(a, b, preferred_element_type=F32)


def dot_nt(a, b):
    return lax.dot_general(a, b, (((1,), (1,)), ((), ())), preferred_element_type=F32)


def in_vmem(kernel, name, outs, scratch, mflops, mbytes, scalars, arrays):
    return pl.pallas_call(
        kernel,
        in_specs=[SMEM] * len(scalars) + [VMEM] * len(arrays),
        out_specs=[VMEM] * len(outs),
        out_shape=[jax.ShapeDtypeStruct(shape, dtype) for shape, dtype in outs],
        scratch_shapes=scratch,
        compiler_params=PARAMS,
        cost_estimate=pl.CostEstimate(
            flops=mflops << 20, bytes_accessed=mbytes << 20, transcendentals=0
        ),
        name=name,
    )(*scalars, *arrays)


def pick_kernel(kept_ref, count_ref, emb_ref, attr_ref, out_ref):
    slots, persons = kept_ref.shape
    items = emb_ref.shape[0]
    live = lax.broadcasted_iota(jnp.int32, (slots, persons), 0) < count_ref[...]
    wanted = jnp.where(live, kept_ref[...], 4095)
    digits = jnp.concatenate([wanted >> 6, wanted & 63], 0).astype(F32).astype(BF)
    n = 256
    for at in range(0, persons * slots, n):
        row = lax.broadcasted_iota(jnp.int32, (n, persons), 0) + at
        owner = (row // slots == lax.broadcasted_iota(jnp.int32, (n, persons), 1)).astype(BF)
        both = dot_nt(owner, digits)
        lane = lax.broadcasted_iota(jnp.int32, (n, 2 * slots), 1)
        slot = lax.broadcasted_iota(jnp.int32, (n, 2 * slots), 0) % slots
        high = jnp.where(lane == slot, both * 64.0, 0.0)
        low = jnp.where(lane == slot + slots, both, 0.0)
        rows = jnp.sum(high + low, axis=1, keepdims=True).astype(jnp.int32)
        hot = (lax.broadcasted_iota(jnp.int32, (n, items), 1) == rows).astype(BF)
        unused = rows >= items
        odd = (lax.broadcasted_iota(jnp.int32, (n, 1), 0) // slots) % 2 == 1
        for c in range(2):
            tables = (
                (emb_ref[...], attr_ref[:, 0:256])
                if c == 0
                else (attr_ref[:, 256:512], attr_ref[:, 512:768])
            )
            low, high = (jnp.where(unused, jnp.inf, dot(hot, t)) for t in tables)
            first = jnp.where(odd, low, high).astype(BF)
            second = jnp.where(odd, high, low).astype(BF)
            for g in range(n // 32):
                out_ref[at // 32 + g, c, :, 0:256] = first[g * 32 : (g + 1) * 32]
                out_ref[at // 32 + g, c, :, 256:512] = second[g * 32 : (g + 1) * 32]


def choose(flags, layer, own, near_x, far_x, near_y, far_y, dst_a, dst_b):
    home = flags[0] == 1
    by_x = flags[1] == layer
    dst_a[...] = jnp.where(by_x, near_x[...], near_y[...])
    dst_b[...] = jnp.where(home, own[layer], jnp.where(by_x, far_x[...], far_y[...]))


def first_kernel(
    flags, recv_ref, ca_ref, cb_ref, u_ref, v0, v1, v2, v3, v4, pay_ref, piece_ref, logit_ref,
    clean, place, va_ref, vb_ref,
):
    slots = recv_ref.shape[0]
    blk = 256
    choose(flags, 0, v0, v1, v2, v3, v4, va_ref, vb_ref)
    r = lax.broadcasted_iota(jnp.int32, (blk, blk), 0)
    q = lax.broadcasted_iota(jnp.int32, (blk, blk), 1)
    upper = (r <= q).astype(BF)
    lane0 = (lax.broadcasted_iota(jnp.int32, (16, 128), 1) == 0).astype(BF)
    before = jnp.zeros((16, 1), F32)
    for i in range(slots // blk):
        got = recv_ref[i * blk : (i + 1) * blk, :].astype(F32)
        live = got < jnp.inf
        clean[i * blk : (i + 1) * blk, :] = jnp.where(live, got, 0.0).astype(BF)
        marks = dot_nt(lane0, live[:, 0:128].astype(F32).astype(BF))
        upto = dot(marks.astype(BF), upper) + before
        place[:, i * blk : (i + 1) * blk] = jnp.where(marks > 0.5, upto - 1.0, -1.0)
        before = upto[:, blk - 1 : blk]
    rows = 256
    for at in range(0, pay_ref.shape[0], rows):
        here = pl.ds(at, rows)
        k = (lax.broadcasted_iota(jnp.int32, (rows, slots), 0) + at).astype(F32)
        hot = (k == place[0:1, :]).astype(BF)
        pay = dot(hot, clean[...]).astype(BF)
        pay_ref[here] = pay
        piece = (
            dot(pay[:, 0:256], va_ref[0:256])
            + dot(ca_ref[here], va_ref[256:768])
            + dot(pay[:, 256:512], vb_ref[0:256])
            + dot(cb_ref[here], vb_ref[256:768])
        )
        piece_ref[here] = piece.astype(BF)
        logit_ref[:, here] = dot_nt(u_ref[...], pay)


def cross(x0, hidden, offset, x):
    x0 = x0.astype(F32)
    return (x0 * (hidden + offset) + x.astype(F32)).astype(BF)


def second_kernel(
    flags, mine_ref, other_ref, pay_ref, ca_ref, cb_ref, ba_ref, bb_ref,
    u0, u1, u2, u3, u4, v0, v1, v2, v3, v4,
    xa_ref, xb_ref, piece_ref, ua_ref, ub_ref, va_ref, vb_ref,
):
    choose(flags, 0, u0, u1, u2, u3, u4, ua_ref, ub_ref)
    choose(flags, 1, v0, v1, v2, v3, v4, va_ref, vb_ref)
    rows = 256
    for start in range(0, pay_ref.shape[0], rows):
        here = pl.ds(start, rows)
        proj = (mine_ref[here].astype(F32) + other_ref[here].astype(F32)).astype(BF)
        piece = None
        for x_ref, u_ref, b_ref, v_ref, c_ref, at in (
            (xa_ref, ua_ref, ba_ref, va_ref, ca_ref, 0),
            (xb_ref, ub_ref, bb_ref, vb_ref, cb_ref, 256),
        ):
            hidden = dot(proj, u_ref[...])
            pay = pay_ref[here, at : at + 256]
            ctx = c_ref[here]
            x_ref[here, 0:256] = cross(pay, hidden[:, 0:256], b_ref[0:1, 0:256], pay)
            x_ref[here, 256:768] = cross(ctx, hidden[:, 256:768], b_ref[0:1, 256:768], ctx)
            term = dot(x_ref[here], v_ref[...])
            piece = term if piece is None else piece + term
        piece_ref[here] = piece.astype(BF)


def last_kernel(
    flags, coefficient, mine_ref, other_ref, pay_ref, ca_ref, cb_ref, xa_ref, xb_ref,
    sa_ref, sb_ref, logit_ref, u0, u1, u2, u3, u4, score_ref, ua_ref, ub_ref,
):
    choose(flags, 1, u0, u1, u2, u3, u4, ua_ref, ub_ref)
    rows = 256
    for start in range(0, pay_ref.shape[0], rows):
        here = pl.ds(start, rows)
        proj = (mine_ref[here].astype(F32) + other_ref[here].astype(F32)).astype(BF)
        score = coefficient[0] * logit_ref[:, here]
        for x_ref, u_ref, s_ref, c_ref, at in (
            (xa_ref, ua_ref, sa_ref, ca_ref, 0),
            (xb_ref, ub_ref, sb_ref, cb_ref, 256),
        ):
            hidden = dot(proj, u_ref[...])
            low = cross(
                pay_ref[here, at : at + 256], hidden[:, 0:256], s_ref[1:2, 0:256], x_ref[here, 0:256]
            )
            high = cross(
                c_ref[here], hidden[:, 256:768], s_ref[1:2, 256:768], x_ref[here, 256:768]
            )
            out = jnp.broadcast_to(s_ref[2:3, :], (16, 768)).astype(BF)
            score = score + dot_nt(out[:, 0:256], low) + dot_nt(out[:, 256:768], high)
        score_ref[:, here] = score


def on_device(
    person_embedding,
    catalog_embedding,
    catalog_attributes,
    kept_part_entries,
    valid_slot_number,
    pair_attributes,
    lowrank_v_matrix,
    lowrank_u_matrix,
    interaction_offset,
    final_projection,
    similarity_coefficient,
):
    shards = lax.axis_size("shard")
    groups = shards // 2
    x = lax.axis_index("tp")
    core = lax.axis_index("shard") % 2
    home = x // 2 == core
    parity = x % 2
    move = functools.partial(lax.ppermute, axis_name=AXES)
    to_core = group_perm(groups, lambda x, c: (x, 1 - c))
    to_near = group_perm(groups, near)
    home_on = group_perm(groups, lambda x, c: (x ^ 3, c), is_home)
    away_swap = group_perm(groups, lambda x, c: (x ^ 1, c), is_away)
    ctx_near = group_perm(groups, lambda x, c: (x ^ 1, c) if is_home(x, c) else (x ^ 3, 1 - c))
    ctx_far = group_perm(groups, lambda x, c: (x ^ 2, 1 - c), is_away)
    stay = lambda x, c: (x, c)
    y_up = group_perm(groups, stay, turn=lambda x, c: 1)
    y_mixed = group_perm(groups, stay, turn=lambda x, c: -1 if is_home(x, c) else 1)
    y_down = group_perm(groups, stay, is_away, lambda x, c: -1)
    by = lax.axis_index("shard") // 2 % 2
    flags = jnp.stack([home.astype(jnp.int32), by])

    persons, _, kept = kept_part_entries.shape
    small = jnp.concatenate([interaction_offset, final_projection[None, :].astype(F32)], 0)
    small_a = move(small, perm=to_near)
    small_b = move(small, perm=ctx_far)
    emb_other = move(person_embedding, perm=to_core)
    masks = (16, 32, 8, 2, 4, 1)
    users = person_embedding[None]

    def double(users, mask):
        pairs = [(i, i ^ mask) for i in range(shards)]
        return jnp.concatenate([users, lax.ppermute(users, "shard", pairs)], 0)

    for mask in masks[:3]:
        users = double(users, mask)

    v_mine = lax.dynamic_index_in_dim(lowrank_v_matrix, by, 0, False)
    u_mine = lax.dynamic_index_in_dim(lowrank_u_matrix, by, 0, False)
    v_near = move(v_mine, perm=to_near)

    (parcel,) = in_vmem(
        pick_kernel, "pick_rows", [((persons // 4, 2, 4 * kept, 512), BF)], [], 4096, 6, [],
        [
            kept_part_entries[:, 0, :].T,
            valid_slot_number.T,
            catalog_embedding,
            catalog_attributes,
        ],
    )
    parcel = parcel.reshape(persons * 2, kept, 512)
    parcel, v_near, small_a, small_b, emb_other, users = lax.optimization_barrier(
        (parcel, v_near, small_a, small_b, emb_other, users)
    )
    recv = lax.all_to_all(parcel, AXES, split_axis=0, concat_axis=0, tiled=True)
    recv = recv.reshape(persons * 2 * kept, 512)

    u_near = move(u_mine, perm=to_near)
    v_far = move(v_near, perm=home_on)
    u_far = move(u_near, perm=away_swap)
    vs = (lowrank_v_matrix, v_near, v_far, move(v_near, perm=y_up), move(v_far, perm=y_down))
    us = (lowrank_u_matrix, u_near, u_far, move(u_near, perm=y_mixed), move(u_far, perm=y_down))
    small_b = jnp.where(home, small, small_b)

    ctx_a = move(lax.dynamic_index_in_dim(pair_attributes, 1 - parity, 0, False), perm=ctx_near)
    ctx_own = lax.dynamic_index_in_dim(pair_attributes, parity, 0, False)
    ctx_b = jnp.where(home, ctx_own, move(ctx_own, perm=ctx_far))

    for mask in masks[3:]:
        users = double(users, mask)
    all_scores = jnp.einsum(
        "ue,ie->ui", users.reshape(persons, -1), catalog_embedding, preferred_element_type=F32
    )
    best = jnp.max(all_scores, axis=1).reshape(shards, persons // shards)

    def halve(best, mask):
        half = best.shape[0] // 2
        pairs = [(i, i ^ mask) for i in range(shards)]
        return jnp.maximum(best[:half], lax.ppermute(best[half:], "shard", pairs))

    def over_x(best, flip):
        return jnp.maximum(best, lax.ppermute(best, "tp", [(i, i ^ flip) for i in range(4)]))

    for mask in masks[:2:-1]:
        best = halve(best, mask)

    query = lax.dynamic_slice_in_dim(jnp.where(home, person_embedding, emb_other), parity, 1, 0)
    query = jnp.where(core == 0, query, jnp.zeros_like(query))
    zero = jnp.zeros_like(query)
    query = jnp.where(
        parity == 1, jnp.concatenate([query, zero], 1), jnp.concatenate([zero, query], 1)
    )
    query = jnp.broadcast_to(query, (16, 512))

    surv = pair_attributes.shape[1]
    tall, wide, lanes = ((surv, 512), BF), ((surv, 768), BF), ((16, surv), F32)
    v_pair = [pltpu.VMEM((768, 512), BF)] * 2
    u_pair = [pltpu.VMEM((512, 768), BF)] * 2
    recv, best = lax.optimization_barrier((recv, best))
    step = over_x(best, 1)
    pay, piece, logit = in_vmem(
        first_kernel, "first_layer", [tall, tall, lanes],
        [pltpu.VMEM(recv.shape, BF), pltpu.VMEM((16, recv.shape[0]), F32)] + v_pair,
        4096, 8, [flags], [recv, ctx_a, ctx_b, query, *vs],
    )
    piece, best = lax.optimization_barrier((piece, step))
    other, best = lax.optimization_barrier((move(piece, perm=to_core), over_x(best, 2)))
    step = halve(best, masks[2])
    x_a, x_b, piece1 = in_vmem(
        second_kernel, "second_layer", [wide, wide, tall], u_pair + v_pair, 3584, 12, [flags],
        [piece, other, pay, ctx_a, ctx_b, small_a, small_b, *us, *vs],
    )
    piece1, best = lax.optimization_barrier((piece1, step))
    other1, best = lax.optimization_barrier((move(piece1, perm=to_core), halve(best, masks[1])))
    step = halve(best, masks[0])
    (score,) = in_vmem(
        last_kernel, "last_layer", [lanes], u_pair, 1792, 10, [flags, similarity_coefficient],
        [piece1, other1, pay, ctx_a, ctx_b, x_a, x_b, small_a, small_b, logit, *us],
    )
    score, best = lax.optimization_barrier((score, step))
    top = jnp.where(home, lax.dynamic_slice_in_dim(best, parity, 1, 1), 0.0)
    score = score[0:1] - similarity_coefficient[0] * top
    score = score + move(score, perm=to_core)
    score_a = move(score, perm=to_near)
    score_b = jnp.where(home, score, move(score, perm=ctx_far))
    return jnp.where(
        parity == 1,
        jnp.concatenate([score_a, score_b], 0),
        jnp.concatenate([score_b, score_a], 0),
    )


def solution(mesh):
    return jax.shard_map(
        on_device,
        mesh=mesh,
        in_specs=(
            P("shard", None),
            P(("shard", "tp"), None),
            P(("shard", "tp"), None),
            P(None, ("shard", "tp"), None),
            P(None, ("shard", "tp")),
            P("shard", None, "tp"),
            P(None, "tp", None),
            P(None, None, "tp"),
            P(None, "tp"),
            P("tp"),
            P(),
        ),
        out_specs=P("shard", None),
        check_vma=False,
    )
```

```python
import functools

import jax
import jax.numpy as jnp
from jax import lax
from jax.experimental import pallas as pl
from jax.experimental.pallas import tpu as pltpu
from jax.sharding import PartitionSpec as P

BF = jnp.bfloat16
F32 = jnp.float32
AXES = ("shard", "tp")
VMEM = pl.BlockSpec(memory_space=pltpu.VMEM)
PICK, CTX, FIRST = 4096, 20000, 15000
SMEM = pl.BlockSpec(memory_space=pltpu.SMEM)
PARAMS = pltpu.CompilerParams(vmem_limit_bytes=24 * 1024 * 1024)


def group_perm(groups, step, member=lambda x, c: True, turn=lambda x, c: 0):
    pairs = []
    for g in range(groups):
        for c in range(2):
            for x in range(4):
                if member(x, c):
                    x2, c2 = step(x, c)
                    g2 = g // 4 * 4 + (g + turn(x, c)) % 4
                    pairs.append((g * 8 + c * 4 + x, g2 * 8 + c2 * 4 + x2))
    return pairs


def is_home(x, c):
    return x // 2 == c


def is_away(x, c):
    return x // 2 != c


def near(x, c):
    return (x ^ 1, x // 2) if is_home(x, c) else (x ^ 3, x // 2)


def dot(a, b):
    return jnp.dot(a, b, preferred_element_type=F32)


def dot_nt(a, b):
    return lax.dot_general(a, b, (((1,), (1,)), ((), ())), preferred_element_type=F32)


def in_vmem(kernel, name, outs, scratch, mflops, mbytes, scalars, arrays):
    return pl.pallas_call(
        kernel,
        in_specs=[SMEM] * len(scalars) + [VMEM] * len(arrays),
        out_specs=[VMEM] * len(outs),
        out_shape=[jax.ShapeDtypeStruct(shape, dtype) for shape, dtype in outs],
        scratch_shapes=scratch,
        compiler_params=PARAMS,
        cost_estimate=pl.CostEstimate(
            flops=mflops << 20, bytes_accessed=mbytes << 20, transcendentals=0
        ),
        name=name,
    )(*scalars, *arrays)


def pick_kernel(kept_ref, count_ref, emb_ref, attr_ref, out_ref):
    slots, persons = kept_ref.shape
    items = emb_ref.shape[0]
    live = lax.broadcasted_iota(jnp.int32, (slots, persons), 0) < count_ref[...]
    wanted = jnp.where(live, kept_ref[...], 4095)
    digits = jnp.concatenate([wanted >> 6, wanted & 63], 0).astype(F32).astype(BF)
    n = 256
    for at in range(0, persons * slots, n):
        row = lax.broadcasted_iota(jnp.int32, (n, persons), 0) + at
        owner = (row // slots == lax.broadcasted_iota(jnp.int32, (n, persons), 1)).astype(BF)
        both = dot_nt(owner, digits)
        lane = lax.broadcasted_iota(jnp.int32, (n, 2 * slots), 1)
        slot = lax.broadcasted_iota(jnp.int32, (n, 2 * slots), 0) % slots
        high = jnp.where(lane == slot, both * 64.0, 0.0)
        low = jnp.where(lane == slot + slots, both, 0.0)
        rows = jnp.sum(high + low, axis=1, keepdims=True).astype(jnp.int32)
        hot = (lax.broadcasted_iota(jnp.int32, (n, items), 1) == rows).astype(BF)
        unused = rows >= items
        odd = (lax.broadcasted_iota(jnp.int32, (n, 1), 0) // slots) % 2 == 1
        for c in range(2):
            tables = (
                (emb_ref[...], attr_ref[:, 0:256])
                if c == 0
                else (attr_ref[:, 256:512], attr_ref[:, 512:768])
            )
            low, high = (jnp.where(unused, jnp.inf, dot(hot, t)) for t in tables)
            first = jnp.where(odd, low, high).astype(BF)
            second = jnp.where(odd, high, low).astype(BF)
            for g in range(n // 32):
                out_ref[at // 32 + g, c, :, 0:256] = first[g * 32 : (g + 1) * 32]
                out_ref[at // 32 + g, c, :, 256:512] = second[g * 32 : (g + 1) * 32]


def choose(flags, layer, own, near_x, far_x, near_y, far_y, dst_a, dst_b):
    home = flags[0] == 1
    by_x = flags[1] == layer
    dst_a[...] = jnp.where(by_x, near_x[...], near_y[...])
    dst_b[...] = jnp.where(home, own[layer], jnp.where(by_x, far_x[...], far_y[...]))


def context_kernel(
    flags, ca_ref, cb_ref, v0, v1, v2, v3, v4, part_ref, pa_ref, pb_ref, va_ref, vb_ref
):
    choose(flags, 0, v0, v1, v2, v3, v4, va_ref, vb_ref)
    pa_ref[...] = va_ref[0:256]
    pb_ref[...] = vb_ref[0:256]
    rows = 256
    for at in range(0, part_ref.shape[0], rows):
        here = pl.ds(at, rows)
        part_ref[here] = dot(ca_ref[here], va_ref[256:768]) + dot(cb_ref[here], vb_ref[256:768])


def first_kernel(
    recv_ref, part_ref, u_ref, pa_ref, pb_ref, pay_ref, piece_ref, logit_ref, clean, place
):
    slots = recv_ref.shape[0]
    blk = 256
    r = lax.broadcasted_iota(jnp.int32, (blk, blk), 0)
    q = lax.broadcasted_iota(jnp.int32, (blk, blk), 1)
    upper = (r <= q).astype(BF)
    lane0 = (lax.broadcasted_iota(jnp.int32, (16, 128), 1) == 0).astype(BF)
    before = jnp.zeros((16, 1), F32)
    for i in range(slots // blk):
        got = recv_ref[i * blk : (i + 1) * blk, :].astype(F32)
        live = got < jnp.inf
        clean[i * blk : (i + 1) * blk, :] = jnp.where(live, got, 0.0).astype(BF)
        marks = dot_nt(lane0, live[:, 0:128].astype(F32).astype(BF))
        upto = dot(marks.astype(BF), upper) + before
        place[:, i * blk : (i + 1) * blk] = jnp.where(marks > 0.5, upto - 1.0, -1.0)
        before = upto[:, blk - 1 : blk]
    rows = 256
    for at in range(0, pay_ref.shape[0], rows):
        here = pl.ds(at, rows)
        k = (lax.broadcasted_iota(jnp.int32, (rows, slots), 0) + at).astype(F32)
        hot = (k == place[0:1, :]).astype(BF)
        pay = dot(hot, clean[...]).astype(BF)
        pay_ref[here] = pay
        piece = part_ref[here] + dot(pay[:, 0:256], pa_ref[...]) + dot(pay[:, 256:512], pb_ref[...])
        piece_ref[here] = piece.astype(BF)
        logit_ref[:, here] = dot_nt(u_ref[...], pay)


def cross(x0, hidden, offset, x):
    x0 = x0.astype(F32)
    return (x0 * (hidden + offset) + x.astype(F32)).astype(BF)


def second_kernel(
    flags, mine_ref, other_ref, pay_ref, ca_ref, cb_ref, ba_ref, bb_ref,
    u0, u1, u2, u3, u4, v0, v1, v2, v3, v4,
    xa_ref, xb_ref, piece_ref, ua_ref, ub_ref, va_ref, vb_ref,
):
    choose(flags, 0, u0, u1, u2, u3, u4, ua_ref, ub_ref)
    choose(flags, 1, v0, v1, v2, v3, v4, va_ref, vb_ref)
    rows = 256
    for start in range(0, pay_ref.shape[0], rows):
        here = pl.ds(start, rows)
        proj = (mine_ref[here].astype(F32) + other_ref[here].astype(F32)).astype(BF)
        piece = None
        for x_ref, u_ref, b_ref, v_ref, c_ref, at in (
            (xa_ref, ua_ref, ba_ref, va_ref, ca_ref, 0),
            (xb_ref, ub_ref, bb_ref, vb_ref, cb_ref, 256),
        ):
            hidden = dot(proj, u_ref[...])
            pay = pay_ref[here, at : at + 256]
            ctx = c_ref[here]
            x_ref[here, 0:256] = cross(pay, hidden[:, 0:256], b_ref[0:1, 0:256], pay)
            x_ref[here, 256:768] = cross(ctx, hidden[:, 256:768], b_ref[0:1, 256:768], ctx)
            term = dot(x_ref[here], v_ref[...])
            piece = term if piece is None else piece + term
        piece_ref[here] = piece.astype(BF)


def last_kernel(
    flags, coefficient, mine_ref, other_ref, pay_ref, ca_ref, cb_ref, xa_ref, xb_ref,
    sa_ref, sb_ref, logit_ref, u0, u1, u2, u3, u4, score_ref, ua_ref, ub_ref,
):
    choose(flags, 1, u0, u1, u2, u3, u4, ua_ref, ub_ref)
    rows = 256
    for start in range(0, pay_ref.shape[0], rows):
        here = pl.ds(start, rows)
        proj = (mine_ref[here].astype(F32) + other_ref[here].astype(F32)).astype(BF)
        score = coefficient[0] * logit_ref[:, here]
        for x_ref, u_ref, s_ref, c_ref, at in (
            (xa_ref, ua_ref, sa_ref, ca_ref, 0),
            (xb_ref, ub_ref, sb_ref, cb_ref, 256),
        ):
            hidden = dot(proj, u_ref[...])
            low = cross(
                pay_ref[here, at : at + 256], hidden[:, 0:256], s_ref[1:2, 0:256], x_ref[here, 0:256]
            )
            high = cross(
                c_ref[here], hidden[:, 256:768], s_ref[1:2, 256:768], x_ref[here, 256:768]
            )
            out = jnp.broadcast_to(s_ref[2:3, :], (16, 768)).astype(BF)
            score = score + dot_nt(out[:, 0:256], low) + dot_nt(out[:, 256:768], high)
        score_ref[:, here] = score


def on_device(
    person_embedding,
    catalog_embedding,
    catalog_attributes,
    kept_part_entries,
    valid_slot_number,
    pair_attributes,
    lowrank_v_matrix,
    lowrank_u_matrix,
    interaction_offset,
    final_projection,
    similarity_coefficient,
):
    shards = lax.axis_size("shard")
    groups = shards // 2
    x = lax.axis_index("tp")
    core = lax.axis_index("shard") % 2
    home = x // 2 == core
    parity = x % 2
    move = functools.partial(lax.ppermute, axis_name=AXES)
    to_core = group_perm(groups, lambda x, c: (x, 1 - c))
    to_near = group_perm(groups, near)
    home_on = group_perm(groups, lambda x, c: (x ^ 3, c), is_home)
    away_swap = group_perm(groups, lambda x, c: (x ^ 1, c), is_away)
    ctx_near = group_perm(groups, lambda x, c: (x ^ 1, c) if is_home(x, c) else (x ^ 3, 1 - c))
    ctx_far = group_perm(groups, lambda x, c: (x ^ 2, 1 - c), is_away)
    stay = lambda x, c: (x, c)
    y_up = group_perm(groups, stay, turn=lambda x, c: 1)
    y_mixed = group_perm(groups, stay, turn=lambda x, c: -1 if is_home(x, c) else 1)
    y_down = group_perm(groups, stay, is_away, lambda x, c: -1)
    by = lax.axis_index("shard") // 2 % 2
    flags = jnp.stack([home.astype(jnp.int32), by])

    persons, _, kept = kept_part_entries.shape
    masks = (16, 32, 8, 2, 4, 1)
    users = person_embedding[None]

    def double(users, mask):
        pairs = [(i, i ^ mask) for i in range(shards)]
        return jnp.concatenate([users, lax.ppermute(users, "shard", pairs)], 0)

    for mask in masks[:3]:
        users = double(users, mask)
    v_mine = lax.dynamic_index_in_dim(lowrank_v_matrix, by, 0, False)
    u_mine = lax.dynamic_index_in_dim(lowrank_u_matrix, by, 0, False)
    v_near = move(v_mine, perm=to_near)
    u_near = move(u_mine, perm=to_near)
    (parcel,) = in_vmem(
        pick_kernel, "pick_rows", [((persons // 4, 2, 4 * kept, 512), BF)], [], PICK, 6, [],
        [
            kept_part_entries[:, 0, :].T,
            valid_slot_number.T,
            catalog_embedding,
            catalog_attributes,
        ],
    )

    parcel = parcel.reshape(persons * 2, kept, 512)
    parcel, v_near, u_near, users = lax.optimization_barrier((parcel, v_near, u_near, users))
    recv = lax.all_to_all(parcel, AXES, split_axis=0, concat_axis=0, tiled=True)
    recv = recv.reshape(persons * 2 * kept, 512)

    small = jnp.concatenate([interaction_offset, final_projection[None, :].astype(F32)], 0)
    small, v_near, u_near = lax.optimization_barrier((small, v_near, u_near))
    small_a = move(small, perm=to_near)
    small_b = move(small, perm=ctx_far)
    v_far = move(v_near, perm=home_on)
    u_far = move(u_near, perm=away_swap)
    v_near_y = move(v_near, perm=y_up)
    u_near_y = move(u_near, perm=y_mixed)

    ctx_away = lax.dynamic_index_in_dim(pair_attributes, 1 - parity, 0, False)
    ctx_own = lax.dynamic_index_in_dim(pair_attributes, parity, 0, False)
    ctx_away, ctx_own, small_a, small_b = lax.optimization_barrier(
        (ctx_away, ctx_own, small_a, small_b)
    )
    ctx_a = move(ctx_away, perm=ctx_near)
    ctx_b = jnp.where(home, ctx_own, move(ctx_own, perm=ctx_far))
    small_b = jnp.where(home, small, small_b)
    v_far, users = lax.optimization_barrier((v_far, users))
    ctx_a, u_far, u_near_y = lax.optimization_barrier((ctx_a, u_far, u_near_y))
    vs = (lowrank_v_matrix, v_near, v_far, v_near_y, move(v_far, perm=y_down))
    us = (lowrank_u_matrix, u_near, u_far, u_near_y, move(u_far, perm=y_down))

    for mask in masks[3:]:
        users = double(users, mask)
    all_scores = jnp.einsum(
        "ue,ie->ui", users.reshape(persons, -1), catalog_embedding, preferred_element_type=F32
    )
    best = jnp.max(all_scores, axis=1).reshape(shards, persons // shards)

    def halve(best, mask):
        half = best.shape[0] // 2
        pairs = [(i, i ^ mask) for i in range(shards)]
        return jnp.maximum(best[:half], lax.ppermute(best[half:], "shard", pairs))

    def over_x(best, flip):
        return jnp.maximum(best, lax.ppermute(best, "tp", [(i, i ^ flip) for i in range(4)]))

    for mask in masks[:2:-1]:
        best = halve(best, mask)

    query = lax.dynamic_slice_in_dim(jnp.where(home, person_embedding, users[shards // 2]), parity, 1, 0)
    query = jnp.where(core == 0, query, jnp.zeros_like(query))
    zero = jnp.zeros_like(query)
    query = jnp.where(
        parity == 1, jnp.concatenate([query, zero], 1), jnp.concatenate([zero, query], 1)
    )
    query = jnp.broadcast_to(query, (16, 512))

    surv = pair_attributes.shape[1]
    tall, wide, lanes = ((surv, 512), BF), ((surv, 768), BF), ((16, surv), F32)
    v_pair = [pltpu.VMEM((768, 512), BF)] * 2
    u_pair = [pltpu.VMEM((512, 768), BF)] * 2
    head = ((256, 512), BF)
    part, head_a, head_b = in_vmem(
        context_kernel, "context_part", [((surv, 512), F32), head, head], v_pair, CTX, 8, [flags],
        [ctx_a, ctx_b, *vs],
    )
    recv, best = lax.optimization_barrier((recv, best))
    step = over_x(best, 1)
    pay, piece, logit = in_vmem(
        first_kernel, "first_layer", [tall, tall, lanes],
        [pltpu.VMEM(recv.shape, BF), pltpu.VMEM((16, recv.shape[0]), F32)],
        FIRST, 8, [], [recv, part, query, head_a, head_b],
    )
    piece, best = lax.optimization_barrier((piece, step))
    other, best = lax.optimization_barrier((move(piece, perm=to_core), over_x(best, 2)))
    step = halve(best, masks[2])
    x_a, x_b, piece1 = in_vmem(
        second_kernel, "second_layer", [wide, wide, tall], u_pair + v_pair, 3584, 12, [flags],
        [piece, other, pay, ctx_a, ctx_b, small_a, small_b, *us, *vs],
    )
    piece1, best = lax.optimization_barrier((piece1, step))
    other1, best = lax.optimization_barrier((move(piece1, perm=to_core), halve(best, masks[1])))
    step = halve(best, masks[0])
    (score,) = in_vmem(
        last_kernel, "last_layer", [lanes], u_pair, 1792, 10, [flags, similarity_coefficient],
        [piece1, other1, pay, ctx_a, ctx_b, x_a, x_b, small_a, small_b, logit, *us],
    )
    score, best = lax.optimization_barrier((score, step))
    top = jnp.where(home, lax.dynamic_slice_in_dim(best, parity, 1, 1), 0.0)
    score = score[0:1] - similarity_coefficient[0] * top
    score = score + move(score, perm=to_core)
    score_a = move(score, perm=to_near)
    score_b = jnp.where(home, score, move(score, perm=ctx_far))
    return jnp.where(
        parity == 1,
        jnp.concatenate([score_a, score_b], 0),
        jnp.concatenate([score_b, score_a], 0),
    )


def solution(mesh):
    return jax.shard_map(
        on_device,
        mesh=mesh,
        in_specs=(
            P("shard", None),
            P(("shard", "tp"), None),
            P(("shard", "tp"), None),
            P(None, ("shard", "tp"), None),
            P(None, ("shard", "tp")),
            P("shard", None, "tp"),
            P(None, "tp", None),
            P(None, None, "tp"),
            P(None, "tp"),
            P("tp"),
            P(),
        ),
        out_specs=P("shard", None),
        check_vma=False,
    )
```

```python
import functools

import jax
import jax.numpy as jnp
from jax import lax
from jax.experimental import pallas as pl
from jax.experimental.pallas import tpu as pltpu
from jax.sharding import PartitionSpec as P

BF = jnp.bfloat16
F32 = jnp.float32
AXES = ("shard", "tp")
VMEM = pl.BlockSpec(memory_space=pltpu.VMEM)
PICK, CTX, FIRST = 4096, 20000, 15000
SMEM = pl.BlockSpec(memory_space=pltpu.SMEM)
ANY = pl.BlockSpec(memory_space=pl.ANY)


def grant(kbytes):
    return pltpu.CompilerParams(vmem_limit_bytes=kbytes * 1000)


def group_perm(groups, step, member=lambda x, c: True, turn=lambda x, c: 0):
    pairs = []
    for g in range(groups):
        for c in range(2):
            for x in range(4):
                if member(x, c):
                    x2, c2 = step(x, c)
                    g2 = g // 4 * 4 + (g + turn(x, c)) % 4
                    pairs.append((g * 8 + c * 4 + x, g2 * 8 + c2 * 4 + x2))
    return pairs


def is_home(x, c):
    return x // 2 == c


def is_away(x, c):
    return x // 2 != c


def near(x, c):
    return (x ^ 1, x // 2) if is_home(x, c) else (x ^ 3, x // 2)


def partners(shards):
    far_z = (6, 7, 4, 5, 2, 3, 0, 1)
    steps = []
    for of_z, of_y, of_core in (
        (lambda z: z ^ 1, None, None),
        (lambda z: z ^ 2, None, None),
        (lambda z: far_z[z], None, None),
        (None, 1, None),
        (None, 3, None),
        (None, None, 1),
    ):
        pairs = []
        for i in range(shards):
            z, y, c = i // 8, i // 2 % 4, i % 2
            z = of_z(z) if of_z else z
            y = y ^ of_y if of_y else y
            c = c ^ of_core if of_core else c
            pairs.append((i, z * 8 + y * 2 + c))
        steps.append(pairs)
    return steps


def dot(a, b):
    return jnp.dot(a, b, preferred_element_type=F32)


def dot_nt(a, b):
    return lax.dot_general(a, b, (((1,), (1,)), ((), ())), preferred_element_type=F32)


def call(kernel, name, kbytes, outs, scratch, mflops, mbytes, scalars, arrays, far, out_specs=None):
    return pl.pallas_call(
        kernel,
        in_specs=[SMEM] * len(scalars) + [VMEM] * len(arrays) + [ANY] * len(far),
        out_specs=out_specs or [VMEM] * len(outs),
        out_shape=[jax.ShapeDtypeStruct(shape, dtype) for shape, dtype in outs],
        scratch_shapes=scratch,
        compiler_params=grant(kbytes),
        cost_estimate=pl.CostEstimate(
            flops=mflops << 20, bytes_accessed=mbytes << 20, transcendentals=0
        ),
        name=name,
    )(*scalars, *arrays, *far)


def pick_kernel(kept_ref, count_ref, emb_ref, attr_ref, out_ref):
    slots, persons = kept_ref.shape
    items = emb_ref.shape[0]
    n = out_ref.shape[0] * 32
    at = pl.program_id(0) * n
    live = lax.broadcasted_iota(jnp.int32, (slots, persons), 0) < count_ref[...]
    wanted = jnp.where(live, kept_ref[...], 4095)
    digits = jnp.concatenate([wanted >> 6, wanted & 63], 0).astype(F32).astype(BF)
    row = lax.broadcasted_iota(jnp.int32, (n, persons), 0) + at
    owner = (row // slots == lax.broadcasted_iota(jnp.int32, (n, persons), 1)).astype(BF)
    both = dot_nt(owner, digits)
    lane = lax.broadcasted_iota(jnp.int32, (n, 2 * slots), 1)
    slot = lax.broadcasted_iota(jnp.int32, (n, 2 * slots), 0) % slots
    high = jnp.where(lane == slot, both * 64.0, 0.0)
    low = jnp.where(lane == slot + slots, both, 0.0)
    rows = jnp.sum(high + low, axis=1, keepdims=True).astype(jnp.int32)
    hot = (lax.broadcasted_iota(jnp.int32, (n, items), 1) == rows).astype(BF)
    unused = rows >= items
    odd = (lax.broadcasted_iota(jnp.int32, (n, 1), 0) // slots) % 2 == 1
    for c in range(2):
        tables = (
            (emb_ref[...], attr_ref[:, 0:256])
            if c == 0
            else (attr_ref[:, 256:512], attr_ref[:, 512:768])
        )
        low, high = (jnp.where(unused, jnp.inf, dot(hot, t)) for t in tables)
        first = jnp.where(odd, low, high).astype(BF)
        second = jnp.where(odd, high, low).astype(BF)
        for g in range(n // 32):
            out_ref[g, c, :, 0:256] = first[g * 32 : (g + 1) * 32]
            out_ref[g, c, :, 256:512] = second[g * 32 : (g + 1) * 32]


def pick_rows(kept, count, emb, attr):
    slots, persons = kept.shape
    steps = 4
    return pl.pallas_call(
        pick_kernel,
        grid=(steps,),
        in_specs=[VMEM] * 4,
        out_specs=pl.BlockSpec((persons // 4 // steps, 2, 4 * slots, 512), lambda i: (i, 0, 0, 0)),
        out_shape=jax.ShapeDtypeStruct((persons // 4, 2, 4 * slots, 512), BF),
        compiler_params=grant(58500),
        cost_estimate=pl.CostEstimate(
            flops=PICK << 20, bytes_accessed=6 << 20, transcendentals=0
        ),
        name="pick_rows",
    )(kept, count, emb, attr)


def fetch(flags, layer, sources, dst_a, dst_b, sems):
    own, near_x, far_x, near_y, far_y = sources
    home = flags[0] == 1
    by_x = flags[1] == layer
    pairs = (
        (by_x, near_x, dst_a, 0),
        (jnp.logical_not(by_x), near_y, dst_a, 0),
        (home, own.at[layer], dst_b, 1),
        (jnp.logical_and(jnp.logical_not(home), by_x), far_x, dst_b, 1),
        (jnp.logical_not(jnp.logical_or(home, by_x)), far_y, dst_b, 1),
    )
    for when, src, dst, i in pairs:

        @pl.when(when)
        def _(src=src, dst=dst, i=i):
            pltpu.make_async_copy(src, dst, sems.at[i]).start()


def fetched(sources, dst_a, dst_b, sems):
    pltpu.make_async_copy(sources[1], dst_a, sems.at[0]).wait()
    pltpu.make_async_copy(sources[1], dst_b, sems.at[1]).wait()


ROWS = 256


def block_copies(src, dst, sems):
    copies = []
    for i in range(dst.shape[0] // ROWS):
        here = pl.ds(i * ROWS, ROWS)
        copies.append(pltpu.make_async_copy(src.at[here], dst.at[here], sems.at[i]))
        copies[-1].start()
    return copies


def context_kernel(
    flags, ca_hbm, cb_hbm, v0, v1, v2, v3, v4, part_hbm, pa_hbm, pb_hbm,
    ca_ref, cb_ref, va_ref, vb_ref, part_ref, v_sems, a_sems, b_sems, out_sems, head_sems,
):
    vs = (v0, v1, v2, v3, v4)
    fetch(flags, 0, vs, va_ref, vb_ref, v_sems)
    a_copies = block_copies(ca_hbm, ca_ref, a_sems)
    b_copies = block_copies(cb_hbm, cb_ref, b_sems)
    fetched(vs, va_ref, vb_ref, v_sems)
    outs = [
        pltpu.make_async_copy(va_ref.at[0:256], pa_hbm, head_sems.at[0]),
        pltpu.make_async_copy(vb_ref.at[0:256], pb_hbm, head_sems.at[1]),
    ]
    for copy in outs:
        copy.start()
    for i in range(part_ref.shape[0] // ROWS):
        here = pl.ds(i * ROWS, ROWS)
        a_copies[i].wait()
        b_copies[i].wait()
        part_ref[here] = dot(ca_ref[here], va_ref[256:768]) + dot(cb_ref[here], vb_ref[256:768])
        outs.append(pltpu.make_async_copy(part_ref.at[here], part_hbm.at[here], out_sems.at[i]))
        outs[-1].start()
    for copy in outs:
        copy.wait()


def first_kernel(
    u_ref, recv_hbm, part_hbm, pa_hbm, pb_hbm, pay_ref, piece_ref, logit_ref,
    clean, place, recv_ref, part_ref, pa_ref, pb_ref, recv_sems, part_sems, head_sems,
):
    slots = recv_ref.shape[0]
    recv_copies = block_copies(recv_hbm, recv_ref, recv_sems)
    heads = [
        pltpu.make_async_copy(pa_hbm, pa_ref, head_sems.at[0]),
        pltpu.make_async_copy(pb_hbm, pb_ref, head_sems.at[1]),
    ]
    for copy in heads:
        copy.start()
    part_copies = block_copies(part_hbm, part_ref, part_sems)
    r = lax.broadcasted_iota(jnp.int32, (ROWS, ROWS), 0)
    q = lax.broadcasted_iota(jnp.int32, (ROWS, ROWS), 1)
    upper = (r <= q).astype(BF)
    lane0 = (lax.broadcasted_iota(jnp.int32, (16, 128), 1) == 0).astype(BF)
    before = jnp.zeros((16, 1), F32)
    for i in range(slots // ROWS):
        here = slice(i * ROWS, (i + 1) * ROWS)
        recv_copies[i].wait()
        got = recv_ref[here].astype(F32)
        live = got < jnp.inf
        clean[here] = jnp.where(live, got, 0.0).astype(BF)
        marks = dot_nt(lane0, live[:, 0:128].astype(F32).astype(BF))
        upto = dot(marks.astype(BF), upper) + before
        place[:, here] = jnp.where(marks > 0.5, upto - 1.0, -1.0)
        before = upto[:, ROWS - 1 : ROWS]
    for copy in heads:
        copy.wait()
    for i in range(pay_ref.shape[0] // ROWS):
        here = pl.ds(i * ROWS, ROWS)
        k = (lax.broadcasted_iota(jnp.int32, (ROWS, slots), 0) + i * ROWS).astype(F32)
        hot = (k == place[0:1, :]).astype(BF)
        pay = dot(hot, clean[...]).astype(BF)
        pay_ref[here] = pay
        part_copies[i].wait()
        piece = part_ref[here] + dot(pay[:, 0:256], pa_ref[...]) + dot(pay[:, 256:512], pb_ref[...])
        piece_ref[here] = piece.astype(BF)
        logit_ref[:, here] = dot_nt(u_ref[...], pay)


def cross(x0, hidden, offset, x):
    x0 = x0.astype(F32)
    return (x0 * (hidden + offset) + x.astype(F32)).astype(BF)


def second_kernel(
    flags, mine_ref, other_ref, pay_ref, ba_ref, bb_ref, ca_hbm, cb_hbm,
    u0, u1, u2, u3, u4, v0, v1, v2, v3, v4, xa_ref, xb_ref, piece_ref,
    ua_ref, ub_ref, va_ref, vb_ref, ca_ref, cb_ref, u_sems, v_sems, a_sems, b_sems,
):
    us, vs = (u0, u1, u2, u3, u4), (v0, v1, v2, v3, v4)
    fetch(flags, 0, us, ua_ref, ub_ref, u_sems)
    a_copies = block_copies(ca_hbm, ca_ref, a_sems)
    b_copies = block_copies(cb_hbm, cb_ref, b_sems)
    fetch(flags, 1, vs, va_ref, vb_ref, v_sems)
    fetched(us, ua_ref, ub_ref, u_sems)
    for i in range(pay_ref.shape[0] // ROWS):
        here = pl.ds(i * ROWS, ROWS)
        proj = (mine_ref[here].astype(F32) + other_ref[here].astype(F32)).astype(BF)
        a_copies[i].wait()
        b_copies[i].wait()
        slots = (
            (xa_ref, ua_ref, ba_ref, ca_ref, 0),
            (xb_ref, ub_ref, bb_ref, cb_ref, 256),
        )
        for x_ref, u_ref, b_ref, c_ref, at in slots:
            hidden = dot(proj, u_ref[...])
            pay = pay_ref[here, at : at + 256]
            ctx = c_ref[here]
            x_ref[here, 0:256] = cross(pay, hidden[:, 0:256], b_ref[0:1, 0:256], pay)
            x_ref[here, 256:768] = cross(ctx, hidden[:, 256:768], b_ref[0:1, 256:768], ctx)
        if i == 0:
            fetched(vs, va_ref, vb_ref, v_sems)
        piece = dot(xa_ref[here], va_ref[...]) + dot(xb_ref[here], vb_ref[...])
        piece_ref[here] = piece.astype(BF)


def last_kernel(
    flags, coefficient, mine_ref, other_ref, pay_ref, xa_ref, xb_ref, sa_ref, sb_ref, logit_ref,
    ca_hbm, cb_hbm, u0, u1, u2, u3, u4, score_ref,
    ua_ref, ub_ref, ca_ref, cb_ref, u_sems, a_sems, b_sems,
):
    us = (u0, u1, u2, u3, u4)
    fetch(flags, 1, us, ua_ref, ub_ref, u_sems)
    a_copies = block_copies(ca_hbm, ca_ref, a_sems)
    b_copies = block_copies(cb_hbm, cb_ref, b_sems)
    fetched(us, ua_ref, ub_ref, u_sems)
    for i in range(pay_ref.shape[0] // ROWS):
        here = pl.ds(i * ROWS, ROWS)
        proj = (mine_ref[here].astype(F32) + other_ref[here].astype(F32)).astype(BF)
        score = coefficient[0] * logit_ref[:, here]
        a_copies[i].wait()
        b_copies[i].wait()
        for x_ref, u_ref, s_ref, c_ref, at in (
            (xa_ref, ua_ref, sa_ref, ca_ref, 0),
            (xb_ref, ub_ref, sb_ref, cb_ref, 256),
        ):
            hidden = dot(proj, u_ref[...])
            low = cross(
                pay_ref[here, at : at + 256], hidden[:, 0:256], s_ref[1:2, 0:256], x_ref[here, 0:256]
            )
            high = cross(
                c_ref[here], hidden[:, 256:768], s_ref[1:2, 256:768], x_ref[here, 256:768]
            )
            out = jnp.broadcast_to(s_ref[2:3, :], (16, 768)).astype(BF)
            score = score + dot_nt(out[:, 0:256], low) + dot_nt(out[:, 256:768], high)
        score_ref[:, here] = score


def on_device(
    person_embedding,
    catalog_embedding,
    catalog_attributes,
    kept_part_entries,
    valid_slot_number,
    pair_attributes,
    lowrank_v_matrix,
    lowrank_u_matrix,
    interaction_offset,
    final_projection,
    similarity_coefficient,
):
    shards = lax.axis_size("shard")
    groups = shards // 2
    x = lax.axis_index("tp")
    core = lax.axis_index("shard") % 2
    home = x // 2 == core
    parity = x % 2
    move = functools.partial(lax.ppermute, axis_name=AXES)
    to_core = group_perm(groups, lambda x, c: (x, 1 - c))
    to_near = group_perm(groups, near)
    home_on = group_perm(groups, lambda x, c: (x ^ 3, c), is_home)
    away_swap = group_perm(groups, lambda x, c: (x ^ 1, c), is_away)
    ctx_near = group_perm(groups, lambda x, c: (x ^ 1, c) if is_home(x, c) else (x ^ 3, 1 - c))
    ctx_far = group_perm(groups, lambda x, c: (x ^ 2, 1 - c), is_away)
    stay = lambda x, c: (x, c)
    y_up = group_perm(groups, stay, turn=lambda x, c: 1)
    y_mixed = group_perm(groups, stay, turn=lambda x, c: -1 if is_home(x, c) else 1)
    y_down = group_perm(groups, stay, is_away, lambda x, c: -1)
    by = lax.axis_index("shard") // 2 % 2
    flags = jnp.stack([home.astype(jnp.int32), by])

    persons, _, kept = kept_part_entries.shape
    hops = partners(shards)
    users = person_embedding[None]

    def double(users, pairs):
        return jnp.concatenate([users, lax.ppermute(users, "shard", pairs)], 0)

    for pairs in hops[:3]:
        users = double(users, pairs)
    v_mine = lax.dynamic_index_in_dim(lowrank_v_matrix, by, 0, False)
    u_mine = lax.dynamic_index_in_dim(lowrank_u_matrix, by, 0, False)
    v_near = move(v_mine, perm=to_near)
    u_near = move(u_mine, perm=to_near)
    ctx_a = move(lax.dynamic_index_in_dim(pair_attributes, 1 - parity, 0, False), perm=ctx_near)
    ctx_own = lax.dynamic_index_in_dim(pair_attributes, parity, 0, False)
    parcel = pick_rows(
        kept_part_entries[:, 0, :].T, valid_slot_number.T, catalog_embedding, catalog_attributes
    )

    parcel = parcel.reshape(persons * 2, kept, 512)
    parcel, v_near, ctx_a, users = lax.optimization_barrier((parcel, v_near, ctx_a, users))
    recv = lax.all_to_all(parcel, AXES, split_axis=0, concat_axis=0, tiled=True)
    recv = recv.reshape(persons * 2 * kept, 512)

    small = jnp.concatenate([interaction_offset, final_projection[None, :].astype(F32)], 0)
    small, v_near = lax.optimization_barrier((small, v_near))
    small_a = move(small, perm=to_near)
    small_b = move(small, perm=ctx_far)
    v_far = move(v_near, perm=home_on)
    u_far = move(u_near, perm=away_swap)
    v_near_y = move(v_near, perm=y_up)
    u_near_y = move(u_near, perm=y_mixed)

    ctx_own, small_a, small_b = lax.optimization_barrier((ctx_own, small_a, small_b))
    ctx_b = jnp.where(home, ctx_own, move(ctx_own, perm=ctx_far))
    small_b = jnp.where(home, small, small_b)
    v_far, users = lax.optimization_barrier((v_far, users))
    v_far_y = move(v_far, perm=y_down)
    u_far_y = move(u_far, perm=y_down)
    ctx_a, u_far, u_near_y, u_far_y = lax.optimization_barrier((ctx_a, u_far, u_near_y, u_far_y))
    vs = (lowrank_v_matrix, v_near, v_far, v_near_y, v_far_y)
    us = (lowrank_u_matrix, u_near, u_far, u_near_y, u_far_y)

    for pairs in hops[3:]:
        users = double(users, pairs)
    all_scores = jnp.einsum(
        "ue,ie->ui", users.reshape(persons, -1), catalog_embedding, preferred_element_type=F32
    )
    best = jnp.max(all_scores, axis=1).reshape(shards, persons // shards)

    def halve(best, pairs):
        half = best.shape[0] // 2
        return jnp.maximum(best[:half], lax.ppermute(best[half:], "shard", pairs))

    def over_x(best, flip):
        return jnp.maximum(best, lax.ppermute(best, "tp", [(i, i ^ flip) for i in range(4)]))

    for pairs in hops[:2:-1]:
        best = halve(best, pairs)

    query = lax.dynamic_slice_in_dim(jnp.where(home, person_embedding, users[shards // 2]), parity, 1, 0)
    query = jnp.where(core == 0, query, jnp.zeros_like(query))
    zero = jnp.zeros_like(query)
    query = jnp.where(
        parity == 1, jnp.concatenate([query, zero], 1), jnp.concatenate([zero, query], 1)
    )
    query = jnp.broadcast_to(query, (16, 512))

    surv = pair_attributes.shape[1]
    blocks = surv // ROWS
    tall, wide, lanes = ((surv, 512), BF), ((surv, 768), BF), ((16, surv), F32)
    part_like, head = ((surv, 512), F32), ((256, 512), BF)
    v_pair = [pltpu.VMEM((768, 512), BF)] * 2
    u_pair = [pltpu.VMEM((512, 768), BF)] * 2
    ctx_pair = [pltpu.VMEM((surv, 512), BF)] * 2

    def sems(*counts):
        return [pltpu.SemaphoreType.DMA((n,)) for n in counts]

    part, head_a, head_b = call(
        context_kernel, "context_part", 62500, [part_like, head, head],
        ctx_pair + v_pair + [pltpu.VMEM(*part_like)] + sems(2, blocks, blocks, blocks, 2),
        CTX, 8, [flags], [], [ctx_a, ctx_b, *vs], [ANY] * 3,
    )
    recv, best = lax.optimization_barrier((recv, best))
    step = over_x(best, 1)
    pay, piece, logit = call(
        first_kernel, "first_layer", 61000, [tall, tall, lanes],
        [pltpu.VMEM(recv.shape, BF), pltpu.VMEM((16, recv.shape[0]), F32)]
        + [pltpu.VMEM(recv.shape, BF), pltpu.VMEM(*part_like)]
        + [pltpu.VMEM(*head)] * 2
        + sems(recv.shape[0] // ROWS, blocks, 2),
        FIRST, 8, [], [query], [recv, part, head_a, head_b],
    )
    piece, best = lax.optimization_barrier((piece, step))
    other, best = lax.optimization_barrier((move(piece, perm=to_core), over_x(best, 3)))
    step = halve(best, hops[2])
    x_a, x_b, piece1 = call(
        second_kernel, "second_layer", 55500, [wide, wide, tall],
        u_pair + v_pair + ctx_pair + sems(2, 2, blocks, blocks),
        3584, 12, [flags], [piece, other, pay, small_a, small_b], [ctx_a, ctx_b, *us, *vs],
    )
    piece1, best = lax.optimization_barrier((piece1, step))
    other1, best = lax.optimization_barrier((move(piece1, perm=to_core), halve(best, hops[1])))
    step = halve(best, hops[0])
    (score,) = call(
        last_kernel, "last_layer", 56500, [lanes], u_pair + ctx_pair + sems(2, blocks, blocks),
        1792, 10, [flags, similarity_coefficient],
        [piece1, other1, pay, x_a, x_b, small_a, small_b, logit], [ctx_a, ctx_b, *us],
    )
    score, best = lax.optimization_barrier((score, step))
    top = jnp.where(home, lax.dynamic_slice_in_dim(best, parity, 1, 1), 0.0)
    score = score[0:1] - similarity_coefficient[0] * top
    score = score + move(score, perm=to_core)
    score_a = move(score, perm=to_near)
    score_b = jnp.where(home, score, move(score, perm=ctx_far))
    return jnp.where(
        parity == 1,
        jnp.concatenate([score_a, score_b], 0),
        jnp.concatenate([score_b, score_a], 0),
    )


def solution(mesh):
    return jax.shard_map(
        on_device,
        mesh=mesh,
        in_specs=(
            P("shard", None),
            P(("shard", "tp"), None),
            P(("shard", "tp"), None),
            P(None, ("shard", "tp"), None),
            P(None, ("shard", "tp")),
            P("shard", None, "tp"),
            P(None, "tp", None),
            P(None, None, "tp"),
            P(None, "tp"),
            P("tp"),
            P(),
        ),
        out_specs=P("shard", None),
        check_vma=False,
    )
```

```python
import functools

import jax
import jax.numpy as jnp
from jax import lax
from jax.experimental import pallas as pl
from jax.experimental.pallas import tpu as pltpu
from jax.sharding import PartitionSpec as P

BF = jnp.bfloat16
F32 = jnp.float32
AXES = ("shard", "tp")
VMEM = pl.BlockSpec(memory_space=pltpu.VMEM)
PICK, CTX, FIRST, SECOND = 4096, 20000, 15000, 15000
SMEM = pl.BlockSpec(memory_space=pltpu.SMEM)
ANY = pl.BlockSpec(memory_space=pl.ANY)


def grant(kbytes):
    return pltpu.CompilerParams(vmem_limit_bytes=kbytes * 1000)


def group_perm(groups, step, member=lambda x, c: True, turn=lambda x, c: 0):
    pairs = []
    for g in range(groups):
        for c in range(2):
            for x in range(4):
                if member(x, c):
                    x2, c2 = step(x, c)
                    g2 = g // 4 * 4 + (g + turn(x, c)) % 4
                    pairs.append((g * 8 + c * 4 + x, g2 * 8 + c2 * 4 + x2))
    return pairs


def is_home(x, c):
    return x // 2 == c


def is_away(x, c):
    return x // 2 != c


def near(x, c):
    return (x ^ 1, x // 2) if is_home(x, c) else (x ^ 3, x // 2)


def partners(shards):
    far_z = (6, 7, 4, 5, 2, 3, 0, 1)
    steps = []
    for of_z, of_y, of_core in (
        (lambda z: z ^ 1, None, None),
        (lambda z: z ^ 2, None, None),
        (lambda z: far_z[z], None, None),
        (None, 1, None),
        (None, 3, None),
        (None, None, 1),
    ):
        pairs = []
        for i in range(shards):
            z, y, c = i // 8, i // 2 % 4, i % 2
            z = of_z(z) if of_z else z
            y = y ^ of_y if of_y else y
            c = c ^ of_core if of_core else c
            pairs.append((i, z * 8 + y * 2 + c))
        steps.append(pairs)
    return steps


def dot(a, b):
    return jnp.dot(a, b, preferred_element_type=F32)


def dot_nt(a, b):
    return lax.dot_general(a, b, (((1,), (1,)), ((), ())), preferred_element_type=F32)


def call(kernel, name, kbytes, outs, scratch, mflops, mbytes, scalars, arrays, far, out_specs=None):
    return pl.pallas_call(
        kernel,
        in_specs=[SMEM] * len(scalars) + [VMEM] * len(arrays) + [ANY] * len(far),
        out_specs=out_specs or [VMEM] * len(outs),
        out_shape=[jax.ShapeDtypeStruct(shape, dtype) for shape, dtype in outs],
        scratch_shapes=scratch,
        compiler_params=grant(kbytes),
        cost_estimate=pl.CostEstimate(
            flops=mflops << 20, bytes_accessed=mbytes << 20, transcendentals=0
        ),
        name=name,
    )(*scalars, *arrays, *far)


def pick_kernel(
    kept_ref, count_ref, emb_hbm, attr_hbm, out_hbm, table, hot_ref, out_ref, in_sems, out_sems
):
    slots, persons = kept_ref.shape
    items = table.shape[1]
    loads = [pltpu.make_async_copy(emb_hbm, table.at[0], in_sems.at[0])]
    for q in range(3):
        columns = attr_hbm.at[:, pl.ds(q * 256, 256)]
        loads.append(pltpu.make_async_copy(columns, table.at[q + 1], in_sems.at[q + 1]))
    for load in loads:
        load.start()
    live = lax.broadcasted_iota(jnp.int32, (slots, persons), 0) < count_ref[...]
    wanted = jnp.where(live, kept_ref[...], 4095)
    digits = jnp.concatenate([wanted >> 6, wanted & 63], 0).astype(F32).astype(BF)
    n = 256
    blocks = persons * slots // n
    lane = lax.broadcasted_iota(jnp.int32, (n, 2 * slots), 1)
    slot = lax.broadcasted_iota(jnp.int32, (n, 2 * slots), 0) % slots
    odd = (lax.broadcasted_iota(jnp.int32, (n, 1), 0) // slots) % 2 == 1
    unused = []
    for b in range(blocks):
        row = lax.broadcasted_iota(jnp.int32, (n, persons), 0) + b * n
        owner = (row // slots == lax.broadcasted_iota(jnp.int32, (n, persons), 1)).astype(BF)
        both = dot_nt(owner, digits)
        high = jnp.where(lane == slot, both * 64.0, 0.0)
        low = jnp.where(lane == slot + slots, both, 0.0)
        rows = jnp.sum(high + low, axis=1, keepdims=True).astype(jnp.int32)
        hot = lax.broadcasted_iota(jnp.int32, (n, items), 1) == rows
        hot_ref[b * n : (b + 1) * n] = hot.astype(BF)
        unused.append(rows >= items)
    stores = []
    for c in range(2):
        loads[2 * c].wait()
        loads[2 * c + 1].wait()
        for b in range(blocks):
            hot = hot_ref[b * n : (b + 1) * n]
            low = jnp.where(unused[b], jnp.inf, dot(hot, table[2 * c]))
            high = jnp.where(unused[b], jnp.inf, dot(hot, table[2 * c + 1]))
            first = jnp.where(odd, low, high).astype(BF)
            second = jnp.where(odd, high, low).astype(BF)
            for g in range(n // 32):
                out_ref[c, b * (n // 32) + g, :, 0:256] = first[g * 32 : (g + 1) * 32]
                out_ref[c, b * (n // 32) + g, :, 256:512] = second[g * 32 : (g + 1) * 32]
        stores.append(pltpu.make_async_copy(out_ref.at[c], out_hbm.at[:, c], out_sems.at[c]))
        stores[-1].start()
    for store in stores:
        store.wait()


def pick_rows(kept, count, emb, attr):
    slots, persons = kept.shape
    out = (persons // 4, 2, 4 * slots, 512)
    return pl.pallas_call(
        pick_kernel,
        in_specs=[VMEM, VMEM, ANY, ANY],
        out_specs=ANY,
        out_shape=jax.ShapeDtypeStruct(out, BF),
        scratch_shapes=[
            pltpu.VMEM((4, emb.shape[0], 256), BF),
            pltpu.VMEM((persons * slots, emb.shape[0]), BF),
            pltpu.VMEM((2, persons // 4, 4 * slots, 512), BF),
            pltpu.SemaphoreType.DMA((4,)),
            pltpu.SemaphoreType.DMA((2,)),
        ],
        compiler_params=grant(62500),
        cost_estimate=pl.CostEstimate(
            flops=PICK << 20, bytes_accessed=6 << 20, transcendentals=0
        ),
        name="pick_rows",
    )(kept, count, emb, attr)


ROWS = 256


def block_copies(src, dst, sems):
    copies = []
    for i in range(dst.shape[0] // ROWS):
        here = pl.ds(i * ROWS, ROWS)
        copies.append(pltpu.make_async_copy(src.at[here], dst.at[here], sems.at[i]))
        copies[-1].start()
    return copies


def context_kernel(ca_ref, cb_ref, va_ref, vb_ref, part_ref, head_ref):
    head_ref[0:256] = va_ref[0:256]
    head_ref[256:512] = vb_ref[0:256]
    for i in range(part_ref.shape[0] // ROWS):
        here = pl.ds(i * ROWS, ROWS)
        part_ref[here] = dot(ca_ref[here], va_ref[256:768]) + dot(cb_ref[here], vb_ref[256:768])


def first_kernel(
    u_ref, part_ref, head_ref, recv_hbm, pay_ref, piece_ref, logit_ref,
    clean, place, recv_ref, recv_sems,
):
    slots = recv_ref.shape[0]
    recv_copies = block_copies(recv_hbm, recv_ref, recv_sems)
    r = lax.broadcasted_iota(jnp.int32, (ROWS, ROWS), 0)
    q = lax.broadcasted_iota(jnp.int32, (ROWS, ROWS), 1)
    upper = (r <= q).astype(BF)
    lane0 = (lax.broadcasted_iota(jnp.int32, (16, 128), 1) == 0).astype(BF)
    before = jnp.zeros((16, 1), F32)
    for i in range(slots // ROWS):
        here = slice(i * ROWS, (i + 1) * ROWS)
        recv_copies[i].wait()
        got = recv_ref[here].astype(F32)
        live = got < jnp.inf
        clean[here] = jnp.where(live, got, 0.0).astype(BF)
        marks = dot_nt(lane0, live[:, 0:128].astype(F32).astype(BF))
        upto = dot(marks.astype(BF), upper) + before
        place[:, here] = jnp.where(marks > 0.5, upto - 1.0, -1.0)
        before = upto[:, ROWS - 1 : ROWS]
    for i in range(pay_ref.shape[0] // ROWS):
        here = pl.ds(i * ROWS, ROWS)
        k = (lax.broadcasted_iota(jnp.int32, (ROWS, slots), 0) + i * ROWS).astype(F32)
        hot = (k == place[0:1, :]).astype(BF)
        pay = dot(hot, clean[...]).astype(BF)
        pay_ref[here] = pay
        piece = part_ref[here] + dot(pay, head_ref[...])
        piece_ref[here] = piece.astype(BF)
        logit_ref[:, here] = dot_nt(u_ref[...], pay)


def cross(x0, hidden, offset, x):
    x0 = x0.astype(F32)
    return (x0 * (hidden + offset) + x.astype(F32)).astype(BF)


def second_kernel(
    mine_ref, other_ref, pay_ref, ba_ref, bb_ref, ca_ref, cb_ref,
    ua_ref, ub_ref, va_ref, vb_ref, xa_ref, xb_ref, piece_ref,
):
    for i in range(pay_ref.shape[0] // ROWS):
        here = pl.ds(i * ROWS, ROWS)
        proj = (mine_ref[here].astype(F32) + other_ref[here].astype(F32)).astype(BF)
        slots = (
            (xa_ref, ua_ref, ba_ref, ca_ref, 0),
            (xb_ref, ub_ref, bb_ref, cb_ref, 256),
        )
        for x_ref, u_ref, b_ref, c_ref, at in slots:
            hidden = dot(proj, u_ref[...])
            pay = pay_ref[here, at : at + 256]
            ctx = c_ref[here]
            x_ref[here, 0:256] = cross(pay, hidden[:, 0:256], b_ref[0:1, 0:256], pay)
            x_ref[here, 256:768] = cross(ctx, hidden[:, 256:768], b_ref[0:1, 256:768], ctx)
        piece = dot(xa_ref[here], va_ref[...]) + dot(xb_ref[here], vb_ref[...])
        piece_ref[here] = piece.astype(BF)


def last_kernel(
    coefficient, mine_ref, other_ref, pay_ref, xa_ref, xb_ref, sa_ref, sb_ref, logit_ref,
    ca_ref, cb_ref, ua_ref, ub_ref, score_ref,
):
    for i in range(pay_ref.shape[0] // ROWS):
        here = pl.ds(i * ROWS, ROWS)
        proj = (mine_ref[here].astype(F32) + other_ref[here].astype(F32)).astype(BF)
        score = coefficient[0] * logit_ref[:, here]
        for x_ref, u_ref, s_ref, c_ref, at in (
            (xa_ref, ua_ref, sa_ref, ca_ref, 0),
            (xb_ref, ub_ref, sb_ref, cb_ref, 256),
        ):
            hidden = dot(proj, u_ref[...])
            low = cross(
                pay_ref[here, at : at + 256], hidden[:, 0:256], s_ref[1:2, 0:256], x_ref[here, 0:256]
            )
            high = cross(
                c_ref[here], hidden[:, 256:768], s_ref[1:2, 256:768], x_ref[here, 256:768]
            )
            out = jnp.broadcast_to(s_ref[2:3, :], (16, 768)).astype(BF)
            score = score + dot_nt(out[:, 0:256], low) + dot_nt(out[:, 256:768], high)
        score_ref[:, here] = score


def on_device(
    person_embedding,
    catalog_embedding,
    catalog_attributes,
    kept_part_entries,
    valid_slot_number,
    pair_attributes,
    lowrank_v_matrix,
    lowrank_u_matrix,
    interaction_offset,
    final_projection,
    similarity_coefficient,
):
    shards = lax.axis_size("shard")
    groups = shards // 2
    x = lax.axis_index("tp")
    core = lax.axis_index("shard") % 2
    home = x // 2 == core
    parity = x % 2
    move = functools.partial(lax.ppermute, axis_name=AXES)
    to_core = group_perm(groups, lambda x, c: (x, 1 - c))
    to_near = group_perm(groups, near)
    home_on = group_perm(groups, lambda x, c: (x ^ 3, c), is_home)
    away_swap = group_perm(groups, lambda x, c: (x ^ 1, c), is_away)
    ctx_near = group_perm(groups, lambda x, c: (x ^ 1, c) if is_home(x, c) else (x ^ 3, 1 - c))
    ctx_far = group_perm(groups, lambda x, c: (x ^ 2, 1 - c), is_away)
    persons, _, kept = kept_part_entries.shape
    hops = partners(shards)
    me = lax.axis_index("shard")
    v0_a = move(lowrank_v_matrix[0], perm=to_near)
    users = jnp.broadcast_to(person_embedding[None], (shards, *person_embedding.shape))
    users = lax.all_to_all(users, "shard", split_axis=0, concat_axis=0, tiled=True)

    parcel = pick_rows(
        kept_part_entries[:, 0, :].T, valid_slot_number.T, catalog_embedding, catalog_attributes
    )
    parcel = parcel.reshape(persons * 2, kept, 512)
    parcel, v0_a, users = lax.optimization_barrier((parcel, v0_a, users))
    recv = lax.all_to_all(parcel, AXES, split_axis=0, concat_axis=0, tiled=True)
    recv = recv.reshape(persons * 2 * kept, 512)

    small = jnp.concatenate([interaction_offset, final_projection[None, :].astype(F32)], 0)
    small, v0_a = lax.optimization_barrier((small, v0_a))
    small_a = move(small, perm=to_near)
    small_b = jnp.where(home, small, move(small, perm=ctx_far))
    v0_b = move(v0_a, perm=home_on)
    u0_a = move(lowrank_u_matrix[0], perm=to_near)
    v1_a = move(lowrank_v_matrix[1], perm=to_near)
    u1_a = move(lowrank_u_matrix[1], perm=to_near)
    v0_b, u0_a, u1_a = lax.optimization_barrier((v0_b, u0_a, u1_a))
    v0_b = jnp.where(home, lowrank_v_matrix[0], v0_b)
    u0_b = jnp.where(home, lowrank_u_matrix[0], move(u0_a, perm=away_swap))
    v1_b = jnp.where(home, lowrank_v_matrix[1], move(v1_a, perm=home_on))
    u1_b = jnp.where(home, lowrank_u_matrix[1], move(u1_a, perm=away_swap))

    ctx_a = move(lax.dynamic_index_in_dim(pair_attributes, 1 - parity, 0, False), perm=ctx_near)
    ctx_own = lax.dynamic_index_in_dim(pair_attributes, parity, 0, False)
    ctx_a, ctx_b = lax.optimization_barrier((ctx_a, move(ctx_own, perm=ctx_far)))
    ctx_b = jnp.where(home, ctx_own, ctx_b)
    ctx_a, u0_b, u1_b = lax.optimization_barrier((ctx_a, u0_b, u1_b))

    all_scores = jnp.einsum(
        "ue,ie->ui", users.reshape(persons, -1), catalog_embedding, preferred_element_type=F32
    )
    best = jnp.max(all_scores, axis=1).reshape(shards, persons // shards)
    order = [[i] for i in range(shards)]
    for pairs in hops:
        order = [order[i] + order[k] for i, k in pairs]
    order = lax.dynamic_index_in_dim(jnp.asarray(order, jnp.int32), me, 0, False)
    chosen = order[:, None] == jnp.arange(shards, dtype=jnp.int32)[None, :]
    best = jnp.sum(jnp.where(chosen[:, :, None], best[None], 0.0), axis=1)

    def halve(best, pairs):
        half = best.shape[0] // 2
        return jnp.maximum(best[:half], lax.ppermute(best[half:], "shard", pairs))

    def over_x(best, flip):
        return jnp.maximum(best, lax.ppermute(best, "tp", [(i, i ^ flip) for i in range(4)]))

    for pairs in hops[:2:-1]:
        best = halve(best, pairs)

    emb_other = lax.dynamic_index_in_dim(users, me ^ 1, 0, False)
    query = lax.dynamic_slice_in_dim(jnp.where(home, person_embedding, emb_other), parity, 1, 0)
    query = jnp.where(core == 0, query, jnp.zeros_like(query))
    zero = jnp.zeros_like(query)
    query = jnp.where(
        parity == 1, jnp.concatenate([query, zero], 1), jnp.concatenate([zero, query], 1)
    )
    query = jnp.broadcast_to(query, (16, 512))

    surv = pair_attributes.shape[1]
    tall, wide, lanes = ((surv, 512), BF), ((surv, 768), BF), ((16, surv), F32)
    part, head = call(
        context_kernel, "context_part", 24000, [((surv, 512), F32), ((512, 512), BF)], [],
        CTX, 8, [], [ctx_a, ctx_b, v0_a, v0_b], [],
    )
    recv, best = lax.optimization_barrier((recv, best))
    step = halve(best, hops[2])
    pay, piece, logit = call(
        first_kernel, "first_layer", 24000, [tall, tall, lanes],
        [pltpu.VMEM(recv.shape, BF), pltpu.VMEM((16, recv.shape[0]), F32)]
        + [pltpu.VMEM(recv.shape, BF), pltpu.SemaphoreType.DMA((recv.shape[0] // ROWS,))],
        FIRST, 8, [], [query, part, head], [recv],
    )
    piece, best = lax.optimization_barrier((piece, step))
    other, best = lax.optimization_barrier((move(piece, perm=to_core), halve(best, hops[1])))
    step = halve(best, hops[0])
    x_a, x_b, piece1 = call(
        second_kernel, "second_layer", 24000, [wide, wide, tall], [],
        SECOND, 12, [],
        [piece, other, pay, small_a, small_b, ctx_a, ctx_b, u0_a, u0_b, v1_a, v1_b], [],
    )
    piece1, best = lax.optimization_barrier((piece1, step))
    other1, best = lax.optimization_barrier((move(piece1, perm=to_core), over_x(best, 1)))
    step = over_x(best, 3)
    (score,) = call(
        last_kernel, "last_layer", 24000, [lanes], [], 1792, 10, [similarity_coefficient],
        [piece1, other1, pay, x_a, x_b, small_a, small_b, logit, ctx_a, ctx_b, u1_a, u1_b], [],
    )
    score, best = lax.optimization_barrier((score, step))
    top = jnp.where(home, lax.dynamic_slice_in_dim(best, parity, 1, 1), 0.0)
    score = score[0:1] - similarity_coefficient[0] * top
    score = score + move(score, perm=to_core)
    score_a = move(score, perm=to_near)
    score_b = jnp.where(home, score, move(score, perm=ctx_far))
    return jnp.where(
        parity == 1,
        jnp.concatenate([score_a, score_b], 0),
        jnp.concatenate([score_b, score_a], 0),
    )


def solution(mesh):
    return jax.shard_map(
        on_device,
        mesh=mesh,
        in_specs=(
            P("shard", None),
            P(("shard", "tp"), None),
            P(("shard", "tp"), None),
            P(None, ("shard", "tp"), None),
            P(None, ("shard", "tp")),
            P("shard", None, "tp"),
            P(None, "tp", None),
            P(None, None, "tp"),
            P(None, "tp"),
            P("tp"),
            P(),
        ),
        out_specs=P("shard", None),
        check_vma=False,
    )
```

```python
import functools

import jax
import jax.numpy as jnp
from jax import lax
from jax.experimental import pallas as pl
from jax.experimental.pallas import tpu as pltpu
from jax.sharding import PartitionSpec as P

BF = jnp.bfloat16
F32 = jnp.float32
AXES = ("shard", "tp")
VMEM = pl.BlockSpec(memory_space=pltpu.VMEM)
PICK, CTX, FIRST, SECOND = 4096, 6000, 15000, 15000
SMEM = pl.BlockSpec(memory_space=pltpu.SMEM)
ANY = pl.BlockSpec(memory_space=pl.ANY)


def grant(kbytes):
    return pltpu.CompilerParams(vmem_limit_bytes=kbytes * 1000)


def group_perm(groups, step, member=lambda x, c: True, turn=lambda x, c: 0):
    pairs = []
    for g in range(groups):
        for c in range(2):
            for x in range(4):
                if member(x, c):
                    x2, c2 = step(x, c)
                    g2 = g // 4 * 4 + (g + turn(x, c)) % 4
                    pairs.append((g * 8 + c * 4 + x, g2 * 8 + c2 * 4 + x2))
    return pairs


def is_home(x, c):
    return x // 2 == c


def is_away(x, c):
    return x // 2 != c


def near(x, c):
    return (x ^ 1, x // 2) if is_home(x, c) else (x ^ 3, x // 2)


def partners(shards):
    far_z = (6, 7, 4, 5, 2, 3, 0, 1)
    steps = []
    for of_z, of_y, of_core in (
        (lambda z: z ^ 1, None, None),
        (lambda z: z ^ 2, None, None),
        (lambda z: far_z[z], None, None),
        (None, 1, None),
        (None, 3, None),
        (None, None, 1),
    ):
        pairs = []
        for i in range(shards):
            z, y, c = i // 8, i // 2 % 4, i % 2
            z = of_z(z) if of_z else z
            y = y ^ of_y if of_y else y
            c = c ^ of_core if of_core else c
            pairs.append((i, z * 8 + y * 2 + c))
        steps.append(pairs)
    return steps


def dot(a, b):
    return jnp.dot(a, b, preferred_element_type=F32)


def dot_nt(a, b):
    return lax.dot_general(a, b, (((1,), (1,)), ((), ())), preferred_element_type=F32)


def call(kernel, name, kbytes, outs, scratch, mflops, mbytes, scalars, arrays, far, out_specs=None):
    return pl.pallas_call(
        kernel,
        in_specs=[SMEM] * len(scalars) + [VMEM] * len(arrays) + [ANY] * len(far),
        out_specs=out_specs or [VMEM] * len(outs),
        out_shape=[jax.ShapeDtypeStruct(shape, dtype) for shape, dtype in outs],
        scratch_shapes=scratch,
        compiler_params=grant(kbytes),
        cost_estimate=pl.CostEstimate(
            flops=mflops << 20, bytes_accessed=mbytes << 20, transcendentals=0
        ),
        name=name,
    )(*scalars, *arrays, *far)


def cut_kernel(where, v_ref, u_ref, ctx_ref, v_out, u_out, own_out, away_out, sems):
    layer, parity = where[0], where[1]
    copies = [
        pltpu.make_async_copy(v_ref.at[layer], v_out, sems.at[0]),
        pltpu.make_async_copy(u_ref.at[layer], u_out, sems.at[1]),
        pltpu.make_async_copy(ctx_ref.at[1 - parity], away_out, sems.at[2]),
        pltpu.make_async_copy(ctx_ref.at[parity], own_out, sems.at[3]),
    ]
    for copy in copies:
        copy.start()
    for copy in copies:
        copy.wait()


def cut_blocks(where, v, u, ctx):
    shapes = [v.shape[1:], u.shape[1:], ctx.shape[1:], ctx.shape[1:]]
    return pl.pallas_call(
        cut_kernel,
        in_specs=[SMEM, ANY, ANY, ANY],
        out_specs=[ANY] * 4,
        out_shape=[jax.ShapeDtypeStruct(shape, BF) for shape in shapes],
        scratch_shapes=[pltpu.SemaphoreType.DMA((4,))],
        compiler_params=grant(63000),
        cost_estimate=pl.CostEstimate(flops=0, bytes_accessed=7 << 20, transcendentals=0),
        name="cut_blocks",
    )(where, v, u, ctx)


def pick_kernel(
    kept_ref, count_ref, emb_hbm, attr_hbm, out_hbm, table, hot_ref, out_ref, in_sems, out_sems
):
    slots, persons = kept_ref.shape
    items = table.shape[1]
    loads = [pltpu.make_async_copy(emb_hbm, table.at[0], in_sems.at[0])]
    for q in range(3):
        columns = attr_hbm.at[:, pl.ds(q * 256, 256)]
        loads.append(pltpu.make_async_copy(columns, table.at[q + 1], in_sems.at[q + 1]))
    for load in loads:
        load.start()
    live = lax.broadcasted_iota(jnp.int32, (slots, persons), 0) < count_ref[...]
    wanted = jnp.where(live, kept_ref[...], 4095)
    digits = jnp.concatenate([wanted >> 6, wanted & 63], 0).astype(F32).astype(BF)
    n = 256
    blocks = persons * slots // n
    lane = lax.broadcasted_iota(jnp.int32, (n, 2 * slots), 1)
    slot = lax.broadcasted_iota(jnp.int32, (n, 2 * slots), 0) % slots
    odd = (lax.broadcasted_iota(jnp.int32, (n, 1), 0) // slots) % 2 == 1
    unused = []
    for b in range(blocks):
        row = lax.broadcasted_iota(jnp.int32, (n, persons), 0) + b * n
        owner = (row // slots == lax.broadcasted_iota(jnp.int32, (n, persons), 1)).astype(BF)
        both = dot_nt(owner, digits)
        high = jnp.where(lane == slot, both * 64.0, 0.0)
        low = jnp.where(lane == slot + slots, both, 0.0)
        rows = jnp.sum(high + low, axis=1, keepdims=True).astype(jnp.int32)
        hot = lax.broadcasted_iota(jnp.int32, (n, items), 1) == rows
        hot_ref[b * n : (b + 1) * n] = hot.astype(BF)
        unused.append(rows >= items)
    stores = []
    for c in range(2):
        loads[2 * c].wait()
        loads[2 * c + 1].wait()
        for b in range(blocks):
            hot = hot_ref[b * n : (b + 1) * n]
            low = jnp.where(unused[b], jnp.inf, dot(hot, table[2 * c]))
            high = jnp.where(unused[b], jnp.inf, dot(hot, table[2 * c + 1]))
            first = jnp.where(odd, low, high).astype(BF)
            second = jnp.where(odd, high, low).astype(BF)
            for g in range(n // 32):
                out_ref[c, b * (n // 32) + g, :, 0:256] = first[g * 32 : (g + 1) * 32]
                out_ref[c, b * (n // 32) + g, :, 256:512] = second[g * 32 : (g + 1) * 32]
        stores.append(pltpu.make_async_copy(out_ref.at[c], out_hbm.at[:, c], out_sems.at[c]))
        stores[-1].start()
    for store in stores:
        store.wait()


def pick_rows(kept, count, emb, attr):
    slots, persons = kept.shape
    out = (persons // 4, 2, 4 * slots, 512)
    return pl.pallas_call(
        pick_kernel,
        in_specs=[VMEM, VMEM, ANY, ANY],
        out_specs=ANY,
        out_shape=jax.ShapeDtypeStruct(out, BF),
        scratch_shapes=[
            pltpu.VMEM((4, emb.shape[0], 256), BF),
            pltpu.VMEM((persons * slots, emb.shape[0]), BF),
            pltpu.VMEM((2, persons // 4, 4 * slots, 512), BF),
            pltpu.SemaphoreType.DMA((4,)),
            pltpu.SemaphoreType.DMA((2,)),
        ],
        compiler_params=grant(62500),
        cost_estimate=pl.CostEstimate(
            flops=PICK << 20, bytes_accessed=6 << 20, transcendentals=0
        ),
        name="pick_rows",
    )(kept, count, emb, attr)


ROWS = 256


def block_copies(src, dst, sems):
    copies = []
    for i in range(dst.shape[0] // ROWS):
        here = pl.ds(i * ROWS, ROWS)
        copies.append(pltpu.make_async_copy(src.at[here], dst.at[here], sems.at[i]))
        copies[-1].start()
    return copies


def context_kernel(ca_ref, cb_ref, va_ref, vb_ref, part_ref, head_ref):
    head_ref[0:256] = va_ref[0:256]
    head_ref[256:512] = vb_ref[0:256]
    for i in range(part_ref.shape[0] // ROWS):
        here = pl.ds(i * ROWS, ROWS)
        part_ref[here] = dot(ca_ref[here], va_ref[256:768]) + dot(cb_ref[here], vb_ref[256:768])


def first_kernel(
    u_ref, part_ref, head_ref, recv_hbm, pay_ref, piece_ref, logit_ref,
    clean, place, recv_ref, recv_sems,
):
    slots = recv_ref.shape[0]
    recv_copies = block_copies(recv_hbm, recv_ref, recv_sems)
    r = lax.broadcasted_iota(jnp.int32, (ROWS, ROWS), 0)
    q = lax.broadcasted_iota(jnp.int32, (ROWS, ROWS), 1)
    upper = (r <= q).astype(BF)
    lane0 = (lax.broadcasted_iota(jnp.int32, (16, 128), 1) == 0).astype(BF)
    before = jnp.zeros((16, 1), F32)
    for i in range(slots // ROWS):
        here = slice(i * ROWS, (i + 1) * ROWS)
        recv_copies[i].wait()
        got = recv_ref[here].astype(F32)
        live = got < jnp.inf
        clean[here] = jnp.where(live, got, 0.0).astype(BF)
        marks = dot_nt(lane0, live[:, 0:128].astype(F32).astype(BF))
        upto = dot(marks.astype(BF), upper) + before
        place[:, here] = jnp.where(marks > 0.5, upto - 1.0, -1.0)
        before = upto[:, ROWS - 1 : ROWS]
    for i in range(pay_ref.shape[0] // ROWS):
        here = pl.ds(i * ROWS, ROWS)
        k = (lax.broadcasted_iota(jnp.int32, (ROWS, slots), 0) + i * ROWS).astype(F32)
        hot = (k == place[0:1, :]).astype(BF)
        pay = dot(hot, clean[...]).astype(BF)
        pay_ref[here] = pay
        piece = part_ref[here] + dot(pay, head_ref[...])
        piece_ref[here] = piece.astype(BF)
        logit_ref[:, here] = dot_nt(u_ref[...], pay)


def cross(x0, hidden, offset, x):
    x0 = x0.astype(F32)
    return (x0 * (hidden + offset) + x.astype(F32)).astype(BF)


def second_kernel(
    mine_ref, other_ref, pay_ref, ba_ref, bb_ref, ca_ref, cb_ref,
    ua_ref, ub_ref, va_ref, vb_ref, xa_ref, xb_ref, piece_ref,
):
    for i in range(pay_ref.shape[0] // ROWS):
        here = pl.ds(i * ROWS, ROWS)
        proj = (mine_ref[here].astype(F32) + other_ref[here].astype(F32)).astype(BF)
        slots = (
            (xa_ref, ua_ref, ba_ref, ca_ref, 0),
            (xb_ref, ub_ref, bb_ref, cb_ref, 256),
        )
        for x_ref, u_ref, b_ref, c_ref, at in slots:
            hidden = dot(proj, u_ref[...])
            pay = pay_ref[here, at : at + 256]
            ctx = c_ref[here]
            x_ref[here, 0:256] = cross(pay, hidden[:, 0:256], b_ref[0:1, 0:256], pay)
            x_ref[here, 256:768] = cross(ctx, hidden[:, 256:768], b_ref[0:1, 256:768], ctx)
        piece = dot(xa_ref[here], va_ref[...]) + dot(xb_ref[here], vb_ref[...])
        piece_ref[here] = piece.astype(BF)


def last_kernel(
    coefficient, mine_ref, other_ref, pay_ref, xa_ref, xb_ref, sa_ref, sb_ref, logit_ref,
    ca_ref, cb_ref, ua_ref, ub_ref, score_ref,
):
    for i in range(pay_ref.shape[0] // ROWS):
        here = pl.ds(i * ROWS, ROWS)
        proj = (mine_ref[here].astype(F32) + other_ref[here].astype(F32)).astype(BF)
        score = coefficient[0] * logit_ref[:, here]
        for x_ref, u_ref, s_ref, c_ref, at in (
            (xa_ref, ua_ref, sa_ref, ca_ref, 0),
            (xb_ref, ub_ref, sb_ref, cb_ref, 256),
        ):
            hidden = dot(proj, u_ref[...])
            low = cross(
                pay_ref[here, at : at + 256], hidden[:, 0:256], s_ref[1:2, 0:256], x_ref[here, 0:256]
            )
            high = cross(
                c_ref[here], hidden[:, 256:768], s_ref[1:2, 256:768], x_ref[here, 256:768]
            )
            out = jnp.broadcast_to(s_ref[2:3, :], (16, 768)).astype(BF)
            score = score + dot_nt(out[:, 0:256], low) + dot_nt(out[:, 256:768], high)
        score_ref[:, here] = score


def on_device(
    person_embedding,
    catalog_embedding,
    catalog_attributes,
    kept_part_entries,
    valid_slot_number,
    pair_attributes,
    lowrank_v_matrix,
    lowrank_u_matrix,
    interaction_offset,
    final_projection,
    similarity_coefficient,
):
    shards = lax.axis_size("shard")
    groups = shards // 2
    x = lax.axis_index("tp")
    core = lax.axis_index("shard") % 2
    home = x // 2 == core
    parity = x % 2
    move = functools.partial(lax.ppermute, axis_name=AXES)
    to_core = group_perm(groups, lambda x, c: (x, 1 - c))
    to_near = group_perm(groups, near)
    home_on = group_perm(groups, lambda x, c: (x ^ 3, c), is_home)
    away_swap = group_perm(groups, lambda x, c: (x ^ 1, c), is_away)
    ctx_near = group_perm(groups, lambda x, c: (x ^ 1, c) if is_home(x, c) else (x ^ 3, 1 - c))
    ctx_far = group_perm(groups, lambda x, c: (x ^ 2, 1 - c), is_away)

    def stay(x, c):
        return x, c

    y_up = group_perm(groups, stay, turn=lambda x, c: 1)
    y_mixed = group_perm(groups, stay, turn=lambda x, c: -1 if is_home(x, c) else 1)
    y_down = group_perm(groups, stay, is_away, lambda x, c: -1)
    odd_y = lax.axis_index("shard") // 2 % 2
    persons, _, kept = kept_part_entries.shape
    hops = partners(shards)
    me = lax.axis_index("shard")
    v_mine, u_mine, ctx_own, ctx_away = cut_blocks(
        jnp.stack([odd_y, parity]), lowrank_v_matrix, lowrank_u_matrix, pair_attributes
    )
    v_near = move(v_mine, perm=to_near)
    u_near = move(u_mine, perm=to_near)
    ctx_a = move(ctx_away, perm=ctx_near)
    ctx_b = move(ctx_own, perm=ctx_far)
    users = jnp.broadcast_to(person_embedding[None], (shards, *person_embedding.shape))
    users = lax.all_to_all(users, "shard", split_axis=0, concat_axis=0, tiled=True)

    parcel = pick_rows(
        kept_part_entries[:, 0, :].T, valid_slot_number.T, catalog_embedding, catalog_attributes
    )
    parcel = parcel.reshape(persons * 2, kept, 512)
    parcel, v_near, u_near, users = lax.optimization_barrier((parcel, v_near, u_near, users))
    recv = lax.all_to_all(parcel, AXES, split_axis=0, concat_axis=0, tiled=True)
    recv = recv.reshape(persons * 2 * kept, 512)

    all_scores = jnp.einsum(
        "ue,ie->ui", users.reshape(persons, -1), catalog_embedding, preferred_element_type=F32
    )
    best = jnp.max(all_scores, axis=1).reshape(shards, persons // shards)
    order = [[i] for i in range(shards)]
    for pairs in hops:
        order = [order[i] + order[k] for i, k in pairs]
    order = lax.dynamic_index_in_dim(jnp.asarray(order, jnp.int32), me, 0, False)
    chosen = order[:, None] == jnp.arange(shards, dtype=jnp.int32)[None, :]
    best = jnp.sum(jnp.where(chosen[:, :, None], best[None], 0.0), axis=1)

    def halve(best, pairs):
        half = best.shape[0] // 2
        return jnp.maximum(best[:half], lax.ppermute(best[half:], "shard", pairs))

    def over_x(best):
        out = best
        for flip in (1, 3, 2):
            out = jnp.maximum(out, lax.ppermute(best, "tp", [(i, i ^ flip) for i in range(4)]))
        return out

    def over_y(best):
        n = best.shape[0] // 4
        out = best[:n]
        for block, flip in ((1, 1), (2, 3), (3, 2)):
            pairs = [(i, i ^ (2 * flip)) for i in range(shards)]
            got = lax.ppermute(best[block * n : (block + 1) * n], "shard", pairs)
            out = jnp.maximum(out, got)
        return out

    best = halve(best, hops[5])

    v_far = move(v_near, perm=home_on)
    u_far = move(u_near, perm=away_swap)
    v_near_y = move(v_near, perm=y_up)
    v_far_y = move(v_far, perm=y_down)
    u_near_y = move(u_near, perm=y_mixed)
    u_far_y = move(u_far, perm=y_down)
    even = odd_y == 0
    v0_a = jnp.where(even, v_near, v_near_y)
    v1_a = jnp.where(even, v_near_y, v_near)
    u0_a = jnp.where(even, u_near, u_near_y)
    u1_a = jnp.where(even, u_near_y, u_near)
    v0_b = jnp.where(home, lowrank_v_matrix[0], jnp.where(even, v_far, v_far_y))
    v1_b = jnp.where(home, lowrank_v_matrix[1], jnp.where(even, v_far_y, v_far))
    u0_b = jnp.where(home, lowrank_u_matrix[0], jnp.where(even, u_far, u_far_y))
    u1_b = jnp.where(home, lowrank_u_matrix[1], jnp.where(even, u_far_y, u_far))
    ctx_b = jnp.where(home, ctx_own, ctx_b)
    small = jnp.concatenate([interaction_offset, final_projection[None, :].astype(F32)], 0)
    small, _ = lax.optimization_barrier((small, u_far))
    small_a = move(small, perm=to_near)
    small_b = jnp.where(home, small, move(small, perm=ctx_far))
    ctx_a, u0_a, u0_b, u1_a, u1_b = lax.optimization_barrier((ctx_a, u0_a, u0_b, u1_a, u1_b))

    emb_other = lax.dynamic_index_in_dim(users, me ^ 1, 0, False)
    query = lax.dynamic_slice_in_dim(jnp.where(home, person_embedding, emb_other), parity, 1, 0)
    query = jnp.where(core == 0, query, jnp.zeros_like(query))
    zero = jnp.zeros_like(query)
    query = jnp.where(
        parity == 1, jnp.concatenate([query, zero], 1), jnp.concatenate([zero, query], 1)
    )
    query = jnp.broadcast_to(query, (16, 512))

    surv = pair_attributes.shape[1]
    tall, wide, lanes = ((surv, 512), BF), ((surv, 768), BF), ((16, surv), F32)
    part, head = call(
        context_kernel, "context_part", 24000, [((surv, 512), F32), ((512, 512), BF)], [],
        CTX, 8, [], [ctx_a, ctx_b, v0_a, v0_b], [],
    )
    recv, best = lax.optimization_barrier((recv, best))
    step = over_y(best)
    pay, piece, logit = call(
        first_kernel, "first_layer", 24000, [tall, tall, lanes],
        [pltpu.VMEM(recv.shape, BF), pltpu.VMEM((16, recv.shape[0]), F32)]
        + [pltpu.VMEM(recv.shape, BF), pltpu.SemaphoreType.DMA((recv.shape[0] // ROWS,))],
        FIRST, 8, [], [query, part, head], [recv],
    )
    piece, best = lax.optimization_barrier((piece, step))
    other, best = lax.optimization_barrier((move(piece, perm=to_core), halve(best, hops[2])))
    step = halve(best, hops[1])
    x_a, x_b, piece1 = call(
        second_kernel, "second_layer", 24000, [wide, wide, tall], [],
        SECOND, 12, [],
        [piece, other, pay, small_a, small_b, ctx_a, ctx_b, u0_a, u0_b, v1_a, v1_b], [],
    )
    piece1, best = lax.optimization_barrier((piece1, step))
    other1, best = lax.optimization_barrier((move(piece1, perm=to_core), halve(best, hops[0])))
    step = over_x(best)
    (score,) = call(
        last_kernel, "last_layer", 24000, [lanes], [], 1792, 10, [similarity_coefficient],
        [piece1, other1, pay, x_a, x_b, small_a, small_b, logit, ctx_a, ctx_b, u1_a, u1_b], [],
    )
    score, best = lax.optimization_barrier((score, step))
    top = jnp.where(home, lax.dynamic_slice_in_dim(best, parity, 1, 1), 0.0)
    score = score[0:1] - similarity_coefficient[0] * top
    score = score + move(score, perm=to_core)
    score_a = move(score, perm=to_near)
    score_b = jnp.where(home, score, move(score, perm=ctx_far))
    return jnp.where(
        parity == 1,
        jnp.concatenate([score_a, score_b], 0),
        jnp.concatenate([score_b, score_a], 0),
    )


def solution(mesh):
    return jax.shard_map(
        on_device,
        mesh=mesh,
        in_specs=(
            P("shard", None),
            P(("shard", "tp"), None),
            P(("shard", "tp"), None),
            P(None, ("shard", "tp"), None),
            P(None, ("shard", "tp")),
            P("shard", None, "tp"),
            P(None, "tp", None),
            P(None, None, "tp"),
            P(None, "tp"),
            P("tp"),
            P(),
        ),
        out_specs=P("shard", None),
        check_vma=False,
    )
```

```python
import functools

import jax
import jax.numpy as jnp
from jax import lax
from jax.experimental import pallas as pl
from jax.experimental.pallas import tpu as pltpu
from jax.sharding import PartitionSpec as P

BF = jnp.bfloat16
F32 = jnp.float32
AXES = ("shard", "tp")
VMEM = pl.BlockSpec(memory_space=pltpu.VMEM)
PICK, CTX, FIRST, SECOND = 4096, 6000, 15000, 15000
SMEM = pl.BlockSpec(memory_space=pltpu.SMEM)
ANY = pl.BlockSpec(memory_space=pl.ANY)


def grant(kbytes):
    return pltpu.CompilerParams(vmem_limit_bytes=kbytes * 1000)


def group_perm(groups, step, member=lambda x, c: True, turn=lambda x, c: 0):
    pairs = []
    for g in range(groups):
        for c in range(2):
            for x in range(4):
                if member(x, c):
                    x2, c2 = step(x, c)
                    g2 = g // 4 * 4 + (g + turn(x, c)) % 4
                    pairs.append((g * 8 + c * 4 + x, g2 * 8 + c2 * 4 + x2))
    return pairs


def is_home(x, c):
    return x // 2 == c


def is_away(x, c):
    return x // 2 != c


def near(x, c):
    return (x ^ 1, x // 2) if is_home(x, c) else (x ^ 3, x // 2)


def partners(shards):
    far_z = (6, 7, 4, 5, 2, 3, 0, 1)
    steps = []
    for of_z, of_y, of_core in (
        (lambda z: z ^ 1, None, None),
        (lambda z: z ^ 2, None, None),
        (lambda z: far_z[z], None, None),
        (None, 1, None),
        (None, 3, None),
        (None, None, 1),
    ):
        pairs = []
        for i in range(shards):
            z, y, c = i // 8, i // 2 % 4, i % 2
            z = of_z(z) if of_z else z
            y = y ^ of_y if of_y else y
            c = c ^ of_core if of_core else c
            pairs.append((i, z * 8 + y * 2 + c))
        steps.append(pairs)
    return steps


def dot(a, b):
    return jnp.dot(a, b, preferred_element_type=F32)


def dot_nt(a, b):
    return lax.dot_general(a, b, (((1,), (1,)), ((), ())), preferred_element_type=F32)


def call(kernel, name, kbytes, outs, scratch, mflops, mbytes, scalars, arrays, far, out_specs=None):
    return pl.pallas_call(
        kernel,
        in_specs=[SMEM] * len(scalars) + [VMEM] * len(arrays) + [ANY] * len(far),
        out_specs=out_specs or [VMEM] * len(outs),
        out_shape=[jax.ShapeDtypeStruct(shape, dtype) for shape, dtype in outs],
        scratch_shapes=scratch,
        compiler_params=grant(kbytes),
        cost_estimate=pl.CostEstimate(
            flops=mflops << 20, bytes_accessed=mbytes << 20, transcendentals=0
        ),
        name=name,
    )(*scalars, *arrays, *far)


def pick_kernel(
    kept_ref, count_ref, emb_hbm, attr_hbm, out_hbm, table, hot_ref, out_ref, in_sems, out_sems
):
    slots, persons = kept_ref.shape
    items = table.shape[1]
    loads = [pltpu.make_async_copy(emb_hbm, table.at[0], in_sems.at[0])]
    for q in range(3):
        columns = attr_hbm.at[:, pl.ds(q * 256, 256)]
        loads.append(pltpu.make_async_copy(columns, table.at[q + 1], in_sems.at[q + 1]))
    for load in loads:
        load.start()
    live = lax.broadcasted_iota(jnp.int32, (slots, persons), 0) < count_ref[...]
    wanted = jnp.where(live, kept_ref[...], 4095)
    digits = jnp.concatenate([wanted >> 6, wanted & 63], 0).astype(F32).astype(BF)
    n = 256
    blocks = persons * slots // n
    lane = lax.broadcasted_iota(jnp.int32, (n, 2 * slots), 1)
    slot = lax.broadcasted_iota(jnp.int32, (n, 2 * slots), 0) % slots
    odd = (lax.broadcasted_iota(jnp.int32, (n, 1), 0) // slots) % 2 == 1
    unused = []
    for b in range(blocks):
        row = lax.broadcasted_iota(jnp.int32, (n, persons), 0) + b * n
        owner = (row // slots == lax.broadcasted_iota(jnp.int32, (n, persons), 1)).astype(BF)
        both = dot_nt(owner, digits)
        high = jnp.where(lane == slot, both * 64.0, 0.0)
        low = jnp.where(lane == slot + slots, both, 0.0)
        rows = jnp.sum(high + low, axis=1, keepdims=True).astype(jnp.int32)
        hot = lax.broadcasted_iota(jnp.int32, (n, items), 1) == rows
        hot_ref[b * n : (b + 1) * n] = hot.astype(BF)
        unused.append(rows >= items)
    stores = []
    for c in range(2):
        loads[2 * c].wait()
        loads[2 * c + 1].wait()
        for b in range(blocks):
            hot = hot_ref[b * n : (b + 1) * n]
            low = jnp.where(unused[b], jnp.inf, dot(hot, table[2 * c]))
            high = jnp.where(unused[b], jnp.inf, dot(hot, table[2 * c + 1]))
            first = jnp.where(odd, low, high).astype(BF)
            second = jnp.where(odd, high, low).astype(BF)
            for g in range(n // 32):
                out_ref[c, b * (n // 32) + g, :, 0:256] = first[g * 32 : (g + 1) * 32]
                out_ref[c, b * (n // 32) + g, :, 256:512] = second[g * 32 : (g + 1) * 32]
        stores.append(pltpu.make_async_copy(out_ref.at[c], out_hbm.at[:, c], out_sems.at[c]))
        stores[-1].start()
    for store in stores:
        store.wait()


def pick_rows(kept, count, emb, attr):
    slots, persons = kept.shape
    out = (persons // 4, 2, 4 * slots, 512)
    return pl.pallas_call(
        pick_kernel,
        in_specs=[VMEM, VMEM, ANY, ANY],
        out_specs=ANY,
        out_shape=jax.ShapeDtypeStruct(out, BF),
        scratch_shapes=[
            pltpu.VMEM((4, emb.shape[0], 256), BF),
            pltpu.VMEM((persons * slots, emb.shape[0]), BF),
            pltpu.VMEM((2, persons // 4, 4 * slots, 512), BF),
            pltpu.SemaphoreType.DMA((4,)),
            pltpu.SemaphoreType.DMA((2,)),
        ],
        compiler_params=grant(62500),
        cost_estimate=pl.CostEstimate(
            flops=PICK << 20, bytes_accessed=6 << 20, transcendentals=0
        ),
        name="pick_rows",
    )(kept, count, emb, attr)


ROWS = 256


def block_copies(src, dst, sems):
    copies = []
    for i in range(dst.shape[0] // ROWS):
        here = pl.ds(i * ROWS, ROWS)
        copies.append(pltpu.make_async_copy(src.at[here], dst.at[here], sems.at[i]))
        copies[-1].start()
    return copies


def context_kernel(ca_ref, cb_ref, va_ref, vb_ref, part_ref, head_ref):
    head_ref[0:256] = va_ref[0:256]
    head_ref[256:512] = vb_ref[0:256]
    for i in range(part_ref.shape[0] // ROWS):
        here = pl.ds(i * ROWS, ROWS)
        part_ref[here] = dot(ca_ref[here], va_ref[256:768]) + dot(cb_ref[here], vb_ref[256:768])


def first_kernel(
    u_ref, part_ref, head_ref, recv_hbm, pay_ref, piece_ref, logit_ref,
    clean, place, recv_ref, recv_sems,
):
    slots = recv_ref.shape[0]
    recv_copies = block_copies(recv_hbm, recv_ref, recv_sems)
    r = lax.broadcasted_iota(jnp.int32, (ROWS, ROWS), 0)
    q = lax.broadcasted_iota(jnp.int32, (ROWS, ROWS), 1)
    upper = (r <= q).astype(BF)
    lane0 = (lax.broadcasted_iota(jnp.int32, (16, 128), 1) == 0).astype(BF)
    before = jnp.zeros((16, 1), F32)
    for i in range(slots // ROWS):
        here = slice(i * ROWS, (i + 1) * ROWS)
        recv_copies[i].wait()
        got = recv_ref[here].astype(F32)
        live = got < jnp.inf
        clean[here] = jnp.where(live, got, 0.0).astype(BF)
        marks = dot_nt(lane0, live[:, 0:128].astype(F32).astype(BF))
        upto = dot(marks.astype(BF), upper) + before
        place[:, here] = jnp.where(marks > 0.5, upto - 1.0, -1.0)
        before = upto[:, ROWS - 1 : ROWS]
    for i in range(pay_ref.shape[0] // ROWS):
        here = pl.ds(i * ROWS, ROWS)
        k = (lax.broadcasted_iota(jnp.int32, (ROWS, slots), 0) + i * ROWS).astype(F32)
        hot = (k == place[0:1, :]).astype(BF)
        pay = dot(hot, clean[...]).astype(BF)
        pay_ref[here] = pay
        piece = part_ref[here] + dot(pay, head_ref[...])
        piece_ref[here] = piece.astype(BF)
        logit_ref[:, here] = dot_nt(u_ref[...], pay)


def cross(x0, hidden, offset, x):
    x0 = x0.astype(F32)
    return (x0 * (hidden + offset) + x.astype(F32)).astype(BF)


def second_kernel(
    mine_ref, other_ref, pay_ref, ba_ref, bb_ref, ca_ref, cb_ref,
    ua_ref, ub_ref, va_ref, vb_ref, xa_ref, xb_ref, piece_ref,
):
    for i in range(pay_ref.shape[0] // ROWS):
        here = pl.ds(i * ROWS, ROWS)
        proj = (mine_ref[here].astype(F32) + other_ref[here].astype(F32)).astype(BF)
        slots = (
            (xa_ref, ua_ref, ba_ref, ca_ref, 0),
            (xb_ref, ub_ref, bb_ref, cb_ref, 256),
        )
        for x_ref, u_ref, b_ref, c_ref, at in slots:
            hidden = dot(proj, u_ref[...])
            pay = pay_ref[here, at : at + 256]
            ctx = c_ref[here]
            x_ref[here, 0:256] = cross(pay, hidden[:, 0:256], b_ref[0:1, 0:256], pay)
            x_ref[here, 256:768] = cross(ctx, hidden[:, 256:768], b_ref[0:1, 256:768], ctx)
        piece = dot(xa_ref[here], va_ref[...]) + dot(xb_ref[here], vb_ref[...])
        piece_ref[here] = piece.astype(BF)


def last_kernel(
    coefficient, mine_ref, other_ref, pay_ref, xa_ref, xb_ref, sa_ref, sb_ref, logit_ref,
    ca_ref, cb_ref, ua_ref, ub_ref, score_ref,
):
    for i in range(pay_ref.shape[0] // ROWS):
        here = pl.ds(i * ROWS, ROWS)
        proj = (mine_ref[here].astype(F32) + other_ref[here].astype(F32)).astype(BF)
        score = coefficient[0] * logit_ref[:, here]
        for x_ref, u_ref, s_ref, c_ref, at in (
            (xa_ref, ua_ref, sa_ref, ca_ref, 0),
            (xb_ref, ub_ref, sb_ref, cb_ref, 256),
        ):
            hidden = dot(proj, u_ref[...])
            low = cross(
                pay_ref[here, at : at + 256], hidden[:, 0:256], s_ref[1:2, 0:256], x_ref[here, 0:256]
            )
            high = cross(
                c_ref[here], hidden[:, 256:768], s_ref[1:2, 256:768], x_ref[here, 256:768]
            )
            out = jnp.broadcast_to(s_ref[2:3, :], (16, 768)).astype(BF)
            score = score + dot_nt(out[:, 0:256], low) + dot_nt(out[:, 256:768], high)
        score_ref[:, here] = score


def on_device(
    person_embedding,
    catalog_embedding,
    catalog_attributes,
    kept_part_entries,
    valid_slot_number,
    pair_attributes,
    lowrank_v_matrix,
    lowrank_u_matrix,
    interaction_offset,
    final_projection,
    similarity_coefficient,
):
    shards = lax.axis_size("shard")
    groups = shards // 2
    x = lax.axis_index("tp")
    core = lax.axis_index("shard") % 2
    home = x // 2 == core
    parity = x % 2
    move = functools.partial(lax.ppermute, axis_name=AXES)
    to_core = group_perm(groups, lambda x, c: (x, 1 - c))
    to_near = group_perm(groups, near)
    home_on = group_perm(groups, lambda x, c: (x ^ 3, c), is_home)
    away_swap = group_perm(groups, lambda x, c: (x ^ 1, c), is_away)
    ctx_near = group_perm(groups, lambda x, c: (x ^ 1, c) if is_home(x, c) else (x ^ 3, 1 - c))
    ctx_far = group_perm(groups, lambda x, c: (x ^ 2, 1 - c), is_away)

    def stay(x, c):
        return x, c

    y_up = group_perm(groups, stay, turn=lambda x, c: 1)
    y_mixed = group_perm(groups, stay, turn=lambda x, c: -1 if is_home(x, c) else 1)
    y_down = group_perm(groups, stay, is_away, lambda x, c: -1)
    odd_y = lax.axis_index("shard") // 2 % 2
    persons, _, kept = kept_part_entries.shape
    hops = partners(shards)
    me = lax.axis_index("shard")
    v_near = move(lax.dynamic_index_in_dim(lowrank_v_matrix, odd_y, 0, False), perm=to_near)
    u_near = move(lax.dynamic_index_in_dim(lowrank_u_matrix, odd_y, 0, False), perm=to_near)
    ctx_own = lax.dynamic_index_in_dim(pair_attributes, parity, 0, False)
    ctx_away = lax.dynamic_index_in_dim(pair_attributes, 1 - parity, 0, False)
    users = jnp.broadcast_to(person_embedding[None], (shards, *person_embedding.shape))
    users = lax.all_to_all(users, "shard", split_axis=0, concat_axis=0, tiled=True)

    parcel = pick_rows(
        kept_part_entries[:, 0, :].T, valid_slot_number.T, catalog_embedding, catalog_attributes
    )
    parcel = parcel.reshape(persons * 2, kept, 512)
    parcel, v_near, u_near, users = lax.optimization_barrier((parcel, v_near, u_near, users))
    recv = lax.all_to_all(parcel, AXES, split_axis=0, concat_axis=0, tiled=True)
    recv = recv.reshape(persons * 2 * kept, 512)

    v_far = move(v_near, perm=home_on)
    u_far = move(u_near, perm=away_swap)
    v_near_y = move(v_near, perm=y_up)
    v_far, u_near_on, ctx_out, ctx_away = lax.optimization_barrier(
        (v_far, u_near, ctx_own, ctx_away)
    )
    ctx_a = move(ctx_away, perm=ctx_near)
    ctx_b = move(ctx_out, perm=ctx_far)
    ctx_a, ctx_b = lax.optimization_barrier((ctx_a, ctx_b))
    v_far_y = move(v_far, perm=y_down)
    u_near_y = move(u_near_on, perm=y_mixed)
    u_far_y = move(u_far, perm=y_down)

    all_scores = jnp.einsum(
        "ue,ie->ui", users.reshape(persons, -1), catalog_embedding, preferred_element_type=F32
    )
    best = jnp.max(all_scores, axis=1).reshape(shards, persons // shards)
    order = [[i] for i in range(shards)]
    for pairs in hops:
        order = [order[i] + order[k] for i, k in pairs]
    order = lax.dynamic_index_in_dim(jnp.asarray(order, jnp.int32), me, 0, False)
    chosen = order[:, None] == jnp.arange(shards, dtype=jnp.int32)[None, :]
    best = jnp.sum(jnp.where(chosen[:, :, None], best[None], 0.0), axis=1)

    def halve(best, pairs):
        half = best.shape[0] // 2
        return jnp.maximum(best[:half], lax.ppermute(best[half:], "shard", pairs))

    def over_x(best):
        out = best
        for flip in (1, 3, 2):
            out = jnp.maximum(out, lax.ppermute(best, "tp", [(i, i ^ flip) for i in range(4)]))
        return out

    def over_y(best):
        n = best.shape[0] // 4
        out = best[:n]
        for block, flip in ((1, 1), (2, 3), (3, 2)):
            pairs = [(i, i ^ (2 * flip)) for i in range(shards)]
            got = lax.ppermute(best[block * n : (block + 1) * n], "shard", pairs)
            out = jnp.maximum(out, got)
        return out

    best = halve(best, hops[5])

    even = odd_y == 0
    v0_a = jnp.where(even, v_near, v_near_y)
    v1_a = jnp.where(even, v_near_y, v_near)
    u0_a = jnp.where(even, u_near, u_near_y)
    u1_a = jnp.where(even, u_near_y, u_near)
    v0_b = jnp.where(home, lowrank_v_matrix[0], jnp.where(even, v_far, v_far_y))
    v1_b = jnp.where(home, lowrank_v_matrix[1], jnp.where(even, v_far_y, v_far))
    u0_b = jnp.where(home, lowrank_u_matrix[0], jnp.where(even, u_far, u_far_y))
    u1_b = jnp.where(home, lowrank_u_matrix[1], jnp.where(even, u_far_y, u_far))
    ctx_b = jnp.where(home, ctx_own, ctx_b)
    small = jnp.concatenate([interaction_offset, final_projection[None, :].astype(F32)], 0)
    small, _ = lax.optimization_barrier((small, u_far))
    small_a = move(small, perm=to_near)
    small_b = jnp.where(home, small, move(small, perm=ctx_far))
    ctx_a, u0_a, u0_b, u1_a, u1_b = lax.optimization_barrier((ctx_a, u0_a, u0_b, u1_a, u1_b))

    emb_other = lax.dynamic_index_in_dim(users, me ^ 1, 0, False)
    query = lax.dynamic_slice_in_dim(jnp.where(home, person_embedding, emb_other), parity, 1, 0)
    query = jnp.where(core == 0, query, jnp.zeros_like(query))
    zero = jnp.zeros_like(query)
    query = jnp.where(
        parity == 1, jnp.concatenate([query, zero], 1), jnp.concatenate([zero, query], 1)
    )
    query = jnp.broadcast_to(query, (16, 512))

    surv = pair_attributes.shape[1]
    tall, wide, lanes = ((surv, 512), BF), ((surv, 768), BF), ((16, surv), F32)
    part, head = call(
        context_kernel, "context_part", 24000, [((surv, 512), F32), ((512, 512), BF)], [],
        CTX, 8, [], [ctx_a, ctx_b, v0_a, v0_b], [],
    )
    recv, best = lax.optimization_barrier((recv, best))
    step = over_y(best)
    pay, piece, logit = call(
        first_kernel, "first_layer", 24000, [tall, tall, lanes],
        [pltpu.VMEM(recv.shape, BF), pltpu.VMEM((16, recv.shape[0]), F32)]
        + [pltpu.VMEM(recv.shape, BF), pltpu.SemaphoreType.DMA((recv.shape[0] // ROWS,))],
        FIRST, 8, [], [query, part, head], [recv],
    )
    piece, best = lax.optimization_barrier((piece, step))
    other, best = lax.optimization_barrier((move(piece, perm=to_core), halve(best, hops[2])))
    step = halve(best, hops[1])
    x_a, x_b, piece1 = call(
        second_kernel, "second_layer", 24000, [wide, wide, tall], [],
        SECOND, 12, [],
        [piece, other, pay, small_a, small_b, ctx_a, ctx_b, u0_a, u0_b, v1_a, v1_b], [],
    )
    piece1, best = lax.optimization_barrier((piece1, step))
    other1, best = lax.optimization_barrier((move(piece1, perm=to_core), halve(best, hops[0])))
    step = over_x(best)
    (score,) = call(
        last_kernel, "last_layer", 24000, [lanes], [], 1792, 10, [similarity_coefficient],
        [piece1, other1, pay, x_a, x_b, small_a, small_b, logit, ctx_a, ctx_b, u1_a, u1_b], [],
    )
    score, best = lax.optimization_barrier((score, step))
    top = jnp.where(home, lax.dynamic_slice_in_dim(best, parity, 1, 1), 0.0)
    score = score[0:1] - similarity_coefficient[0] * top
    score = score + move(score, perm=to_core)
    score_a = move(score, perm=to_near)
    score_b = jnp.where(home, score, move(score, perm=ctx_far))
    return jnp.where(
        parity == 1,
        jnp.concatenate([score_a, score_b], 0),
        jnp.concatenate([score_b, score_a], 0),
    )


def solution(mesh):
    return jax.shard_map(
        on_device,
        mesh=mesh,
        in_specs=(
            P("shard", None),
            P(("shard", "tp"), None),
            P(("shard", "tp"), None),
            P(None, ("shard", "tp"), None),
            P(None, ("shard", "tp")),
            P("shard", None, "tp"),
            P(None, "tp", None),
            P(None, None, "tp"),
            P(None, "tp"),
            P("tp"),
            P(),
        ),
        out_specs=P("shard", None),
        check_vma=False,
    )
```

```python
import functools

import jax
import jax.numpy as jnp
from jax import lax
from jax.experimental import pallas as pl
from jax.experimental.pallas import tpu as pltpu
from jax.sharding import PartitionSpec as P

BF = jnp.bfloat16
F32 = jnp.float32
AXES = ("shard", "tp")
VMEM = pl.BlockSpec(memory_space=pltpu.VMEM)
PICK, CTX, FIRST, SECOND = 4096, 6000, 15000, 15000
SMEM = pl.BlockSpec(memory_space=pltpu.SMEM)
ANY = pl.BlockSpec(memory_space=pl.ANY)


def grant(kbytes):
    return pltpu.CompilerParams(vmem_limit_bytes=kbytes * 1000)


def group_perm(groups, step, member=lambda x, c: True, turn=lambda x, c: 0):
    pairs = []
    for g in range(groups):
        for c in range(2):
            for x in range(4):
                if member(x, c):
                    x2, c2 = step(x, c)
                    g2 = g // 4 * 4 + (g + turn(x, c)) % 4
                    pairs.append((g * 8 + c * 4 + x, g2 * 8 + c2 * 4 + x2))
    return pairs


def is_home(x, c):
    return x // 2 == c


def is_away(x, c):
    return x // 2 != c


def near(x, c):
    return (x ^ 1, x // 2) if is_home(x, c) else (x ^ 3, x // 2)


def partners(shards):
    far_z = (6, 7, 4, 5, 2, 3, 0, 1)
    steps = []
    for of_z, of_y, of_core in (
        (lambda z: z ^ 1, None, None),
        (lambda z: z ^ 2, None, None),
        (lambda z: far_z[z], None, None),
        (None, 1, None),
        (None, 3, None),
        (None, None, 1),
    ):
        pairs = []
        for i in range(shards):
            z, y, c = i // 8, i // 2 % 4, i % 2
            z = of_z(z) if of_z else z
            y = y ^ of_y if of_y else y
            c = c ^ of_core if of_core else c
            pairs.append((i, z * 8 + y * 2 + c))
        steps.append(pairs)
    return steps


def dot(a, b):
    return jnp.dot(a, b, preferred_element_type=F32)


def dot_nt(a, b):
    return lax.dot_general(a, b, (((1,), (1,)), ((), ())), preferred_element_type=F32)


def call(kernel, name, kbytes, outs, scratch, mflops, mbytes, scalars, arrays, far, out_specs=None):
    return pl.pallas_call(
        kernel,
        in_specs=[SMEM] * len(scalars) + [VMEM] * len(arrays) + [ANY] * len(far),
        out_specs=out_specs or [VMEM] * len(outs),
        out_shape=[jax.ShapeDtypeStruct(shape, dtype) for shape, dtype in outs],
        scratch_shapes=scratch,
        compiler_params=grant(kbytes),
        cost_estimate=pl.CostEstimate(
            flops=mflops << 20, bytes_accessed=mbytes << 20, transcendentals=0
        ),
        name=name,
    )(*scalars, *arrays, *far)


def pick_kernel(
    kept_ref, count_ref, emb_hbm, attr_hbm, out_hbm, table, hot_ref, out_ref, in_sems, out_sems
):
    slots, persons = kept_ref.shape
    items = table.shape[1]
    loads = [pltpu.make_async_copy(emb_hbm, table.at[0], in_sems.at[0])]
    for q in range(3):
        columns = attr_hbm.at[:, pl.ds(q * 256, 256)]
        loads.append(pltpu.make_async_copy(columns, table.at[q + 1], in_sems.at[q + 1]))
    for load in loads:
        load.start()
    live = lax.broadcasted_iota(jnp.int32, (slots, persons), 0) < count_ref[...]
    wanted = jnp.where(live, kept_ref[...], 4095)
    digits = jnp.concatenate([wanted >> 6, wanted & 63], 0).astype(F32).astype(BF)
    n = 256
    blocks = persons * slots // n
    lane = lax.broadcasted_iota(jnp.int32, (n, 2 * slots), 1)
    slot = lax.broadcasted_iota(jnp.int32, (n, 2 * slots), 0) % slots
    odd = (lax.broadcasted_iota(jnp.int32, (n, 1), 0) // slots) % 2 == 1
    unused = []
    for b in range(blocks):
        row = lax.broadcasted_iota(jnp.int32, (n, persons), 0) + b * n
        owner = (row // slots == lax.broadcasted_iota(jnp.int32, (n, persons), 1)).astype(BF)
        both = dot_nt(owner, digits)
        high = jnp.where(lane == slot, both * 64.0, 0.0)
        low = jnp.where(lane == slot + slots, both, 0.0)
        rows = jnp.sum(high + low, axis=1, keepdims=True).astype(jnp.int32)
        hot = lax.broadcasted_iota(jnp.int32, (n, items), 1) == rows
        hot_ref[b * n : (b + 1) * n] = hot.astype(BF)
        unused.append(rows >= items)
    stores = []
    for c in range(2):
        loads[2 * c].wait()
        loads[2 * c + 1].wait()
        for b in range(blocks):
            hot = hot_ref[b * n : (b + 1) * n]
            low = jnp.where(unused[b], jnp.inf, dot(hot, table[2 * c]))
            high = jnp.where(unused[b], jnp.inf, dot(hot, table[2 * c + 1]))
            first = jnp.where(odd, low, high).astype(BF)
            second = jnp.where(odd, high, low).astype(BF)
            for g in range(n // 32):
                out_ref[c, b * (n // 32) + g, :, 0:256] = first[g * 32 : (g + 1) * 32]
                out_ref[c, b * (n // 32) + g, :, 256:512] = second[g * 32 : (g + 1) * 32]
        stores.append(pltpu.make_async_copy(out_ref.at[c], out_hbm.at[:, c], out_sems.at[c]))
        stores[-1].start()
    for store in stores:
        store.wait()


def pick_rows(kept, count, emb, attr):
    slots, persons = kept.shape
    out = (persons // 4, 2, 4 * slots, 512)
    return pl.pallas_call(
        pick_kernel,
        in_specs=[VMEM, VMEM, ANY, ANY],
        out_specs=ANY,
        out_shape=jax.ShapeDtypeStruct(out, BF),
        scratch_shapes=[
            pltpu.VMEM((4, emb.shape[0], 256), BF),
            pltpu.VMEM((persons * slots, emb.shape[0]), BF),
            pltpu.VMEM((2, persons // 4, 4 * slots, 512), BF),
            pltpu.SemaphoreType.DMA((4,)),
            pltpu.SemaphoreType.DMA((2,)),
        ],
        compiler_params=grant(62500),
        cost_estimate=pl.CostEstimate(
            flops=PICK << 20, bytes_accessed=6 << 20, transcendentals=0
        ),
        name="pick_rows",
    )(kept, count, emb, attr)


ROWS = 256


def block_copies(src, dst, sems):
    copies = []
    for i in range(dst.shape[0] // ROWS):
        here = pl.ds(i * ROWS, ROWS)
        copies.append(pltpu.make_async_copy(src.at[here], dst.at[here], sems.at[i]))
        copies[-1].start()
    return copies


def context_kernel(ca_ref, cb_ref, va_ref, vb_ref, part_ref, head_ref):
    head_ref[0:256] = va_ref[0:256]
    head_ref[256:512] = vb_ref[0:256]
    for i in range(part_ref.shape[0] // ROWS):
        here = pl.ds(i * ROWS, ROWS)
        part_ref[here] = dot(ca_ref[here], va_ref[256:768]) + dot(cb_ref[here], vb_ref[256:768])


def first_kernel(
    u_ref, part_ref, head_ref, recv_hbm, pay_ref, piece_ref, logit_ref,
    clean, place, recv_ref, recv_sems,
):
    slots = recv_ref.shape[0]
    recv_copies = block_copies(recv_hbm, recv_ref, recv_sems)
    r = lax.broadcasted_iota(jnp.int32, (ROWS, ROWS), 0)
    q = lax.broadcasted_iota(jnp.int32, (ROWS, ROWS), 1)
    upper = (r <= q).astype(BF)
    lane0 = (lax.broadcasted_iota(jnp.int32, (16, 128), 1) == 0).astype(BF)
    before = jnp.zeros((16, 1), F32)
    for i in range(slots // ROWS):
        here = slice(i * ROWS, (i + 1) * ROWS)
        recv_copies[i].wait()
        got = recv_ref[here].astype(F32)
        live = got < jnp.inf
        clean[here] = jnp.where(live, got, 0.0).astype(BF)
        marks = dot_nt(lane0, live[:, 0:128].astype(F32).astype(BF))
        upto = dot(marks.astype(BF), upper) + before
        place[:, here] = jnp.where(marks > 0.5, upto - 1.0, -1.0)
        before = upto[:, ROWS - 1 : ROWS]
    for i in range(pay_ref.shape[0] // ROWS):
        here = pl.ds(i * ROWS, ROWS)
        k = (lax.broadcasted_iota(jnp.int32, (ROWS, slots), 0) + i * ROWS).astype(F32)
        hot = (k == place[0:1, :]).astype(BF)
        pay = dot(hot, clean[...]).astype(BF)
        pay_ref[here] = pay
        piece = part_ref[here] + dot(pay, head_ref[...])
        piece_ref[here] = piece.astype(BF)
        logit_ref[:, here] = dot_nt(u_ref[...], pay)


def cross(x0, hidden, offset, x):
    x0 = x0.astype(F32)
    return (x0 * (hidden + offset) + x.astype(F32)).astype(BF)


def second_kernel(
    mine_ref, other_ref, pay_ref, ba_ref, bb_ref, ca_ref, cb_ref,
    ua_ref, ub_ref, va_ref, vb_ref, xa_ref, xb_ref, piece_ref,
):
    for i in range(pay_ref.shape[0] // ROWS):
        here = pl.ds(i * ROWS, ROWS)
        proj = (mine_ref[here].astype(F32) + other_ref[here].astype(F32)).astype(BF)
        slots = (
            (xa_ref, ua_ref, ba_ref, ca_ref, 0),
            (xb_ref, ub_ref, bb_ref, cb_ref, 256),
        )
        for x_ref, u_ref, b_ref, c_ref, at in slots:
            hidden = dot(proj, u_ref[...])
            pay = pay_ref[here, at : at + 256]
            ctx = c_ref[here]
            x_ref[here, 0:256] = cross(pay, hidden[:, 0:256], b_ref[0:1, 0:256], pay)
            x_ref[here, 256:768] = cross(ctx, hidden[:, 256:768], b_ref[0:1, 256:768], ctx)
        piece = dot(xa_ref[here], va_ref[...]) + dot(xb_ref[here], vb_ref[...])
        piece_ref[here] = piece.astype(BF)


def last_kernel(
    coefficient, mine_ref, other_ref, pay_ref, xa_ref, xb_ref, sa_ref, sb_ref, logit_ref,
    ca_ref, cb_ref, ua_ref, ub_ref, score_ref,
):
    for i in range(pay_ref.shape[0] // ROWS):
        here = pl.ds(i * ROWS, ROWS)
        proj = (mine_ref[here].astype(F32) + other_ref[here].astype(F32)).astype(BF)
        score = coefficient[0] * logit_ref[:, here]
        for x_ref, u_ref, s_ref, c_ref, at in (
            (xa_ref, ua_ref, sa_ref, ca_ref, 0),
            (xb_ref, ub_ref, sb_ref, cb_ref, 256),
        ):
            hidden = dot(proj, u_ref[...])
            low = cross(
                pay_ref[here, at : at + 256], hidden[:, 0:256], s_ref[1:2, 0:256], x_ref[here, 0:256]
            )
            high = cross(
                c_ref[here], hidden[:, 256:768], s_ref[1:2, 256:768], x_ref[here, 256:768]
            )
            out = jnp.broadcast_to(s_ref[2:3, :], (16, 768)).astype(BF)
            score = score + dot_nt(out[:, 0:256], low) + dot_nt(out[:, 256:768], high)
        score_ref[:, here] = score


def on_device(
    person_embedding,
    catalog_embedding,
    catalog_attributes,
    kept_part_entries,
    valid_slot_number,
    pair_attributes,
    lowrank_v_matrix,
    lowrank_u_matrix,
    interaction_offset,
    final_projection,
    similarity_coefficient,
):
    shards = lax.axis_size("shard")
    groups = shards // 2
    x = lax.axis_index("tp")
    core = lax.axis_index("shard") % 2
    home = x // 2 == core
    parity = x % 2
    move = functools.partial(lax.ppermute, axis_name=AXES)
    to_core = group_perm(groups, lambda x, c: (x, 1 - c))
    to_near = group_perm(groups, near)
    home_on = group_perm(groups, lambda x, c: (x ^ 3, c), is_home)
    away_swap = group_perm(groups, lambda x, c: (x ^ 1, c), is_away)
    ctx_near = group_perm(groups, lambda x, c: (x ^ 1, c) if is_home(x, c) else (x ^ 3, 1 - c))
    ctx_far = group_perm(groups, lambda x, c: (x ^ 2, 1 - c), is_away)

    def stay(x, c):
        return x, c

    y_up = group_perm(groups, stay, turn=lambda x, c: 1)
    y_mixed = group_perm(groups, stay, turn=lambda x, c: -1 if is_home(x, c) else 1)
    y_down = group_perm(groups, stay, is_away, lambda x, c: -1)
    odd_y = lax.axis_index("shard") // 2 % 2
    persons, _, kept = kept_part_entries.shape
    hops = partners(shards)
    me = lax.axis_index("shard")
    v_near = move(lax.dynamic_index_in_dim(lowrank_v_matrix, odd_y, 0, False), perm=to_near)
    u_near = move(lax.dynamic_index_in_dim(lowrank_u_matrix, odd_y, 0, False), perm=to_near)
    ctx_own = lax.dynamic_index_in_dim(pair_attributes, parity, 0, False)
    ctx_away = lax.dynamic_index_in_dim(pair_attributes, 1 - parity, 0, False)
    users = jnp.broadcast_to(person_embedding[None], (shards, *person_embedding.shape))
    users = lax.all_to_all(users, "shard", split_axis=0, concat_axis=0, tiled=True)

    parcel = pick_rows(
        kept_part_entries[:, 0, :].T, valid_slot_number.T, catalog_embedding, catalog_attributes
    )
    parcel = parcel.reshape(persons * 2, kept, 512)
    parcel, v_near, u_near, users = lax.optimization_barrier((parcel, v_near, u_near, users))
    recv = lax.all_to_all(parcel, AXES, split_axis=0, concat_axis=0, tiled=True)
    recv = recv.reshape(persons * 2 * kept, 512)

    v_far = move(v_near, perm=home_on)
    u_far = move(u_near, perm=away_swap)
    v_far, ctx_out, ctx_away = lax.optimization_barrier((v_far, ctx_own, ctx_away))
    ctx_a = move(ctx_away, perm=ctx_near)
    ctx_b = move(ctx_out, perm=ctx_far)
    ctx_a, ctx_b = lax.optimization_barrier((ctx_a, ctx_b))

    all_scores = jnp.einsum(
        "ue,ie->ui", users.reshape(persons, -1), catalog_embedding, preferred_element_type=F32
    )
    best = jnp.max(all_scores, axis=1).reshape(shards, persons // shards)
    order = [[i] for i in range(shards)]
    for pairs in hops:
        order = [order[i] + order[k] for i, k in pairs]
    order = lax.dynamic_index_in_dim(jnp.asarray(order, jnp.int32), me, 0, False)
    chosen = order[:, None] == jnp.arange(shards, dtype=jnp.int32)[None, :]
    best = jnp.sum(jnp.where(chosen[:, :, None], best[None], 0.0), axis=1)

    def halve(best, pairs):
        half = best.shape[0] // 2
        return jnp.maximum(best[:half], lax.ppermute(best[half:], "shard", pairs))

    def over_x(best):
        out = best
        for flip in (1, 3, 2):
            out = jnp.maximum(out, lax.ppermute(best, "tp", [(i, i ^ flip) for i in range(4)]))
        return out

    def over_y(best):
        n = best.shape[0] // 4
        out = best[:n]
        for block, flip in ((1, 1), (2, 3), (3, 2)):
            pairs = [(i, i ^ (2 * flip)) for i in range(shards)]
            got = lax.ppermute(best[block * n : (block + 1) * n], "shard", pairs)
            out = jnp.maximum(out, got)
        return out

    best = over_y(halve(best, hops[5]))

    small = jnp.concatenate([interaction_offset, final_projection[None, :].astype(F32)], 0)
    best, v_near_on = lax.optimization_barrier((best, v_near))
    v_near_y = move(v_near_on, perm=y_up)
    v_far_y = move(v_far, perm=y_down)
    v_near_y, u_near_on = lax.optimization_barrier((v_near_y, u_near))
    u_near_y = move(u_near_on, perm=y_mixed)
    u_far_y = move(u_far, perm=y_down)
    ctx_a, best, small = lax.optimization_barrier((ctx_a, best, small))
    best = halve(best, hops[2])
    small_a = move(small, perm=to_near)
    small_b = move(small, perm=ctx_far)
    even = odd_y == 0
    v0_a = jnp.where(even, v_near, v_near_y)
    v1_a = jnp.where(even, v_near_y, v_near)
    u0_a = jnp.where(even, u_near, u_near_y)
    u1_a = jnp.where(even, u_near_y, u_near)
    v0_b = jnp.where(home, lowrank_v_matrix[0], jnp.where(even, v_far, v_far_y))
    v1_b = jnp.where(home, lowrank_v_matrix[1], jnp.where(even, v_far_y, v_far))
    u0_b = jnp.where(home, lowrank_u_matrix[0], jnp.where(even, u_far, u_far_y))
    u1_b = jnp.where(home, lowrank_u_matrix[1], jnp.where(even, u_far_y, u_far))
    ctx_b = jnp.where(home, ctx_own, ctx_b)
    ctx_a, u0_a, u0_b, u1_a, u1_b = lax.optimization_barrier((ctx_a, u0_a, u0_b, u1_a, u1_b))

    emb_other = lax.dynamic_index_in_dim(users, me ^ 1, 0, False)
    query = lax.dynamic_slice_in_dim(jnp.where(home, person_embedding, emb_other), parity, 1, 0)
    query = jnp.where(core == 0, query, jnp.zeros_like(query))
    zero = jnp.zeros_like(query)
    query = jnp.where(
        parity == 1, jnp.concatenate([query, zero], 1), jnp.concatenate([zero, query], 1)
    )
    query = jnp.broadcast_to(query, (16, 512))

    surv = pair_attributes.shape[1]
    tall, wide, lanes = ((surv, 512), BF), ((surv, 768), BF), ((16, surv), F32)
    part, head = call(
        context_kernel, "context_part", 24000, [((surv, 512), F32), ((512, 512), BF)], [],
        CTX, 8, [], [ctx_a, ctx_b, v0_a, v0_b], [],
    )
    recv, best = lax.optimization_barrier((recv, best))
    step = halve(best, hops[1])
    pay, piece, logit = call(
        first_kernel, "first_layer", 24000, [tall, tall, lanes],
        [pltpu.VMEM(recv.shape, BF), pltpu.VMEM((16, recv.shape[0]), F32)]
        + [pltpu.VMEM(recv.shape, BF), pltpu.SemaphoreType.DMA((recv.shape[0] // ROWS,))],
        FIRST, 8, [], [query, part, head], [recv],
    )
    piece, best, small_a, small_b = lax.optimization_barrier((piece, step, small_a, small_b))
    small_b = jnp.where(home, small, small_b)
    other, best = lax.optimization_barrier((move(piece, perm=to_core), halve(best, hops[0])))
    step = over_x(best)
    x_a, x_b, piece1 = call(
        second_kernel, "second_layer", 24000, [wide, wide, tall], [],
        SECOND, 12, [],
        [piece, other, pay, small_a, small_b, ctx_a, ctx_b, u0_a, u0_b, v1_a, v1_b], [],
    )
    piece1, best = lax.optimization_barrier((piece1, step))
    other1 = move(piece1, perm=to_core)
    (score,) = call(
        last_kernel, "last_layer", 24000, [lanes], [], 1792, 10, [similarity_coefficient],
        [piece1, other1, pay, x_a, x_b, small_a, small_b, logit, ctx_a, ctx_b, u1_a, u1_b], [],
    )
    top = jnp.where(home, lax.dynamic_slice_in_dim(best, parity, 1, 1), 0.0)
    score = score[0:1] - similarity_coefficient[0] * top
    score = score + move(score, perm=to_core)
    score_a = move(score, perm=to_near)
    score_b = jnp.where(home, score, move(score, perm=ctx_far))
    return jnp.where(
        parity == 1,
        jnp.concatenate([score_a, score_b], 0),
        jnp.concatenate([score_b, score_a], 0),
    )


def solution(mesh):
    return jax.shard_map(
        on_device,
        mesh=mesh,
        in_specs=(
            P("shard", None),
            P(("shard", "tp"), None),
            P(("shard", "tp"), None),
            P(None, ("shard", "tp"), None),
            P(None, ("shard", "tp")),
            P("shard", None, "tp"),
            P(None, "tp", None),
            P(None, None, "tp"),
            P(None, "tp"),
            P("tp"),
            P(),
        ),
        out_specs=P("shard", None),
        check_vma=False,
    )
```

```python
import functools

import jax
import jax.numpy as jnp
from jax import lax
from jax.experimental import pallas as pl
from jax.experimental.pallas import tpu as pltpu
from jax.sharding import PartitionSpec as P

BF = jnp.bfloat16
F32 = jnp.float32
AXES = ("shard", "tp")
VMEM = pl.BlockSpec(memory_space=pltpu.VMEM)
PICK, CTX, FIRST, SECOND = 4096, 6000, 15000, 15000
SMEM = pl.BlockSpec(memory_space=pltpu.SMEM)
ANY = pl.BlockSpec(memory_space=pl.ANY)


def grant(kbytes):
    return pltpu.CompilerParams(vmem_limit_bytes=kbytes * 1000)


def group_perm(groups, step, member=lambda x, c: True, turn=lambda x, c: 0):
    pairs = []
    for g in range(groups):
        for c in range(2):
            for x in range(4):
                if member(x, c):
                    x2, c2 = step(x, c)
                    g2 = g // 4 * 4 + (g + turn(x, c)) % 4
                    pairs.append((g * 8 + c * 4 + x, g2 * 8 + c2 * 4 + x2))
    return pairs


def is_home(x, c):
    return x // 2 == c


def is_away(x, c):
    return x // 2 != c


def near(x, c):
    return (x ^ 1, x // 2) if is_home(x, c) else (x ^ 3, x // 2)


def partners(shards):
    far_z = (6, 7, 4, 5, 2, 3, 0, 1)
    steps = []
    for of_z, of_y, of_core in (
        (lambda z: z ^ 1, None, None),
        (lambda z: z ^ 2, None, None),
        (lambda z: far_z[z], None, None),
        (None, 1, None),
        (None, 3, None),
        (None, None, 1),
    ):
        pairs = []
        for i in range(shards):
            z, y, c = i // 8, i // 2 % 4, i % 2
            z = of_z(z) if of_z else z
            y = y ^ of_y if of_y else y
            c = c ^ of_core if of_core else c
            pairs.append((i, z * 8 + y * 2 + c))
        steps.append(pairs)
    return steps


def dot(a, b):
    return jnp.dot(a, b, preferred_element_type=F32)


def dot_nt(a, b):
    return lax.dot_general(a, b, (((1,), (1,)), ((), ())), preferred_element_type=F32)


def call(kernel, name, kbytes, outs, scratch, mflops, mbytes, scalars, arrays, far, out_specs=None):
    return pl.pallas_call(
        kernel,
        in_specs=[SMEM] * len(scalars) + [VMEM] * len(arrays) + [ANY] * len(far),
        out_specs=out_specs or [VMEM] * len(outs),
        out_shape=[jax.ShapeDtypeStruct(shape, dtype) for shape, dtype in outs],
        scratch_shapes=scratch,
        compiler_params=grant(kbytes),
        cost_estimate=pl.CostEstimate(
            flops=mflops << 20, bytes_accessed=mbytes << 20, transcendentals=0
        ),
        name=name,
    )(*scalars, *arrays, *far)


def pick_kernel(
    kept_ref, count_ref, emb_hbm, attr_hbm, out_hbm, table, hot_ref, out_ref, in_sems, out_sems
):
    slots, persons = kept_ref.shape
    items = table.shape[1]
    loads = [pltpu.make_async_copy(emb_hbm, table.at[0], in_sems.at[0])]
    for q in range(3):
        columns = attr_hbm.at[:, pl.ds(q * 256, 256)]
        loads.append(pltpu.make_async_copy(columns, table.at[q + 1], in_sems.at[q + 1]))
    for load in loads:
        load.start()
    live = lax.broadcasted_iota(jnp.int32, (slots, persons), 0) < count_ref[...]
    wanted = jnp.where(live, kept_ref[...], 4095)
    digits = jnp.concatenate([wanted >> 6, wanted & 63], 0).astype(F32).astype(BF)
    n = 256
    blocks = persons * slots // n
    lane = lax.broadcasted_iota(jnp.int32, (n, 2 * slots), 1)
    slot = lax.broadcasted_iota(jnp.int32, (n, 2 * slots), 0) % slots
    odd = (lax.broadcasted_iota(jnp.int32, (n, 1), 0) // slots) % 2 == 1
    unused = []
    for b in range(blocks):
        row = lax.broadcasted_iota(jnp.int32, (n, persons), 0) + b * n
        owner = (row // slots == lax.broadcasted_iota(jnp.int32, (n, persons), 1)).astype(BF)
        both = dot_nt(owner, digits)
        high = jnp.where(lane == slot, both * 64.0, 0.0)
        low = jnp.where(lane == slot + slots, both, 0.0)
        rows = jnp.sum(high + low, axis=1, keepdims=True).astype(jnp.int32)
        hot = lax.broadcasted_iota(jnp.int32, (n, items), 1) == rows
        hot_ref[b * n : (b + 1) * n] = hot.astype(BF)
        unused.append(rows >= items)
    stores = []
    for c in range(2):
        loads[2 * c].wait()
        loads[2 * c + 1].wait()
        for b in range(blocks):
            hot = hot_ref[b * n : (b + 1) * n]
            low = jnp.where(unused[b], jnp.inf, dot(hot, table[2 * c]))
            high = jnp.where(unused[b], jnp.inf, dot(hot, table[2 * c + 1]))
            first = jnp.where(odd, low, high).astype(BF)
            second = jnp.where(odd, high, low).astype(BF)
            for g in range(n // 32):
                out_ref[c, b * (n // 32) + g, :, 0:256] = first[g * 32 : (g + 1) * 32]
                out_ref[c, b * (n // 32) + g, :, 256:512] = second[g * 32 : (g + 1) * 32]
        stores.append(pltpu.make_async_copy(out_ref.at[c], out_hbm.at[:, c], out_sems.at[c]))
        stores[-1].start()
    for store in stores:
        store.wait()


def pick_rows(kept, count, emb, attr):
    slots, persons = kept.shape
    out = (persons // 4, 2, 4 * slots, 512)
    return pl.pallas_call(
        pick_kernel,
        in_specs=[VMEM, VMEM, ANY, ANY],
        out_specs=ANY,
        out_shape=jax.ShapeDtypeStruct(out, BF),
        scratch_shapes=[
            pltpu.VMEM((4, emb.shape[0], 256), BF),
            pltpu.VMEM((persons * slots, emb.shape[0]), BF),
            pltpu.VMEM((2, persons // 4, 4 * slots, 512), BF),
            pltpu.SemaphoreType.DMA((4,)),
            pltpu.SemaphoreType.DMA((2,)),
        ],
        compiler_params=grant(62500),
        cost_estimate=pl.CostEstimate(
            flops=PICK << 20, bytes_accessed=6 << 20, transcendentals=0
        ),
        name="pick_rows",
    )(kept, count, emb, attr)


ROWS = 256


def block_copies(src, dst, sems):
    copies = []
    for i in range(dst.shape[0] // ROWS):
        here = pl.ds(i * ROWS, ROWS)
        copies.append(pltpu.make_async_copy(src.at[here], dst.at[here], sems.at[i]))
        copies[-1].start()
    return copies


def context_kernel(ca_ref, cb_ref, va_ref, vb_ref, part_ref, head_ref):
    head_ref[0:256] = va_ref[0:256]
    head_ref[256:512] = vb_ref[0:256]
    for i in range(part_ref.shape[0] // ROWS):
        here = pl.ds(i * ROWS, ROWS)
        part_ref[here] = dot(ca_ref[here], va_ref[256:768]) + dot(cb_ref[here], vb_ref[256:768])


def first_kernel(
    u_ref, part_ref, head_ref, recv_hbm, pay_ref, piece_ref, logit_ref,
    clean, place, recv_ref, recv_sems,
):
    slots = recv_ref.shape[0]
    recv_copies = block_copies(recv_hbm, recv_ref, recv_sems)
    r = lax.broadcasted_iota(jnp.int32, (ROWS, ROWS), 0)
    q = lax.broadcasted_iota(jnp.int32, (ROWS, ROWS), 1)
    upper = (r <= q).astype(BF)
    lane0 = (lax.broadcasted_iota(jnp.int32, (16, 128), 1) == 0).astype(BF)
    before = jnp.zeros((16, 1), F32)
    for i in range(slots // ROWS):
        here = slice(i * ROWS, (i + 1) * ROWS)
        recv_copies[i].wait()
        got = recv_ref[here].astype(F32)
        live = got < jnp.inf
        clean[here] = jnp.where(live, got, 0.0).astype(BF)
        marks = dot_nt(lane0, live[:, 0:128].astype(F32).astype(BF))
        upto = dot(marks.astype(BF), upper) + before
        place[:, here] = jnp.where(marks > 0.5, upto - 1.0, -1.0)
        before = upto[:, ROWS - 1 : ROWS]
    for i in range(pay_ref.shape[0] // ROWS):
        here = pl.ds(i * ROWS, ROWS)
        k = (lax.broadcasted_iota(jnp.int32, (ROWS, slots), 0) + i * ROWS).astype(F32)
        hot = (k == place[0:1, :]).astype(BF)
        pay = dot(hot, clean[...]).astype(BF)
        pay_ref[here] = pay
        piece = part_ref[here] + dot(pay, head_ref[...])
        piece_ref[here] = piece.astype(BF)
        logit_ref[:, here] = dot_nt(u_ref[...], pay)


def cross(x0, hidden, offset, x):
    x0 = x0.astype(F32)
    return (x0 * (hidden + offset) + x.astype(F32)).astype(BF)


def second_kernel(
    mine_ref, other_ref, pay_ref, ba_ref, bb_ref, ca_ref, cb_ref,
    ua_ref, ub_ref, va_ref, vb_ref, xa_ref, xb_ref, piece_ref,
):
    for i in range(pay_ref.shape[0] // ROWS):
        here = pl.ds(i * ROWS, ROWS)
        proj = (mine_ref[here].astype(F32) + other_ref[here].astype(F32)).astype(BF)
        slots = (
            (xa_ref, ua_ref, ba_ref, ca_ref, 0),
            (xb_ref, ub_ref, bb_ref, cb_ref, 256),
        )
        for x_ref, u_ref, b_ref, c_ref, at in slots:
            hidden = dot(proj, u_ref[...])
            pay = pay_ref[here, at : at + 256]
            ctx = c_ref[here]
            x_ref[here, 0:256] = cross(pay, hidden[:, 0:256], b_ref[0:1, 0:256], pay)
            x_ref[here, 256:768] = cross(ctx, hidden[:, 256:768], b_ref[0:1, 256:768], ctx)
        piece = dot(xa_ref[here], va_ref[...]) + dot(xb_ref[here], vb_ref[...])
        piece_ref[here] = piece.astype(BF)


def last_kernel(
    coefficient, mine_ref, other_ref, pay_ref, xa_ref, xb_ref, sa_ref, sb_ref, logit_ref,
    ca_ref, cb_ref, ua_ref, ub_ref, score_ref,
):
    for i in range(pay_ref.shape[0] // ROWS):
        here = pl.ds(i * ROWS, ROWS)
        proj = (mine_ref[here].astype(F32) + other_ref[here].astype(F32)).astype(BF)
        score = coefficient[0] * logit_ref[:, here]
        for x_ref, u_ref, s_ref, c_ref, at in (
            (xa_ref, ua_ref, sa_ref, ca_ref, 0),
            (xb_ref, ub_ref, sb_ref, cb_ref, 256),
        ):
            hidden = dot(proj, u_ref[...])
            low = cross(
                pay_ref[here, at : at + 256], hidden[:, 0:256], s_ref[1:2, 0:256], x_ref[here, 0:256]
            )
            high = cross(
                c_ref[here], hidden[:, 256:768], s_ref[1:2, 256:768], x_ref[here, 256:768]
            )
            out = jnp.broadcast_to(s_ref[2:3, :], (16, 768)).astype(BF)
            score = score + dot_nt(out[:, 0:256], low) + dot_nt(out[:, 256:768], high)
        score_ref[:, here] = score


def on_device(
    person_embedding,
    catalog_embedding,
    catalog_attributes,
    kept_part_entries,
    valid_slot_number,
    pair_attributes,
    lowrank_v_matrix,
    lowrank_u_matrix,
    interaction_offset,
    final_projection,
    similarity_coefficient,
):
    shards = lax.axis_size("shard")
    groups = shards // 2
    x = lax.axis_index("tp")
    core = lax.axis_index("shard") % 2
    home = x // 2 == core
    parity = x % 2
    move = functools.partial(lax.ppermute, axis_name=AXES)
    to_core = group_perm(groups, lambda x, c: (x, 1 - c))
    to_near = group_perm(groups, near)
    home_on = group_perm(groups, lambda x, c: (x ^ 3, c), is_home)
    away_swap = group_perm(groups, lambda x, c: (x ^ 1, c), is_away)
    ctx_near = group_perm(groups, lambda x, c: (x ^ 1, c) if is_home(x, c) else (x ^ 3, 1 - c))
    ctx_far = group_perm(groups, lambda x, c: (x ^ 2, 1 - c), is_away)

    def stay(x, c):
        return x, c

    y_split = group_perm(groups, stay, turn=lambda x, c: -1 if is_home(x, c) else 1)
    y_mirror = group_perm(groups, stay, turn=lambda x, c: 1 if is_home(x, c) else -1)
    y_up = group_perm(groups, stay, is_away, lambda x, c: 1)
    y_down = group_perm(groups, stay, is_away, lambda x, c: -1)
    odd_y = lax.axis_index("shard") // 2 % 2
    persons, _, kept = kept_part_entries.shape
    hops = partners(shards)
    me = lax.axis_index("shard")
    v_near = move(lax.dynamic_index_in_dim(lowrank_v_matrix, odd_y, 0, False), perm=to_near)
    u_near = move(lax.dynamic_index_in_dim(lowrank_u_matrix, odd_y, 0, False), perm=to_near)
    ctx_own = lax.dynamic_index_in_dim(pair_attributes, parity, 0, False)
    ctx_away = lax.dynamic_index_in_dim(pair_attributes, 1 - parity, 0, False)
    users = jnp.broadcast_to(person_embedding[None], (shards, *person_embedding.shape))
    users = lax.all_to_all(users, "shard", split_axis=0, concat_axis=0, tiled=True)

    parcel = pick_rows(
        kept_part_entries[:, 0, :].T, valid_slot_number.T, catalog_embedding, catalog_attributes
    )
    parcel = parcel.reshape(persons * 2, kept, 512)
    parcel, v_near, u_near, users = lax.optimization_barrier((parcel, v_near, u_near, users))
    recv = lax.all_to_all(parcel, AXES, split_axis=0, concat_axis=0, tiled=True)
    recv = recv.reshape(persons * 2 * kept, 512)

    v_far = move(v_near, perm=home_on)
    u_far = move(u_near, perm=away_swap)

    all_scores = jnp.einsum(
        "ue,ie->ui", users.reshape(persons, -1), catalog_embedding, preferred_element_type=F32
    )
    best = jnp.max(all_scores, axis=1).reshape(shards, persons // shards)
    order = [[i] for i in range(shards)]
    for pairs in hops:
        order = [order[i] + order[k] for i, k in pairs]
    order = lax.dynamic_index_in_dim(jnp.asarray(order, jnp.int32), me, 0, False)
    chosen = order[:, None] == jnp.arange(shards, dtype=jnp.int32)[None, :]
    best = jnp.sum(jnp.where(chosen[:, :, None], best[None], 0.0), axis=1)

    def halve(best, pairs):
        half = best.shape[0] // 2
        return jnp.maximum(best[:half], lax.ppermute(best[half:], "shard", pairs))

    def over_x(best):
        out = best
        for flip in (1, 3, 2):
            out = jnp.maximum(out, lax.ppermute(best, "tp", [(i, i ^ flip) for i in range(4)]))
        return out

    def over_y(best):
        n = best.shape[0] // 4
        out = best[:n]
        for block, flip in ((1, 1), (2, 3), (3, 2)):
            pairs = [(i, i ^ (2 * flip)) for i in range(shards)]
            got = lax.ppermute(best[block * n : (block + 1) * n], "shard", pairs)
            out = jnp.maximum(out, got)
        return out

    best = over_y(halve(best, hops[5]))

    small = jnp.concatenate([interaction_offset, final_projection[None, :].astype(F32)], 0)
    best, v_near_on, ctx_out, ctx_away = lax.optimization_barrier(
        (best, v_near, ctx_own, ctx_away)
    )
    ctx_a = move(ctx_away, perm=ctx_near)
    ctx_b = move(ctx_out, perm=ctx_far)
    ctx_a, ctx_b = lax.optimization_barrier((ctx_a, ctx_b))
    v_near_y = move(v_near_on, perm=y_split)
    v_far_y = move(v_far, perm=y_down)
    v_near_y, u_near_on = lax.optimization_barrier((v_near_y, u_near))
    u_near_y = move(u_near_on, perm=y_mirror)
    u_far_y = move(u_far, perm=y_up)
    ctx_b = jnp.where(home, ctx_own, ctx_b)
    even = odd_y == 0
    v0_a = jnp.where(even, v_near, v_near_y)
    v1_a = jnp.where(even, v_near_y, v_near)
    u0_a = jnp.where(even, u_near, u_near_y)
    u1_a = jnp.where(even, u_near_y, u_near)
    v0_b = jnp.where(home, lowrank_v_matrix[0], jnp.where(even, v_far, v_far_y))
    v1_b = jnp.where(home, lowrank_v_matrix[1], jnp.where(even, v_far_y, v_far))
    u0_b = jnp.where(home, lowrank_u_matrix[0], jnp.where(even, u_far, u_far_y))
    u1_b = jnp.where(home, lowrank_u_matrix[1], jnp.where(even, u_far_y, u_far))
    ctx_a, u0_a, u0_b, u1_a, u1_b, best, small = lax.optimization_barrier(
        (ctx_a, u0_a, u0_b, u1_a, u1_b, best, small)
    )
    best = halve(best, hops[2])
    small_a = move(small, perm=to_near)
    small_b = move(small, perm=ctx_far)

    emb_other = lax.dynamic_index_in_dim(users, me ^ 1, 0, False)
    query = lax.dynamic_slice_in_dim(jnp.where(home, person_embedding, emb_other), parity, 1, 0)
    query = jnp.where(core == 0, query, jnp.zeros_like(query))
    zero = jnp.zeros_like(query)
    query = jnp.where(
        parity == 1, jnp.concatenate([query, zero], 1), jnp.concatenate([zero, query], 1)
    )
    query = jnp.broadcast_to(query, (16, 512))

    surv = pair_attributes.shape[1]
    tall, wide, lanes = ((surv, 512), BF), ((surv, 768), BF), ((16, surv), F32)
    part, head = call(
        context_kernel, "context_part", 24000, [((surv, 512), F32), ((512, 512), BF)], [],
        CTX, 8, [], [ctx_a, ctx_b, v0_a, v0_b], [],
    )
    recv, best = lax.optimization_barrier((recv, best))
    step = halve(best, hops[1])
    pay, piece, logit = call(
        first_kernel, "first_layer", 24000, [tall, tall, lanes],
        [pltpu.VMEM(recv.shape, BF), pltpu.VMEM((16, recv.shape[0]), F32)]
        + [pltpu.VMEM(recv.shape, BF), pltpu.SemaphoreType.DMA((recv.shape[0] // ROWS,))],
        FIRST, 8, [], [query, part, head], [recv],
    )
    piece, best, small_a, small_b = lax.optimization_barrier((piece, step, small_a, small_b))
    small_b = jnp.where(home, small, small_b)
    other, best = lax.optimization_barrier((move(piece, perm=to_core), halve(best, hops[0])))
    step = over_x(best)
    x_a, x_b, piece1 = call(
        second_kernel, "second_layer", 24000, [wide, wide, tall], [],
        SECOND, 12, [],
        [piece, other, pay, small_a, small_b, ctx_a, ctx_b, u0_a, u0_b, v1_a, v1_b], [],
    )
    piece1, best = lax.optimization_barrier((piece1, step))
    other1 = move(piece1, perm=to_core)
    (score,) = call(
        last_kernel, "last_layer", 24000, [lanes], [], 1792, 10, [similarity_coefficient],
        [piece1, other1, pay, x_a, x_b, small_a, small_b, logit, ctx_a, ctx_b, u1_a, u1_b], [],
    )
    top = jnp.where(home, lax.dynamic_slice_in_dim(best, parity, 1, 1), 0.0)
    score = score[0:1] - similarity_coefficient[0] * top
    score = score + move(score, perm=to_core)
    score_a = move(score, perm=to_near)
    score_b = jnp.where(home, score, move(score, perm=ctx_far))
    return jnp.where(
        parity == 1,
        jnp.concatenate([score_a, score_b], 0),
        jnp.concatenate([score_b, score_a], 0),
    )


def solution(mesh):
    return jax.shard_map(
        on_device,
        mesh=mesh,
        in_specs=(
            P("shard", None),
            P(("shard", "tp"), None),
            P(("shard", "tp"), None),
            P(None, ("shard", "tp"), None),
            P(None, ("shard", "tp")),
            P("shard", None, "tp"),
            P(None, "tp", None),
            P(None, None, "tp"),
            P(None, "tp"),
            P("tp"),
            P(),
        ),
        out_specs=P("shard", None),
        check_vma=False,
    )
```

```python
import functools

import jax
import jax.numpy as jnp
from jax import lax
from jax.experimental import pallas as pl
from jax.experimental.pallas import tpu as pltpu
from jax.sharding import PartitionSpec as P

BF = jnp.bfloat16
F32 = jnp.float32
AXES = ("shard", "tp")
VMEM = pl.BlockSpec(memory_space=pltpu.VMEM)
PICK, CTX, FIRST, SECOND = 4096, 11000, 15000, 15000
SMEM = pl.BlockSpec(memory_space=pltpu.SMEM)
ANY = pl.BlockSpec(memory_space=pl.ANY)


def grant(kbytes):
    return pltpu.CompilerParams(vmem_limit_bytes=kbytes * 1000)


def group_perm(groups, step, member=lambda x, c: True, turn=lambda x, c: 0):
    pairs = []
    for g in range(groups):
        for c in range(2):
            for x in range(4):
                if member(x, c):
                    x2, c2 = step(x, c)
                    g2 = g // 4 * 4 + (g + turn(x, c)) % 4
                    pairs.append((g * 8 + c * 4 + x, g2 * 8 + c2 * 4 + x2))
    return pairs


def is_home(x, c):
    return x // 2 == c


def is_away(x, c):
    return x // 2 != c


def near(x, c):
    return (x ^ 1, x // 2) if is_home(x, c) else (x ^ 3, x // 2)


def partners(shards):
    far_z = (6, 7, 4, 5, 2, 3, 0, 1)
    steps = []
    for of_z, of_y, of_core in (
        (lambda z: z ^ 1, None, None),
        (lambda z: z ^ 2, None, None),
        (lambda z: far_z[z], None, None),
        (None, 1, None),
        (None, 3, None),
        (None, None, 1),
    ):
        pairs = []
        for i in range(shards):
            z, y, c = i // 8, i // 2 % 4, i % 2
            z = of_z(z) if of_z else z
            y = y ^ of_y if of_y else y
            c = c ^ of_core if of_core else c
            pairs.append((i, z * 8 + y * 2 + c))
        steps.append(pairs)
    return steps


def dot(a, b):
    return jnp.dot(a, b, preferred_element_type=F32)


def dot_nt(a, b):
    return lax.dot_general(a, b, (((1,), (1,)), ((), ())), preferred_element_type=F32)


def call(kernel, name, kbytes, outs, scratch, mflops, mbytes, scalars, arrays, far, out_specs=None):
    return pl.pallas_call(
        kernel,
        in_specs=[SMEM] * len(scalars) + [VMEM] * len(arrays) + [ANY] * len(far),
        out_specs=out_specs or [VMEM] * len(outs),
        out_shape=[jax.ShapeDtypeStruct(shape, dtype) for shape, dtype in outs],
        scratch_shapes=scratch,
        compiler_params=grant(kbytes),
        cost_estimate=pl.CostEstimate(
            flops=mflops << 20, bytes_accessed=mbytes << 20, transcendentals=0
        ),
        name=name,
    )(*scalars, *arrays, *far)


def pick_kernel(
    kept_ref, count_ref, emb_hbm, attr_hbm, out_hbm, table, hot_ref, out_ref, in_sems, out_sems
):
    slots, persons = kept_ref.shape
    items = table.shape[1]
    loads = [pltpu.make_async_copy(emb_hbm, table.at[0], in_sems.at[0])]
    for q in range(3):
        columns = attr_hbm.at[:, pl.ds(q * 256, 256)]
        loads.append(pltpu.make_async_copy(columns, table.at[q + 1], in_sems.at[q + 1]))
    for load in loads:
        load.start()
    live = lax.broadcasted_iota(jnp.int32, (slots, persons), 0) < count_ref[...]
    wanted = jnp.where(live, kept_ref[...], 4095)
    digits = jnp.concatenate([wanted >> 6, wanted & 63], 0).astype(F32).astype(BF)
    n = 256
    blocks = persons * slots // n
    lane = lax.broadcasted_iota(jnp.int32, (n, 2 * slots), 1)
    slot = lax.broadcasted_iota(jnp.int32, (n, 2 * slots), 0) % slots
    odd = (lax.broadcasted_iota(jnp.int32, (n, 1), 0) // slots) % 2 == 1
    unused = []
    for b in range(blocks):
        row = lax.broadcasted_iota(jnp.int32, (n, persons), 0) + b * n
        owner = (row // slots == lax.broadcasted_iota(jnp.int32, (n, persons), 1)).astype(BF)
        both = dot_nt(owner, digits)
        high = jnp.where(lane == slot, both * 64.0, 0.0)
        low = jnp.where(lane == slot + slots, both, 0.0)
        rows = jnp.sum(high + low, axis=1, keepdims=True).astype(jnp.int32)
        hot = lax.broadcasted_iota(jnp.int32, (n, items), 1) == rows
        hot_ref[b * n : (b + 1) * n] = hot.astype(BF)
        unused.append(rows >= items)
    stores = []
    for c in range(2):
        loads[2 * c].wait()
        loads[2 * c + 1].wait()
        for b in range(blocks):
            hot = hot_ref[b * n : (b + 1) * n]
            low = jnp.where(unused[b], jnp.inf, dot(hot, table[2 * c]))
            high = jnp.where(unused[b], jnp.inf, dot(hot, table[2 * c + 1]))
            first = jnp.where(odd, low, high).astype(BF)
            second = jnp.where(odd, high, low).astype(BF)
            for g in range(n // 32):
                out_ref[c, b * (n // 32) + g, :, 0:256] = first[g * 32 : (g + 1) * 32]
                out_ref[c, b * (n // 32) + g, :, 256:512] = second[g * 32 : (g + 1) * 32]
        stores.append(pltpu.make_async_copy(out_ref.at[c], out_hbm.at[:, c], out_sems.at[c]))
        stores[-1].start()
    for store in stores:
        store.wait()


def pick_rows(kept, count, emb, attr):
    slots, persons = kept.shape
    out = (persons // 4, 2, 4 * slots, 512)
    return pl.pallas_call(
        pick_kernel,
        in_specs=[VMEM, VMEM, ANY, ANY],
        out_specs=ANY,
        out_shape=jax.ShapeDtypeStruct(out, BF),
        scratch_shapes=[
            pltpu.VMEM((4, emb.shape[0], 256), BF),
            pltpu.VMEM((persons * slots, emb.shape[0]), BF),
            pltpu.VMEM((2, persons // 4, 4 * slots, 512), BF),
            pltpu.SemaphoreType.DMA((4,)),
            pltpu.SemaphoreType.DMA((2,)),
        ],
        compiler_params=grant(62500),
        cost_estimate=pl.CostEstimate(
            flops=PICK << 20, bytes_accessed=6 << 20, transcendentals=0
        ),
        name="pick_rows",
    )(kept, count, emb, attr)


ROWS = 256


def block_copies(src, dst, sems):
    copies = []
    for i in range(dst.shape[0] // ROWS):
        here = pl.ds(i * ROWS, ROWS)
        copies.append(pltpu.make_async_copy(src.at[here], dst.at[here], sems.at[i]))
        copies[-1].start()
    return copies


def context_kernel(ca_ref, cb_ref, va_ref, vb_ref, part_ref, head_ref):
    head_ref[0:256] = va_ref[0:256]
    head_ref[256:512] = vb_ref[0:256]
    for i in range(part_ref.shape[0] // ROWS):
        here = pl.ds(i * ROWS, ROWS)
        part_ref[here] = dot(ca_ref[here], va_ref[256:768]) + dot(cb_ref[here], vb_ref[256:768])


def first_kernel(
    u_ref, part_ref, head_ref, recv_hbm, pay_ref, piece_ref, logit_ref,
    clean, place, recv_ref, recv_sems,
):
    slots = recv_ref.shape[0]
    recv_copies = block_copies(recv_hbm, recv_ref, recv_sems)
    r = lax.broadcasted_iota(jnp.int32, (ROWS, ROWS), 0)
    q = lax.broadcasted_iota(jnp.int32, (ROWS, ROWS), 1)
    upper = (r <= q).astype(BF)
    lane0 = (lax.broadcasted_iota(jnp.int32, (16, 128), 1) == 0).astype(BF)
    before = jnp.zeros((16, 1), F32)
    for i in range(slots // ROWS):
        here = slice(i * ROWS, (i + 1) * ROWS)
        recv_copies[i].wait()
        got = recv_ref[here].astype(F32)
        live = got < jnp.inf
        clean[here] = jnp.where(live, got, 0.0).astype(BF)
        marks = dot_nt(lane0, live[:, 0:128].astype(F32).astype(BF))
        upto = dot(marks.astype(BF), upper) + before
        place[:, here] = jnp.where(marks > 0.5, upto - 1.0, -1.0)
        before = upto[:, ROWS - 1 : ROWS]
    for i in range(pay_ref.shape[0] // ROWS):
        here = pl.ds(i * ROWS, ROWS)
        k = (lax.broadcasted_iota(jnp.int32, (ROWS, slots), 0) + i * ROWS).astype(F32)
        hot = (k == place[0:1, :]).astype(BF)
        pay = dot(hot, clean[...]).astype(BF)
        pay_ref[here] = pay
        piece = part_ref[here] + dot(pay, head_ref[...])
        piece_ref[here] = piece.astype(BF)
        logit_ref[:, here] = dot_nt(u_ref[...], pay)


def cross(x0, hidden, offset, x):
    x0 = x0.astype(F32)
    return (x0 * (hidden + offset) + x.astype(F32)).astype(BF)


def second_kernel(
    mine_ref, other_ref, pay_ref, ba_ref, bb_ref, ca_ref, cb_ref,
    ua_ref, ub_ref, va_ref, vb_ref, xa_ref, xb_ref, piece_ref,
):
    for i in range(pay_ref.shape[0] // ROWS):
        here = pl.ds(i * ROWS, ROWS)
        proj = (mine_ref[here].astype(F32) + other_ref[here].astype(F32)).astype(BF)
        slots = (
            (xa_ref, ua_ref, ba_ref, ca_ref, 0),
            (xb_ref, ub_ref, bb_ref, cb_ref, 256),
        )
        for x_ref, u_ref, b_ref, c_ref, at in slots:
            hidden = dot(proj, u_ref[...])
            pay = pay_ref[here, at : at + 256]
            ctx = c_ref[here]
            x_ref[here, 0:256] = cross(pay, hidden[:, 0:256], b_ref[0:1, 0:256], pay)
            x_ref[here, 256:768] = cross(ctx, hidden[:, 256:768], b_ref[0:1, 256:768], ctx)
        piece = dot(xa_ref[here], va_ref[...]) + dot(xb_ref[here], vb_ref[...])
        piece_ref[here] = piece.astype(BF)


def last_kernel(
    coefficient, mine_ref, other_ref, pay_ref, xa_ref, xb_ref, sa_ref, sb_ref, logit_ref,
    ca_ref, cb_ref, ua_ref, ub_ref, score_ref,
):
    for i in range(pay_ref.shape[0] // ROWS):
        here = pl.ds(i * ROWS, ROWS)
        proj = (mine_ref[here].astype(F32) + other_ref[here].astype(F32)).astype(BF)
        score = coefficient[0] * logit_ref[:, here]
        for x_ref, u_ref, s_ref, c_ref, at in (
            (xa_ref, ua_ref, sa_ref, ca_ref, 0),
            (xb_ref, ub_ref, sb_ref, cb_ref, 256),
        ):
            hidden = dot(proj, u_ref[...])
            low = cross(
                pay_ref[here, at : at + 256], hidden[:, 0:256], s_ref[1:2, 0:256], x_ref[here, 0:256]
            )
            high = cross(
                c_ref[here], hidden[:, 256:768], s_ref[1:2, 256:768], x_ref[here, 256:768]
            )
            out = jnp.broadcast_to(s_ref[2:3, :], (16, 768)).astype(BF)
            score = score + dot_nt(out[:, 0:256], low) + dot_nt(out[:, 256:768], high)
        score_ref[:, here] = score


def on_device(
    person_embedding,
    catalog_embedding,
    catalog_attributes,
    kept_part_entries,
    valid_slot_number,
    pair_attributes,
    lowrank_v_matrix,
    lowrank_u_matrix,
    interaction_offset,
    final_projection,
    similarity_coefficient,
):
    shards = lax.axis_size("shard")
    groups = shards // 2
    x = lax.axis_index("tp")
    core = lax.axis_index("shard") % 2
    home = x // 2 == core
    parity = x % 2
    move = functools.partial(lax.ppermute, axis_name=AXES)
    to_core = group_perm(groups, lambda x, c: (x, 1 - c))
    to_near = group_perm(groups, near)
    home_on = group_perm(groups, lambda x, c: (x ^ 3, c), is_home)
    away_swap = group_perm(groups, lambda x, c: (x ^ 1, c), is_away)
    ctx_near = group_perm(groups, lambda x, c: (x ^ 1, c) if is_home(x, c) else (x ^ 3, 1 - c))
    ctx_far = group_perm(groups, lambda x, c: (x ^ 2, 1 - c), is_away)

    def stay(x, c):
        return x, c

    y_split = group_perm(groups, stay, turn=lambda x, c: -1 if is_home(x, c) else 1)
    y_mirror = group_perm(groups, stay, turn=lambda x, c: 1 if is_home(x, c) else -1)
    y_up = group_perm(groups, stay, is_away, lambda x, c: 1)
    y_down = group_perm(groups, stay, is_away, lambda x, c: -1)
    odd_y = lax.axis_index("shard") // 2 % 2
    persons, _, kept = kept_part_entries.shape
    hops = partners(shards)
    me = lax.axis_index("shard")
    v_near = move(lax.dynamic_index_in_dim(lowrank_v_matrix, odd_y, 0, False), perm=to_near)
    u_near = move(lax.dynamic_index_in_dim(lowrank_u_matrix, odd_y, 0, False), perm=to_near)
    users = jnp.broadcast_to(person_embedding[None], (shards, *person_embedding.shape))
    users = lax.all_to_all(users, "shard", split_axis=0, concat_axis=0, tiled=True)

    parcel = pick_rows(
        kept_part_entries[:, 0, :].T, valid_slot_number.T, catalog_embedding, catalog_attributes
    )
    parcel = parcel.reshape(persons * 2, kept, 512)
    parcel, v_near, u_near, users = lax.optimization_barrier((parcel, v_near, u_near, users))
    recv = lax.all_to_all(parcel, AXES, split_axis=0, concat_axis=0, tiled=True)
    recv = recv.reshape(persons * 2 * kept, 512)

    v_far = move(v_near, perm=home_on)
    u_far = move(u_near, perm=away_swap)
    v_far, pair_attributes = lax.optimization_barrier((v_far, pair_attributes))
    ctx_own = lax.dynamic_index_in_dim(pair_attributes, parity, 0, False)
    ctx_away = lax.dynamic_index_in_dim(pair_attributes, 1 - parity, 0, False)
    ctx_a = move(ctx_away, perm=ctx_near)
    ctx_b = move(ctx_own, perm=ctx_far)
    ctx_a, ctx_b = lax.optimization_barrier((ctx_a, ctx_b))

    all_scores = jnp.einsum(
        "ue,ie->ui", users.reshape(persons, -1), catalog_embedding, preferred_element_type=F32
    )
    best = jnp.max(all_scores, axis=1).reshape(shards, persons // shards)
    order = [[i] for i in range(shards)]
    for pairs in hops:
        order = [order[i] + order[k] for i, k in pairs]
    order = lax.dynamic_index_in_dim(jnp.asarray(order, jnp.int32), me, 0, False)
    chosen = order[:, None] == jnp.arange(shards, dtype=jnp.int32)[None, :]
    best = jnp.sum(jnp.where(chosen[:, :, None], best[None], 0.0), axis=1)

    def halve(best, pairs):
        half = best.shape[0] // 2
        return jnp.maximum(best[:half], lax.ppermute(best[half:], "shard", pairs))

    def over_x(best):
        out = best
        for flip in (1, 3, 2):
            out = jnp.maximum(out, lax.ppermute(best, "tp", [(i, i ^ flip) for i in range(4)]))
        return out

    def over_y(best):
        n = best.shape[0] // 4
        out = best[:n]
        for block, flip in ((1, 1), (2, 3), (3, 2)):
            pairs = [(i, i ^ (2 * flip)) for i in range(shards)]
            got = lax.ppermute(best[block * n : (block + 1) * n], "shard", pairs)
            out = jnp.maximum(out, got)
        return out

    best = over_y(halve(best, hops[5]))

    small = jnp.concatenate([interaction_offset, final_projection[None, :].astype(F32)], 0)
    v_near_y = move(v_near, perm=y_split)
    v_far_y = move(v_far, perm=y_down)
    v_near_y, u_near_on = lax.optimization_barrier((v_near_y, u_near))
    u_near_y = move(u_near_on, perm=y_mirror)
    u_far_y = move(u_far, perm=y_up)
    ctx_a, best, small = lax.optimization_barrier((ctx_a, best, small))
    best = halve(best, hops[2])
    small_a = move(small, perm=to_near)
    small_b = move(small, perm=ctx_far)
    even = odd_y == 0
    v0_a = jnp.where(even, v_near, v_near_y)
    v1_a = jnp.where(even, v_near_y, v_near)
    u0_a = jnp.where(even, u_near, u_near_y)
    u1_a = jnp.where(even, u_near_y, u_near)
    v0_b = jnp.where(home, lowrank_v_matrix[0], jnp.where(even, v_far, v_far_y))
    v1_b = jnp.where(home, lowrank_v_matrix[1], jnp.where(even, v_far_y, v_far))
    u0_b = jnp.where(home, lowrank_u_matrix[0], jnp.where(even, u_far, u_far_y))
    u1_b = jnp.where(home, lowrank_u_matrix[1], jnp.where(even, u_far_y, u_far))
    ctx_b = jnp.where(home, ctx_own, ctx_b)
    ctx_a, u0_a, u0_b, u1_a, u1_b = lax.optimization_barrier((ctx_a, u0_a, u0_b, u1_a, u1_b))

    emb_other = lax.dynamic_index_in_dim(users, me ^ 1, 0, False)
    query = lax.dynamic_slice_in_dim(jnp.where(home, person_embedding, emb_other), parity, 1, 0)
    query = jnp.where(core == 0, query, jnp.zeros_like(query))
    zero = jnp.zeros_like(query)
    query = jnp.where(
        parity == 1, jnp.concatenate([query, zero], 1), jnp.concatenate([zero, query], 1)
    )
    query = jnp.broadcast_to(query, (16, 512))

    surv = pair_attributes.shape[1]
    tall, wide, lanes = ((surv, 512), BF), ((surv, 768), BF), ((16, surv), F32)
    part, head = call(
        context_kernel, "context_part", 24000, [((surv, 512), F32), ((512, 512), BF)], [],
        CTX, 8, [], [ctx_a, ctx_b, v0_a, v0_b], [],
    )
    recv, best = lax.optimization_barrier((recv, best))
    step = halve(best, hops[1])
    pay, piece, logit = call(
        first_kernel, "first_layer", 24000, [tall, tall, lanes],
        [pltpu.VMEM(recv.shape, BF), pltpu.VMEM((16, recv.shape[0]), F32)]
        + [pltpu.VMEM(recv.shape, BF), pltpu.SemaphoreType.DMA((recv.shape[0] // ROWS,))],
        FIRST, 8, [], [query, part, head], [recv],
    )
    piece, best, small_a, small_b = lax.optimization_barrier((piece, step, small_a, small_b))
    small_b = jnp.where(home, small, small_b)
    other, best = lax.optimization_barrier((move(piece, perm=to_core), halve(best, hops[0])))
    step = over_x(best)
    x_a, x_b, piece1 = call(
        second_kernel, "second_layer", 24000, [wide, wide, tall], [],
        SECOND, 12, [],
        [piece, other, pay, small_a, small_b, ctx_a, ctx_b, u0_a, u0_b, v1_a, v1_b], [],
    )
    piece1, best = lax.optimization_barrier((piece1, step))
    other1 = move(piece1, perm=to_core)
    (score,) = call(
        last_kernel, "last_layer", 24000, [lanes], [], 1792, 10, [similarity_coefficient],
        [piece1, other1, pay, x_a, x_b, small_a, small_b, logit, ctx_a, ctx_b, u1_a, u1_b], [],
    )
    top = jnp.where(home, lax.dynamic_slice_in_dim(best, parity, 1, 1), 0.0)
    score = score[0:1] - similarity_coefficient[0] * top
    score = score + move(score, perm=to_core)
    score_a = move(score, perm=to_near)
    score_b = jnp.where(home, score, move(score, perm=ctx_far))
    return jnp.where(
        parity == 1,
        jnp.concatenate([score_a, score_b], 0),
        jnp.concatenate([score_b, score_a], 0),
    )


def solution(mesh):
    return jax.shard_map(
        on_device,
        mesh=mesh,
        in_specs=(
            P("shard", None),
            P(("shard", "tp"), None),
            P(("shard", "tp"), None),
            P(None, ("shard", "tp"), None),
            P(None, ("shard", "tp")),
            P("shard", None, "tp"),
            P(None, "tp", None),
            P(None, None, "tp"),
            P(None, "tp"),
            P("tp"),
            P(),
        ),
        out_specs=P("shard", None),
        check_vma=False,
    )
```

```python
import functools

import jax
import jax.numpy as jnp
from jax import lax
from jax.experimental import pallas as pl
from jax.experimental.pallas import tpu as pltpu
from jax.sharding import PartitionSpec as P

BF = jnp.bfloat16
F32 = jnp.float32
AXES = ("shard", "tp")
VMEM = pl.BlockSpec(memory_space=pltpu.VMEM)
PICK, CTX, FIRST, SECOND = 4096, 13500, 15000, 15000
SMEM = pl.BlockSpec(memory_space=pltpu.SMEM)
ANY = pl.BlockSpec(memory_space=pl.ANY)


def grant(kbytes):
    return pltpu.CompilerParams(vmem_limit_bytes=kbytes * 1000)


def group_perm(groups, step, member=lambda x, c: True, turn=lambda x, c: 0):
    pairs = []
    for g in range(groups):
        for c in range(2):
            for x in range(4):
                if member(x, c):
                    x2, c2 = step(x, c)
                    g2 = g // 4 * 4 + (g + turn(x, c)) % 4
                    pairs.append((g * 8 + c * 4 + x, g2 * 8 + c2 * 4 + x2))
    return pairs


def is_home(x, c):
    return x // 2 == c


def is_away(x, c):
    return x // 2 != c


def near(x, c):
    return (x ^ 1, x // 2) if is_home(x, c) else (x ^ 3, x // 2)


def partners(shards):
    far_z = (6, 7, 4, 5, 2, 3, 0, 1)
    steps = []
    for of_z, of_y, of_core in (
        (lambda z: far_z[z], None, None),
        (lambda z: z ^ 2, None, None),
        (lambda z: z ^ 1, None, None),
        (None, 1, None),
        (None, 3, None),
        (None, None, 1),
    ):
        pairs = []
        for i in range(shards):
            z, y, c = i // 8, i // 2 % 4, i % 2
            z = of_z(z) if of_z else z
            y = y ^ of_y if of_y else y
            c = c ^ of_core if of_core else c
            pairs.append((i, z * 8 + y * 2 + c))
        steps.append(pairs)
    return steps


def dot(a, b):
    return jnp.dot(a, b, preferred_element_type=F32)


def dot_nt(a, b):
    return lax.dot_general(a, b, (((1,), (1,)), ((), ())), preferred_element_type=F32)


def call(kernel, name, kbytes, outs, scratch, mflops, mbytes, scalars, arrays, far, out_specs=None):
    return pl.pallas_call(
        kernel,
        in_specs=[SMEM] * len(scalars) + [VMEM] * len(arrays) + [ANY] * len(far),
        out_specs=out_specs or [VMEM] * len(outs),
        out_shape=[jax.ShapeDtypeStruct(shape, dtype) for shape, dtype in outs],
        scratch_shapes=scratch,
        compiler_params=grant(kbytes),
        cost_estimate=pl.CostEstimate(
            flops=mflops << 20, bytes_accessed=mbytes << 20, transcendentals=0
        ),
        name=name,
    )(*scalars, *arrays, *far)


def pick_kernel(
    kept_ref, count_ref, emb_hbm, attr_hbm, out_hbm, table, hot_ref, out_ref, in_sems, out_sems
):
    slots, persons = kept_ref.shape
    items = table.shape[1]
    loads = [pltpu.make_async_copy(emb_hbm, table.at[0], in_sems.at[0])]
    for q in range(3):
        columns = attr_hbm.at[:, pl.ds(q * 256, 256)]
        loads.append(pltpu.make_async_copy(columns, table.at[q + 1], in_sems.at[q + 1]))
    for load in loads:
        load.start()
    live = lax.broadcasted_iota(jnp.int32, (slots, persons), 0) < count_ref[...]
    wanted = jnp.where(live, kept_ref[...], 4095)
    digits = jnp.concatenate([wanted >> 6, wanted & 63], 0).astype(F32).astype(BF)
    n = 256
    blocks = persons * slots // n
    lane = lax.broadcasted_iota(jnp.int32, (n, 2 * slots), 1)
    slot = lax.broadcasted_iota(jnp.int32, (n, 2 * slots), 0) % slots
    odd = (lax.broadcasted_iota(jnp.int32, (n, 1), 0) // slots) % 2 == 1
    unused = []
    for b in range(blocks):
        row = lax.broadcasted_iota(jnp.int32, (n, persons), 0) + b * n
        owner = (row // slots == lax.broadcasted_iota(jnp.int32, (n, persons), 1)).astype(BF)
        both = dot_nt(owner, digits)
        high = jnp.where(lane == slot, both * 64.0, 0.0)
        low = jnp.where(lane == slot + slots, both, 0.0)
        rows = jnp.sum(high + low, axis=1, keepdims=True).astype(jnp.int32)
        hot = lax.broadcasted_iota(jnp.int32, (n, items), 1) == rows
        hot_ref[b * n : (b + 1) * n] = hot.astype(BF)
        unused.append(rows >= items)
    stores = []
    for c in range(2):
        loads[2 * c].wait()
        loads[2 * c + 1].wait()
        for b in range(blocks):
            hot = hot_ref[b * n : (b + 1) * n]
            low = jnp.where(unused[b], jnp.inf, dot(hot, table[2 * c]))
            high = jnp.where(unused[b], jnp.inf, dot(hot, table[2 * c + 1]))
            first = jnp.where(odd, low, high).astype(BF)
            second = jnp.where(odd, high, low).astype(BF)
            for g in range(n // 32):
                out_ref[c, b * (n // 32) + g, :, 0:256] = first[g * 32 : (g + 1) * 32]
                out_ref[c, b * (n // 32) + g, :, 256:512] = second[g * 32 : (g + 1) * 32]
        stores.append(pltpu.make_async_copy(out_ref.at[c], out_hbm.at[:, c], out_sems.at[c]))
        stores[-1].start()
    for store in stores:
        store.wait()


def pick_rows(kept, count, emb, attr):
    slots, persons = kept.shape
    out = (persons // 4, 2, 4 * slots, 512)
    return pl.pallas_call(
        pick_kernel,
        in_specs=[VMEM, VMEM, ANY, ANY],
        out_specs=ANY,
        out_shape=jax.ShapeDtypeStruct(out, BF),
        scratch_shapes=[
            pltpu.VMEM((4, emb.shape[0], 256), BF),
            pltpu.VMEM((persons * slots, emb.shape[0]), BF),
            pltpu.VMEM((2, persons // 4, 4 * slots, 512), BF),
            pltpu.SemaphoreType.DMA((4,)),
            pltpu.SemaphoreType.DMA((2,)),
        ],
        compiler_params=grant(62500),
        cost_estimate=pl.CostEstimate(
            flops=PICK << 20, bytes_accessed=6 << 20, transcendentals=0
        ),
        name="pick_rows",
    )(kept, count, emb, attr)


ROWS = 256


def block_copies(src, dst, sems):
    copies = []
    for i in range(dst.shape[0] // ROWS):
        here = pl.ds(i * ROWS, ROWS)
        copies.append(pltpu.make_async_copy(src.at[here], dst.at[here], sems.at[i]))
        copies[-1].start()
    return copies


def context_kernel(ca_ref, cb_ref, va_ref, vb_ref, part_ref, head_ref):
    head_ref[0:256] = va_ref[0:256]
    head_ref[256:512] = vb_ref[0:256]
    for i in range(part_ref.shape[0] // ROWS):
        here = pl.ds(i * ROWS, ROWS)
        part_ref[here] = dot(ca_ref[here], va_ref[256:768]) + dot(cb_ref[here], vb_ref[256:768])


def first_kernel(
    u_ref, part_ref, head_ref, recv_hbm, pay_ref, piece_ref, logit_ref,
    clean, place, recv_ref, recv_sems,
):
    slots = recv_ref.shape[0]
    recv_copies = block_copies(recv_hbm, recv_ref, recv_sems)
    r = lax.broadcasted_iota(jnp.int32, (ROWS, ROWS), 0)
    q = lax.broadcasted_iota(jnp.int32, (ROWS, ROWS), 1)
    upper = (r <= q).astype(BF)
    lane0 = (lax.broadcasted_iota(jnp.int32, (16, 128), 1) == 0).astype(BF)
    before = jnp.zeros((16, 1), F32)
    for i in range(slots // ROWS):
        here = slice(i * ROWS, (i + 1) * ROWS)
        recv_copies[i].wait()
        got = recv_ref[here].astype(F32)
        live = got < jnp.inf
        clean[here] = jnp.where(live, got, 0.0).astype(BF)
        marks = dot_nt(lane0, live[:, 0:128].astype(F32).astype(BF))
        upto = dot(marks.astype(BF), upper) + before
        place[:, here] = jnp.where(marks > 0.5, upto - 1.0, -1.0)
        before = upto[:, ROWS - 1 : ROWS]
    for i in range(pay_ref.shape[0] // ROWS):
        here = pl.ds(i * ROWS, ROWS)
        k = (lax.broadcasted_iota(jnp.int32, (ROWS, slots), 0) + i * ROWS).astype(F32)
        hot = (k == place[0:1, :]).astype(BF)
        pay = dot(hot, clean[...]).astype(BF)
        pay_ref[here] = pay
        piece = part_ref[here] + dot(pay, head_ref[...])
        piece_ref[here] = piece.astype(BF)
        logit_ref[:, here] = dot_nt(u_ref[...], pay)


def cross(x0, hidden, offset, x):
    x0 = x0.astype(F32)
    return (x0 * (hidden + offset) + x.astype(F32)).astype(BF)


def second_kernel(
    mine_ref, other_ref, pay_ref, ba_ref, bb_ref, ca_ref, cb_ref,
    ua_ref, ub_ref, va_ref, vb_ref, xa_ref, xb_ref, piece_ref,
):
    for i in range(pay_ref.shape[0] // ROWS):
        here = pl.ds(i * ROWS, ROWS)
        proj = (mine_ref[here].astype(F32) + other_ref[here].astype(F32)).astype(BF)
        slots = (
            (xa_ref, ua_ref, ba_ref, ca_ref, 0),
            (xb_ref, ub_ref, bb_ref, cb_ref, 256),
        )
        for x_ref, u_ref, b_ref, c_ref, at in slots:
            hidden = dot(proj, u_ref[...])
            pay = pay_ref[here, at : at + 256]
            ctx = c_ref[here]
            x_ref[here, 0:256] = cross(pay, hidden[:, 0:256], b_ref[0:1, 0:256], pay)
            x_ref[here, 256:768] = cross(ctx, hidden[:, 256:768], b_ref[0:1, 256:768], ctx)
        piece = dot(xa_ref[here], va_ref[...]) + dot(xb_ref[here], vb_ref[...])
        piece_ref[here] = piece.astype(BF)


def last_kernel(
    coefficient, mine_ref, other_ref, pay_ref, xa_ref, xb_ref, sa_ref, sb_ref, logit_ref,
    ca_ref, cb_ref, ua_ref, ub_ref, score_ref,
):
    for i in range(pay_ref.shape[0] // ROWS):
        here = pl.ds(i * ROWS, ROWS)
        proj = (mine_ref[here].astype(F32) + other_ref[here].astype(F32)).astype(BF)
        score = coefficient[0] * logit_ref[:, here]
        for x_ref, u_ref, s_ref, c_ref, at in (
            (xa_ref, ua_ref, sa_ref, ca_ref, 0),
            (xb_ref, ub_ref, sb_ref, cb_ref, 256),
        ):
            hidden = dot(proj, u_ref[...])
            low = cross(
                pay_ref[here, at : at + 256], hidden[:, 0:256], s_ref[1:2, 0:256], x_ref[here, 0:256]
            )
            high = cross(
                c_ref[here], hidden[:, 256:768], s_ref[1:2, 256:768], x_ref[here, 256:768]
            )
            out = jnp.broadcast_to(s_ref[2:3, :], (16, 768)).astype(BF)
            score = score + dot_nt(out[:, 0:256], low) + dot_nt(out[:, 256:768], high)
        score_ref[:, here] = score


def on_device(
    person_embedding,
    catalog_embedding,
    catalog_attributes,
    kept_part_entries,
    valid_slot_number,
    pair_attributes,
    lowrank_v_matrix,
    lowrank_u_matrix,
    interaction_offset,
    final_projection,
    similarity_coefficient,
):
    shards = lax.axis_size("shard")
    groups = shards // 2
    x = lax.axis_index("tp")
    core = lax.axis_index("shard") % 2
    home = x // 2 == core
    parity = x % 2
    move = functools.partial(lax.ppermute, axis_name=AXES)
    to_core = group_perm(groups, lambda x, c: (x, 1 - c))
    to_near = group_perm(groups, near)
    home_on = group_perm(groups, lambda x, c: (x ^ 3, c), is_home)
    away_swap = group_perm(groups, lambda x, c: (x ^ 1, c), is_away)
    ctx_near = group_perm(groups, lambda x, c: (x ^ 1, c) if is_home(x, c) else (x ^ 3, 1 - c))
    ctx_far = group_perm(groups, lambda x, c: (x ^ 2, 1 - c), is_away)

    def stay(x, c):
        return x, c

    y_split = group_perm(groups, stay, turn=lambda x, c: -1 if is_home(x, c) else 1)
    y_mirror = group_perm(groups, stay, turn=lambda x, c: 1 if is_home(x, c) else -1)
    y_up = group_perm(groups, stay, is_away, lambda x, c: 1)
    y_down = group_perm(groups, stay, is_away, lambda x, c: -1)
    odd_y = lax.axis_index("shard") // 2 % 2
    persons, _, kept = kept_part_entries.shape
    hops = partners(shards)
    me = lax.axis_index("shard")
    v_near = move(lax.dynamic_index_in_dim(lowrank_v_matrix, odd_y, 0, False), perm=to_near)
    u_near = move(lax.dynamic_index_in_dim(lowrank_u_matrix, odd_y, 0, False), perm=to_near)
    users = jnp.broadcast_to(person_embedding[None], (shards, *person_embedding.shape))
    users = lax.all_to_all(users, "shard", split_axis=0, concat_axis=0, tiled=True)

    parcel = pick_rows(
        kept_part_entries[:, 0, :].T, valid_slot_number.T, catalog_embedding, catalog_attributes
    )
    parcel = parcel.reshape(persons * 2, kept, 512)
    parcel, v_near, u_near, users = lax.optimization_barrier((parcel, v_near, u_near, users))
    recv = lax.all_to_all(parcel, AXES, split_axis=0, concat_axis=0, tiled=True)
    recv = recv.reshape(persons * 2 * kept, 512)

    v_far = move(v_near, perm=home_on)
    u_far = move(u_near, perm=away_swap)
    v_far, pair_attributes = lax.optimization_barrier((v_far, pair_attributes))
    ctx_own = lax.dynamic_index_in_dim(pair_attributes, parity, 0, False)
    ctx_away = lax.dynamic_index_in_dim(pair_attributes, 1 - parity, 0, False)
    ctx_a = move(ctx_away, perm=ctx_near)
    ctx_b = move(ctx_own, perm=ctx_far)
    ctx_a, ctx_b = lax.optimization_barrier((ctx_a, ctx_b))

    all_scores = jnp.einsum(
        "ue,ie->ui", users.reshape(persons, -1), catalog_embedding, preferred_element_type=F32
    )
    best = jnp.max(all_scores, axis=1).reshape(shards, persons // shards)
    order = [[i] for i in range(shards)]
    for pairs in hops:
        order = [order[i] + order[k] for i, k in pairs]
    order = lax.dynamic_index_in_dim(jnp.asarray(order, jnp.int32), me, 0, False)
    chosen = order[:, None] == jnp.arange(shards, dtype=jnp.int32)[None, :]
    best = jnp.sum(jnp.where(chosen[:, :, None], best[None], 0.0), axis=1)

    def halve(best, pairs):
        half = best.shape[0] // 2
        return jnp.maximum(best[:half], lax.ppermute(best[half:], "shard", pairs))

    def over_x(best):
        out = best
        for flip in (1, 3, 2):
            out = jnp.maximum(out, lax.ppermute(best, "tp", [(i, i ^ flip) for i in range(4)]))
        return out

    def over_y(best):
        n = best.shape[0] // 4
        out = best[:n]
        for block, flip in ((1, 1), (2, 3), (3, 2)):
            pairs = [(i, i ^ (2 * flip)) for i in range(shards)]
            got = lax.ppermute(best[block * n : (block + 1) * n], "shard", pairs)
            out = jnp.maximum(out, got)
        return out

    best = over_y(halve(best, hops[5]))

    small = jnp.concatenate([interaction_offset, final_projection[None, :].astype(F32)], 0)
    v_near_y = move(v_near, perm=y_split)
    v_far_y = move(v_far, perm=y_down)
    best, u_near_on = lax.optimization_barrier((best, u_near))
    u_near_y = move(u_near_on, perm=y_mirror)
    u_far_y = move(u_far, perm=y_up)
    ctx_a, best, small = lax.optimization_barrier((ctx_a, best, small))
    best = halve(best, hops[2])
    small_a = move(small, perm=to_near)
    small_b = move(small, perm=ctx_far)
    even = odd_y == 0
    v0_a = jnp.where(even, v_near, v_near_y)
    v1_a = jnp.where(even, v_near_y, v_near)
    u0_a = jnp.where(even, u_near, u_near_y)
    u1_a = jnp.where(even, u_near_y, u_near)
    v0_b = jnp.where(home, lowrank_v_matrix[0], jnp.where(even, v_far, v_far_y))
    v1_b = jnp.where(home, lowrank_v_matrix[1], jnp.where(even, v_far_y, v_far))
    u0_b = jnp.where(home, lowrank_u_matrix[0], jnp.where(even, u_far, u_far_y))
    u1_b = jnp.where(home, lowrank_u_matrix[1], jnp.where(even, u_far_y, u_far))
    ctx_b = jnp.where(home, ctx_own, ctx_b)
    ctx_a, u0_a, u0_b, u1_a, u1_b = lax.optimization_barrier((ctx_a, u0_a, u0_b, u1_a, u1_b))

    emb_other = lax.dynamic_index_in_dim(users, me ^ 1, 0, False)
    query = lax.dynamic_slice_in_dim(jnp.where(home, person_embedding, emb_other), parity, 1, 0)
    query = jnp.where(core == 0, query, jnp.zeros_like(query))
    zero = jnp.zeros_like(query)
    query = jnp.where(
        parity == 1, jnp.concatenate([query, zero], 1), jnp.concatenate([zero, query], 1)
    )
    query = jnp.broadcast_to(query, (16, 512))

    surv = pair_attributes.shape[1]
    tall, wide, lanes = ((surv, 512), BF), ((surv, 768), BF), ((16, surv), F32)
    part, head = call(
        context_kernel, "context_part", 24000, [((surv, 512), F32), ((512, 512), BF)], [],
        CTX, 8, [], [ctx_a, ctx_b, v0_a, v0_b], [],
    )
    recv, best = lax.optimization_barrier((recv, best))
    step = halve(best, hops[1])
    pay, piece, logit = call(
        first_kernel, "first_layer", 24000, [tall, tall, lanes],
        [pltpu.VMEM(recv.shape, BF), pltpu.VMEM((16, recv.shape[0]), F32)]
        + [pltpu.VMEM(recv.shape, BF), pltpu.SemaphoreType.DMA((recv.shape[0] // ROWS,))],
        FIRST, 8, [], [query, part, head], [recv],
    )
    piece, best, small_a, small_b = lax.optimization_barrier((piece, step, small_a, small_b))
    small_b = jnp.where(home, small, small_b)
    other, best = lax.optimization_barrier((move(piece, perm=to_core), halve(best, hops[0])))
    step = over_x(best)
    x_a, x_b, piece1 = call(
        second_kernel, "second_layer", 24000, [wide, wide, tall], [],
        SECOND, 12, [],
        [piece, other, pay, small_a, small_b, ctx_a, ctx_b, u0_a, u0_b, v1_a, v1_b], [],
    )
    piece1, best = lax.optimization_barrier((piece1, step))
    other1 = move(piece1, perm=to_core)
    (score,) = call(
        last_kernel, "last_layer", 24000, [lanes], [], 1792, 10, [similarity_coefficient],
        [piece1, other1, pay, x_a, x_b, small_a, small_b, logit, ctx_a, ctx_b, u1_a, u1_b], [],
    )
    top = jnp.where(home, lax.dynamic_slice_in_dim(best, parity, 1, 1), 0.0)
    score = score[0:1] - similarity_coefficient[0] * top
    score = score + move(score, perm=to_core)
    score_a = move(score, perm=to_near)
    score_b = jnp.where(home, score, move(score, perm=ctx_far))
    return jnp.where(
        parity == 1,
        jnp.concatenate([score_a, score_b], 0),
        jnp.concatenate([score_b, score_a], 0),
    )


def solution(mesh):
    return jax.shard_map(
        on_device,
        mesh=mesh,
        in_specs=(
            P("shard", None),
            P(("shard", "tp"), None),
            P(("shard", "tp"), None),
            P(None, ("shard", "tp"), None),
            P(None, ("shard", "tp")),
            P("shard", None, "tp"),
            P(None, "tp", None),
            P(None, None, "tp"),
            P(None, "tp"),
            P("tp"),
            P(),
        ),
        out_specs=P("shard", None),
        check_vma=False,
    )
```

```python
import functools

import jax
import jax.numpy as jnp
from jax import lax
from jax.experimental import pallas as pl
from jax.experimental.pallas import tpu as pltpu
from jax.sharding import PartitionSpec as P

BF = jnp.bfloat16
F32 = jnp.float32
AXES = ("shard", "tp")
VMEM = pl.BlockSpec(memory_space=pltpu.VMEM)
PICK, CTX, FIRST, SECOND = 4096, 13500, 15000, 15000
SMEM = pl.BlockSpec(memory_space=pltpu.SMEM)
ANY = pl.BlockSpec(memory_space=pl.ANY)


def grant(kbytes):
    return pltpu.CompilerParams(vmem_limit_bytes=kbytes * 1000)


def group_perm(groups, step, member=lambda x, c: True, turn=lambda x, c: 0):
    pairs = []
    for g in range(groups):
        for c in range(2):
            for x in range(4):
                if member(x, c):
                    x2, c2 = step(x, c)
                    g2 = g // 4 * 4 + (g + turn(x, c)) % 4
                    pairs.append((g * 8 + c * 4 + x, g2 * 8 + c2 * 4 + x2))
    return pairs


def is_home(x, c):
    return x // 2 == c


def is_away(x, c):
    return x // 2 != c


def near(x, c):
    return (x ^ 1, x // 2) if is_home(x, c) else (x ^ 3, x // 2)


def partners(shards):
    far_z = (6, 7, 4, 5, 2, 3, 0, 1)
    steps = []
    for of_z, of_y, of_core in (
        (lambda z: far_z[z], None, None),
        (lambda z: z ^ 2, None, None),
        (lambda z: z ^ 1, None, None),
        (None, 1, None),
        (None, 3, None),
        (None, None, 1),
    ):
        pairs = []
        for i in range(shards):
            z, y, c = i // 8, i // 2 % 4, i % 2
            z = of_z(z) if of_z else z
            y = y ^ of_y if of_y else y
            c = c ^ of_core if of_core else c
            pairs.append((i, z * 8 + y * 2 + c))
        steps.append(pairs)
    return steps


def dot(a, b):
    return jnp.dot(a, b, preferred_element_type=F32)


def dot_nt(a, b):
    return lax.dot_general(a, b, (((1,), (1,)), ((), ())), preferred_element_type=F32)


def call(kernel, name, kbytes, outs, scratch, mflops, mbytes, scalars, arrays, far, out_specs=None):
    return pl.pallas_call(
        kernel,
        in_specs=[SMEM] * len(scalars) + [VMEM] * len(arrays) + [ANY] * len(far),
        out_specs=out_specs or [VMEM] * len(outs),
        out_shape=[jax.ShapeDtypeStruct(shape, dtype) for shape, dtype in outs],
        scratch_shapes=scratch,
        compiler_params=grant(kbytes),
        cost_estimate=pl.CostEstimate(
            flops=mflops << 20, bytes_accessed=mbytes << 20, transcendentals=0
        ),
        name=name,
    )(*scalars, *arrays, *far)


def pick_kernel(
    kept_ref, count_ref, emb_hbm, attr_hbm, out_hbm, table, hot_ref, out_ref, in_sems, out_sems
):
    slots, persons = kept_ref.shape
    items = table.shape[1]
    loads = [pltpu.make_async_copy(emb_hbm, table.at[0], in_sems.at[0])]
    for q in range(3):
        columns = attr_hbm.at[:, pl.ds(q * 256, 256)]
        loads.append(pltpu.make_async_copy(columns, table.at[q + 1], in_sems.at[q + 1]))
    for load in loads:
        load.start()
    live = lax.broadcasted_iota(jnp.int32, (slots, persons), 0) < count_ref[...]
    wanted = jnp.where(live, kept_ref[...], 4095)
    digits = jnp.concatenate([wanted >> 6, wanted & 63], 0).astype(F32).astype(BF)
    n = 256
    blocks = persons * slots // n
    lane = lax.broadcasted_iota(jnp.int32, (n, 2 * slots), 1)
    slot = lax.broadcasted_iota(jnp.int32, (n, 2 * slots), 0) % slots
    odd = (lax.broadcasted_iota(jnp.int32, (n, 1), 0) // slots) % 2 == 1
    unused = []
    for b in range(blocks):
        row = lax.broadcasted_iota(jnp.int32, (n, persons), 0) + b * n
        owner = (row // slots == lax.broadcasted_iota(jnp.int32, (n, persons), 1)).astype(BF)
        both = dot_nt(owner, digits)
        high = jnp.where(lane == slot, both * 64.0, 0.0)
        low = jnp.where(lane == slot + slots, both, 0.0)
        rows = jnp.sum(high + low, axis=1, keepdims=True).astype(jnp.int32)
        hot = lax.broadcasted_iota(jnp.int32, (n, items), 1) == rows
        hot_ref[b * n : (b + 1) * n] = hot.astype(BF)
        unused.append(rows >= items)
    stores = []
    for c in range(2):
        loads[2 * c].wait()
        loads[2 * c + 1].wait()
        for b in range(blocks):
            hot = hot_ref[b * n : (b + 1) * n]
            low = jnp.where(unused[b], jnp.inf, dot(hot, table[2 * c]))
            high = jnp.where(unused[b], jnp.inf, dot(hot, table[2 * c + 1]))
            first = jnp.where(odd, low, high).astype(BF)
            second = jnp.where(odd, high, low).astype(BF)
            for g in range(n // 32):
                out_ref[c, b * (n // 32) + g, :, 0:256] = first[g * 32 : (g + 1) * 32]
                out_ref[c, b * (n // 32) + g, :, 256:512] = second[g * 32 : (g + 1) * 32]
        stores.append(pltpu.make_async_copy(out_ref.at[c], out_hbm.at[:, c], out_sems.at[c]))
        stores[-1].start()
    for store in stores:
        store.wait()


def pick_rows(kept, count, emb, attr):
    slots, persons = kept.shape
    out = (persons // 4, 2, 4 * slots, 512)
    return pl.pallas_call(
        pick_kernel,
        in_specs=[VMEM, VMEM, ANY, ANY],
        out_specs=ANY,
        out_shape=jax.ShapeDtypeStruct(out, BF),
        scratch_shapes=[
            pltpu.VMEM((4, emb.shape[0], 256), BF),
            pltpu.VMEM((persons * slots, emb.shape[0]), BF),
            pltpu.VMEM((2, persons // 4, 4 * slots, 512), BF),
            pltpu.SemaphoreType.DMA((4,)),
            pltpu.SemaphoreType.DMA((2,)),
        ],
        compiler_params=grant(62500),
        cost_estimate=pl.CostEstimate(
            flops=PICK << 20, bytes_accessed=6 << 20, transcendentals=0
        ),
        name="pick_rows",
    )(kept, count, emb, attr)


ROWS = 256


def block_copies(src, dst, sems):
    copies = []
    for i in range(dst.shape[0] // ROWS):
        here = pl.ds(i * ROWS, ROWS)
        copies.append(pltpu.make_async_copy(src.at[here], dst.at[here], sems.at[i]))
        copies[-1].start()
    return copies


def context_kernel(ca_ref, cb_ref, va_ref, vb_ref, part_ref, head_ref):
    head_ref[0:256] = va_ref[0:256]
    head_ref[256:512] = vb_ref[0:256]
    for i in range(part_ref.shape[0] // ROWS):
        here = pl.ds(i * ROWS, ROWS)
        part_ref[here] = dot(ca_ref[here], va_ref[256:768]) + dot(cb_ref[here], vb_ref[256:768])


def first_kernel(
    u_ref, part_ref, head_ref, recv_hbm, pay_ref, piece_ref, logit_ref,
    clean, place, recv_ref, recv_sems,
):
    slots = recv_ref.shape[0]
    recv_copies = block_copies(recv_hbm, recv_ref, recv_sems)
    r = lax.broadcasted_iota(jnp.int32, (ROWS, ROWS), 0)
    q = lax.broadcasted_iota(jnp.int32, (ROWS, ROWS), 1)
    upper = (r <= q).astype(BF)
    lane0 = (lax.broadcasted_iota(jnp.int32, (16, 128), 1) == 0).astype(BF)
    before = jnp.zeros((16, 1), F32)
    for i in range(slots // ROWS):
        here = slice(i * ROWS, (i + 1) * ROWS)
        recv_copies[i].wait()
        got = recv_ref[here].astype(F32)
        live = got < jnp.inf
        clean[here] = jnp.where(live, got, 0.0).astype(BF)
        marks = dot_nt(lane0, live[:, 0:128].astype(F32).astype(BF))
        upto = dot(marks.astype(BF), upper) + before
        place[:, here] = jnp.where(marks > 0.5, upto - 1.0, -1.0)
        before = upto[:, ROWS - 1 : ROWS]
    for i in range(pay_ref.shape[0] // ROWS):
        here = pl.ds(i * ROWS, ROWS)
        k = (lax.broadcasted_iota(jnp.int32, (ROWS, slots), 0) + i * ROWS).astype(F32)
        hot = (k == place[0:1, :]).astype(BF)
        pay = dot(hot, clean[...]).astype(BF)
        pay_ref[here] = pay
        piece = part_ref[here] + dot(pay, head_ref[...])
        piece_ref[here] = piece.astype(BF)
        logit_ref[:, here] = dot_nt(u_ref[...], pay)


def cross(x0, hidden, offset, x):
    x0 = x0.astype(F32)
    return (x0 * (hidden + offset) + x.astype(F32)).astype(BF)


def second_kernel(
    mine_ref, other_ref, pay_ref, ba_ref, bb_ref, ca_ref, cb_ref,
    ua_ref, ub_ref, va_ref, vb_ref, xa_ref, xb_ref, piece_ref,
):
    for i in range(pay_ref.shape[0] // ROWS):
        here = pl.ds(i * ROWS, ROWS)
        proj = (mine_ref[here].astype(F32) + other_ref[here].astype(F32)).astype(BF)
        slots = (
            (xa_ref, ua_ref, ba_ref, ca_ref, 0),
            (xb_ref, ub_ref, bb_ref, cb_ref, 256),
        )
        for x_ref, u_ref, b_ref, c_ref, at in slots:
            hidden = dot(proj, u_ref[...])
            pay = pay_ref[here, at : at + 256]
            ctx = c_ref[here]
            x_ref[here, 0:256] = cross(pay, hidden[:, 0:256], b_ref[0:1, 0:256], pay)
            x_ref[here, 256:768] = cross(ctx, hidden[:, 256:768], b_ref[0:1, 256:768], ctx)
        piece = dot(xa_ref[here], va_ref[...]) + dot(xb_ref[here], vb_ref[...])
        piece_ref[here] = piece.astype(BF)


def last_kernel(
    coefficient, mine_ref, other_ref, pay_ref, xa_ref, xb_ref, sa_ref, sb_ref, logit_ref,
    ca_ref, cb_ref, ua_ref, ub_ref, score_ref,
):
    for i in range(pay_ref.shape[0] // ROWS):
        here = pl.ds(i * ROWS, ROWS)
        proj = (mine_ref[here].astype(F32) + other_ref[here].astype(F32)).astype(BF)
        score = coefficient[0] * logit_ref[:, here]
        for x_ref, u_ref, s_ref, c_ref, at in (
            (xa_ref, ua_ref, sa_ref, ca_ref, 0),
            (xb_ref, ub_ref, sb_ref, cb_ref, 256),
        ):
            hidden = dot(proj, u_ref[...])
            low = cross(
                pay_ref[here, at : at + 256], hidden[:, 0:256], s_ref[1:2, 0:256], x_ref[here, 0:256]
            )
            high = cross(
                c_ref[here], hidden[:, 256:768], s_ref[1:2, 256:768], x_ref[here, 256:768]
            )
            out = jnp.broadcast_to(s_ref[2:3, :], (16, 768)).astype(BF)
            score = score + dot_nt(out[:, 0:256], low) + dot_nt(out[:, 256:768], high)
        score_ref[:, here] = score


def on_device(
    person_embedding,
    catalog_embedding,
    catalog_attributes,
    kept_part_entries,
    valid_slot_number,
    pair_attributes,
    lowrank_v_matrix,
    lowrank_u_matrix,
    interaction_offset,
    final_projection,
    similarity_coefficient,
):
    shards = lax.axis_size("shard")
    groups = shards // 2
    x = lax.axis_index("tp")
    core = lax.axis_index("shard") % 2
    home = x // 2 == core
    parity = x % 2
    move = functools.partial(lax.ppermute, axis_name=AXES)
    to_core = group_perm(groups, lambda x, c: (x, 1 - c))
    to_near = group_perm(groups, near)
    home_on = group_perm(groups, lambda x, c: (x ^ 3, c), is_home)
    away_swap = group_perm(groups, lambda x, c: (x ^ 1, c), is_away)
    ctx_near = group_perm(groups, lambda x, c: (x ^ 1, c) if is_home(x, c) else (x ^ 3, 1 - c))
    ctx_far = group_perm(groups, lambda x, c: (x ^ 2, 1 - c), is_away)

    def stay(x, c):
        return x, c

    y_split = group_perm(groups, stay, turn=lambda x, c: -1 if is_home(x, c) else 1)
    y_mirror = group_perm(groups, stay, turn=lambda x, c: 1 if is_home(x, c) else -1)
    y_up = group_perm(groups, stay, is_away, lambda x, c: 1)
    y_down = group_perm(groups, stay, is_away, lambda x, c: -1)
    odd_y = lax.axis_index("shard") // 2 % 2
    persons, _, kept = kept_part_entries.shape
    hops = partners(shards)
    me = lax.axis_index("shard")
    v_near = move(lax.dynamic_index_in_dim(lowrank_v_matrix, odd_y, 0, False), perm=to_near)
    u_near = move(lax.dynamic_index_in_dim(lowrank_u_matrix, odd_y, 0, False), perm=to_near)
    users = jnp.broadcast_to(person_embedding[None], (shards, *person_embedding.shape))
    users = lax.all_to_all(users, "shard", split_axis=0, concat_axis=0, tiled=True)

    parcel = pick_rows(
        kept_part_entries[:, 0, :].T, valid_slot_number.T, catalog_embedding, catalog_attributes
    )
    parcel = parcel.reshape(persons * 2, kept, 512)
    parcel, v_near, u_near, users = lax.optimization_barrier((parcel, v_near, u_near, users))
    recv = lax.all_to_all(parcel, AXES, split_axis=0, concat_axis=0, tiled=True)
    recv = recv.reshape(persons * 2 * kept, 512)

    v_far = move(v_near, perm=home_on)
    u_far = move(u_near, perm=away_swap)
    v_far, pair_attributes = lax.optimization_barrier((v_far, pair_attributes))
    ctx_own = lax.dynamic_index_in_dim(pair_attributes, parity, 0, False)
    ctx_away = lax.dynamic_index_in_dim(pair_attributes, 1 - parity, 0, False)
    ctx_a = move(ctx_away, perm=ctx_near)
    ctx_b = move(ctx_own, perm=ctx_far)
    ctx_a, ctx_b = lax.optimization_barrier((ctx_a, ctx_b))

    all_scores = jnp.einsum(
        "ue,ie->ui", users.reshape(persons, -1), catalog_embedding, preferred_element_type=F32
    )
    best = jnp.max(all_scores, axis=1).reshape(shards, persons // shards)
    order = [[i] for i in range(shards)]
    for pairs in hops:
        order = [order[i] + order[k] for i, k in pairs]
    order = lax.dynamic_index_in_dim(jnp.asarray(order, jnp.int32), me, 0, False)
    chosen = order[:, None] == jnp.arange(shards, dtype=jnp.int32)[None, :]
    best = jnp.sum(jnp.where(chosen[:, :, None], best[None], 0.0), axis=1)

    def halve(best, pairs):
        half = best.shape[0] // 2
        return jnp.maximum(best[:half], lax.ppermute(best[half:], "shard", pairs))

    def over_x(best):
        out = best
        for flip in (1, 3, 2):
            out = jnp.maximum(out, lax.ppermute(best, "tp", [(i, i ^ flip) for i in range(4)]))
        return out

    def over_y(best):
        n = best.shape[0] // 4
        out = best[:n]
        for block, flip in ((1, 1), (2, 3), (3, 2)):
            pairs = [(i, i ^ (2 * flip)) for i in range(shards)]
            got = lax.ppermute(best[block * n : (block + 1) * n], "shard", pairs)
            out = jnp.maximum(out, got)
        return out

    best = over_y(halve(best, hops[5]))

    small = jnp.concatenate([interaction_offset, final_projection[None, :].astype(F32)], 0)
    v_near_y = move(v_near, perm=y_split)
    v_far_y = move(v_far, perm=y_down)
    best, v_near_y, u_near_on = lax.optimization_barrier((best, v_near_y, u_near))
    u_near_y = move(u_near_on, perm=y_mirror)
    u_far_y = move(u_far, perm=y_up)
    ctx_a, best, small = lax.optimization_barrier((ctx_a, best, small))
    best = halve(best, hops[2])
    small_a = move(small, perm=to_near)
    small_b = move(small, perm=ctx_far)
    even = odd_y == 0
    v0_a = jnp.where(even, v_near, v_near_y)
    v1_a = jnp.where(even, v_near_y, v_near)
    u0_a = jnp.where(even, u_near, u_near_y)
    u1_a = jnp.where(even, u_near_y, u_near)
    v0_b = jnp.where(home, lowrank_v_matrix[0], jnp.where(even, v_far, v_far_y))
    v1_b = jnp.where(home, lowrank_v_matrix[1], jnp.where(even, v_far_y, v_far))
    u0_b = jnp.where(home, lowrank_u_matrix[0], jnp.where(even, u_far, u_far_y))
    u1_b = jnp.where(home, lowrank_u_matrix[1], jnp.where(even, u_far_y, u_far))
    ctx_b = jnp.where(home, ctx_own, ctx_b)
    ctx_a, u0_a, u0_b, u1_a, u1_b = lax.optimization_barrier((ctx_a, u0_a, u0_b, u1_a, u1_b))

    emb_other = lax.dynamic_index_in_dim(users, me ^ 1, 0, False)
    query = lax.dynamic_slice_in_dim(jnp.where(home, person_embedding, emb_other), parity, 1, 0)
    query = jnp.where(core == 0, query, jnp.zeros_like(query))
    zero = jnp.zeros_like(query)
    query = jnp.where(
        parity == 1, jnp.concatenate([query, zero], 1), jnp.concatenate([zero, query], 1)
    )
    query = jnp.broadcast_to(query, (16, 512))

    surv = pair_attributes.shape[1]
    tall, wide, lanes = ((surv, 512), BF), ((surv, 768), BF), ((16, surv), F32)
    part, head = call(
        context_kernel, "context_part", 24000, [((surv, 512), F32), ((512, 512), BF)], [],
        CTX, 8, [], [ctx_a, ctx_b, v0_a, v0_b], [],
    )
    recv, best = lax.optimization_barrier((recv, best))
    step = halve(best, hops[1])
    pay, piece, logit = call(
        first_kernel, "first_layer", 24000, [tall, tall, lanes],
        [pltpu.VMEM(recv.shape, BF), pltpu.VMEM((16, recv.shape[0]), F32)]
        + [pltpu.VMEM(recv.shape, BF), pltpu.SemaphoreType.DMA((recv.shape[0] // ROWS,))],
        FIRST, 8, [], [query, part, head], [recv],
    )
    piece, best, small_a, small_b = lax.optimization_barrier((piece, step, small_a, small_b))
    small_b = jnp.where(home, small, small_b)
    other, best = lax.optimization_barrier((move(piece, perm=to_core), halve(best, hops[0])))
    step = over_x(best)
    x_a, x_b, piece1 = call(
        second_kernel, "second_layer", 24000, [wide, wide, tall], [],
        SECOND, 12, [],
        [piece, other, pay, small_a, small_b, ctx_a, ctx_b, u0_a, u0_b, v1_a, v1_b], [],
    )
    piece1, best = lax.optimization_barrier((piece1, step))
    other1 = move(piece1, perm=to_core)
    (score,) = call(
        last_kernel, "last_layer", 24000, [lanes], [], 1792, 10, [similarity_coefficient],
        [piece1, other1, pay, x_a, x_b, small_a, small_b, logit, ctx_a, ctx_b, u1_a, u1_b], [],
    )
    top = jnp.where(home, lax.dynamic_slice_in_dim(best, parity, 1, 1), 0.0)
    score = score[0:1] - similarity_coefficient[0] * top
    score = score + move(score, perm=to_core)
    score_a = move(score, perm=to_near)
    score_b = jnp.where(home, score, move(score, perm=ctx_far))
    return jnp.where(
        parity == 1,
        jnp.concatenate([score_a, score_b], 0),
        jnp.concatenate([score_b, score_a], 0),
    )


def solution(mesh):
    return jax.shard_map(
        on_device,
        mesh=mesh,
        in_specs=(
            P("shard", None),
            P(("shard", "tp"), None),
            P(("shard", "tp"), None),
            P(None, ("shard", "tp"), None),
            P(None, ("shard", "tp")),
            P("shard", None, "tp"),
            P(None, "tp", None),
            P(None, None, "tp"),
            P(None, "tp"),
            P("tp"),
            P(),
        ),
        out_specs=P("shard", None),
        check_vma=False,
    )
```
